32 devices in a mesh: replica: 4 (over z), fsdp: 4 (over y, core), ctx: 2 (over x).
Axes of the slice: x: 2, y: 2, z: 4, core: 2. Of those that a mesh axis runs over, the one named last changes fastest.
Arguments:
- tokens: bfloat16 [16, 256, 1024], P(('replica', 'fsdp'), 'ctx'), may hold values from -6 to 6
- input_gain: bfloat16 [1024], P(('fsdp', 'ctx')), may hold values from 0.099609375 to 1.8984375
- qkv_weight: bfloat16 [1024, 3072], P(('fsdp', 'ctx')), may hold values from -0.1875 to 0.1875
- output_weight: bfloat16 [1024, 1024], P(('fsdp', 'ctx')), may hold values from -1.5 to 1.5
- mlp_gain: bfloat16 [1024], P(('fsdp', 'ctx')), may hold values from 0.099609375 to 1.8984375
- expand_weight: bfloat16 [1024, 5248], P(('fsdp', 'ctx')), may hold values from -0.1875 to 0.1875
- contract_weight: bfloat16 [1024, 2624], P(('fsdp', 'ctx')), may hold values from -0.125 to 0.125
- positions: int32 [16, 256], P(('replica', 'fsdp'), 'ctx'), may hold values from 0 to 199, as said below
- mask_bias: float32 [16, 256, 256], P(('replica', 'fsdp'), 'ctx'), may hold values from -1000000000 to 0, as said below
- cotangent: bfloat16 [16, 256, 1024], P(('replica', 'fsdp'), 'ctx'), may hold values from -6 to 6
Outputs:
- layer_out: bfloat16 [16, 256, 1024], P(('replica', 'fsdp'), 'ctx')
- input_grad: bfloat16 [16, 256, 1024], P(('replica', 'fsdp'), 'ctx')
- input_gain_grad: float32 [1024], P(('fsdp', 'ctx'))
- qkv_weight_grad: float32 [1024, 3072], P(('fsdp', 'ctx'))
- output_weight_grad: float32 [1024, 1024], P(('fsdp', 'ctx'))
- mlp_gain_grad: float32 [1024], P(('fsdp', 'ctx'))
- expand_weight_grad: float32 [1024, 5248], P(('fsdp', 'ctx'))
- contract_weight_grad: float32 [1024, 2624], P(('fsdp', 'ctx'))
The draws below stay inside these ranges and needn't reach their ends.
Inputs may be any that keep to these rules, and one draw needn't show every extreme that they name: `positions`: each sequence is a pack of documents one after another; a token's position is its index inside its document, 0 at a document's first token and rising by one; every sequence holds one document of exactly 200 tokens and none longer. mask_bias[s, t, j] is 0 where the key token k = 128 * (t // 128) - 64 + j lies inside the sequence, |k - t| <= 64, and k is in the same document as t (as positions give the documents); else -1e9.
All inputs are finite; a program needn't handle non-finite values.
Results may differ from the reference program's by a relative error of at most 0.015.
Values may be sent and summed in bfloat16 or wider, within the bound.
No kernel may reach another device: no remote copies, remote signals or barrier semaphores. Data moves between devices by JAX's collectives and lax.ppermute only.
A program may use at most 256 MiB of HBM per device.

```python
import math
import jax
import jax.numpy as jnp
from jax import lax

D = 1024
HEADS = 16
HEAD_DIM = 64
FF = 2624
HALF = 64
BLOCK = 128
LENGTH = 256
SEQS = 16
DOC_MOST = 200


def pack_docs(key):
    doc_key = jax.random.fold_in(key, 7)
    lowest = max(DOC_MOST // 8, 1)
    count = LENGTH // lowest + 2
    sizes = jax.random.randint(jax.random.fold_in(doc_key, 1), (SEQS, count), lowest, DOC_MOST + 1)
    longest = jax.random.randint(jax.random.fold_in(doc_key, 2), (SEQS, 1), 0, 2)
    slots = jnp.arange(count, dtype=jnp.int32)[None, :]
    sizes = jnp.where((slots == 0) & (longest == 1), jnp.minimum(sizes, LENGTH - DOC_MOST), sizes)
    sizes = jnp.where(slots == longest, DOC_MOST, sizes).astype(jnp.int32)
    ends = jnp.cumsum(sizes, axis=1).astype(jnp.int32)
    places = jnp.arange(LENGTH, dtype=jnp.int32)
    segment = jnp.sum((places[None, :, None] >= ends[:, None, :]).astype(jnp.int32), axis=-1).astype(jnp.int32)
    starts = ends - sizes
    begins = jnp.take_along_axis(starts, segment, axis=1)
    return (segment, (places[None, :] - begins).astype(jnp.int32))


def draw_positions(key, part):
    return pack_docs(key)[1].astype(jnp.int32)


def draw_mask_bias(key, part):
    segment, unused_pos = pack_docs(key)
    extent = BLOCK + 2 * HALF
    places = jnp.arange(LENGTH, dtype=jnp.int32)
    columns = jnp.arange(extent, dtype=jnp.int32)
    key_place = places[:, None] // BLOCK * BLOCK - HALF + columns[None, :]
    inside = (key_place >= 0) & (key_place < LENGTH) & (jnp.abs(key_place - places[:, None]) <= HALF)
    clipped = jnp.clip(key_place, 0, LENGTH - 1)
    key_segment = segment[:, clipped]
    same_doc = key_segment == segment[:, :, None]
    allowed = inside[None, :, :] & same_doc
    return jnp.where(allowed, 0.0, -1000000000.0).astype(jnp.float32)


def strengthened(entries, key, source, target, parts, factor):
    def block_of(position):
        return (jnp.arange(entries.shape[position]) // (entries.shape[position] // parts)).reshape((-1,) + (1,) * (entries.ndim - 1 - position))

    near = jax.random.permutation(key, parts)[block_of(target)]
    second = (block_of(target) + parts // 2) % parts
    return jnp.where((block_of(source) == near) | (block_of(source) == second), factor * entries, entries)


def block_levels(stream_key, dims, split, low, high):
    level, own = 1.0, jax.random.fold_in(stream_key, 6)
    for axis_at, blocks in split:
        heights = jnp.exp(jax.random.uniform(jax.random.fold_in(own, axis_at), (blocks,), jnp.float32, low / len(split), high / len(split)))
        level = level * jnp.repeat(heights, dims[axis_at] // blocks).reshape([-1 if axis == axis_at else 1 for axis in range(len(dims))])
    return level


def scatter_about(stream_key, shape, deviation, most, shards=(), kind=jnp.bfloat16):
    result = jax.random.normal(stream_key, shape, jnp.float32) * deviation
    if len(shards) > 0:
        result = block_levels(stream_key, shape, shards, -0.22, 0.18) * result
    return jnp.clip(result, min=-most, max=most).astype(kind)


def gaussian_with(stream_key, dims, scale, bound, pieces, heavy, kind=jnp.bfloat16):
    values = scale * jax.random.normal(stream_key, dims, jnp.float32)
    if pieces:
        values = values * block_levels(stream_key, dims, pieces, -0.22, 0.18)
    return jnp.clip(strengthened(values, jax.random.fold_in(stream_key, 3), *heavy), -bound, bound).astype(kind)


def setup_inputs(seed: int = 0) -> dict:
    splits = jax.random.split(jax.random.key(seed), 11)
    tokens = scatter_about(splits[0], (SEQS, LENGTH, D), 1.0, 6.0, ((0, 16), (1, 2)))
    input_gain = jnp.clip(1.0 + 0.18 * jax.random.normal(splits[1], (D,), jnp.float32), 0.099609375, 1.8984375).astype(jnp.bfloat16)
    qkv_weight = scatter_about(splits[2], (D, 3 * D), D ** -0.5, 0.1875, ((0, 8),))
    output_weight = scatter_about(splits[3], (D, D), (D // 64) ** -0.5, 1.5, ((0, 8),))
    mlp_gain = jnp.clip(1.0 + 0.18 * jax.random.normal(splits[4], (D,), jnp.float32), 0.099609375, 1.8984375).astype(jnp.bfloat16)
    expand_weight = scatter_about(splits[5], (D, 2 * FF), D ** -0.5, 0.1875, ((0, 8),))
    contract_weight = scatter_about(splits[6], (D, FF), FF ** -0.5, 0.125, ((0, 8),))
    positions = draw_positions(jax.random.fold_in(splits[10], 71), 0)
    mask_bias = draw_mask_bias(jax.random.fold_in(splits[10], 71), 0)
    cotangent = gaussian_with(splits[9], (SEQS, LENGTH, D), 1.0, 6.0, ((0, 16), (1, 2)), (0, 2, 16, 2.0))
    return {"tokens": tokens, "input_gain": input_gain, "qkv_weight": qkv_weight, "output_weight": output_weight, "mlp_gain": mlp_gain, "expand_weight": expand_weight, "contract_weight": contract_weight, "positions": positions, "mask_bias": mask_bias, "cotangent": cotangent}


EPS = 1e-05
THETA = 10000.0

def widen(values):
    return lax.optimization_barrier(values).astype(jnp.float32)

def layer_norm(values, gain):
    center = values - lax.optimization_barrier(jnp.mean(values, axis=-1, keepdims=True))
    variance = lax.optimization_barrier(jnp.mean(center * center, axis=-1, keepdims=True))
    scaled = lax.rsqrt(variance + EPS)
    normed = center * scaled
    return (normed, scaled, (normed * gain.astype(jnp.float32)).astype(jnp.bfloat16))

def layer_norm_back(incoming, normed, scaled, gain):
    weighted = incoming * gain.astype(jnp.float32)
    gain_grad = lax.optimization_barrier(jnp.sum(incoming * normed, axis=0))
    mean_one = lax.optimization_barrier(jnp.mean(weighted, axis=-1, keepdims=True))
    mean_two = lax.optimization_barrier(jnp.mean(weighted * normed, axis=-1, keepdims=True))
    return (scaled * (weighted - mean_one - normed * mean_two), gain_grad)

def rope_tables(positions, head_size):
    half_dim = head_size // 2
    exponent = jnp.arange(half_dim, dtype=jnp.float32) * (2.0 / head_size)
    frequency = jnp.exp(-math.log(THETA) * exponent)
    angles = positions.astype(jnp.float32)[:, None] * frequency[None, :]
    return (jnp.cos(angles)[:, None, :], jnp.sin(angles)[:, None, :])

def rotate(values, cosine, sine):
    half_dim = values.shape[-1] // 2
    lower_half, upper_half = (values[..., :half_dim], values[..., half_dim:])
    return jnp.concatenate([lower_half * cosine - upper_half * sine, upper_half * cosine + lower_half * sine], axis=-1)

def rotate_back(values, cosine, sine):
    half_dim = values.shape[-1] // 2
    lower_half, upper_half = (values[..., :half_dim], values[..., half_dim:])
    return jnp.concatenate([lower_half * cosine + upper_half * sine, upper_half * cosine - lower_half * sine], axis=-1)

def gelu_slope(values):
    cdf_part = 0.5 * (1.0 + jax.scipy.special.erf(values * (1.0 / math.sqrt(2.0))))
    density = jnp.exp(-0.5 * values * values) * (1.0 / math.sqrt(2.0 * math.pi))
    return cdf_part + values * density

def block_scores(queries, key_rows, additive):
    factor = 1.0 / math.sqrt(queries.shape[-1])
    scores = jnp.einsum('qhd,khd->hqk', widen(queries), widen(key_rows), precision=lax.Precision.HIGHEST)
    return scores * factor + additive[None]

def attend(queries, key_rows, value_rows, additive):
    scores = block_scores(queries, key_rows, additive)
    row_peak = lax.optimization_barrier(jnp.max(scores, axis=-1, keepdims=True))
    exponent = jnp.exp(scores - row_peak)
    row_total = lax.optimization_barrier(jnp.sum(exponent, axis=-1, keepdims=True))
    soft_weights = (exponent / row_total).astype(jnp.bfloat16)
    mixed = jnp.einsum('hqk,khd->qhd', widen(soft_weights), widen(value_rows), precision=lax.Precision.HIGHEST)
    return (mixed.astype(jnp.bfloat16), row_peak[..., 0] + jnp.log(row_total[..., 0]))

def attend_back(queries, key_rows, value_rows, additive, log_total, d_mixed):
    factor = 1.0 / math.sqrt(queries.shape[-1])
    scores = block_scores(queries, key_rows, additive)
    recomputed = jnp.exp(scores - log_total[..., None])
    d_soft = jnp.einsum('qhd,khd->hqk', widen(d_mixed), widen(value_rows), precision=lax.Precision.HIGHEST)
    center = lax.optimization_barrier(jnp.sum(recomputed * d_soft, axis=-1, keepdims=True))
    d_scores = (recomputed * (d_soft - center) * factor).astype(jnp.bfloat16)
    d_queries = jnp.einsum('hqk,khd->qhd', widen(d_scores), widen(key_rows), precision=lax.Precision.HIGHEST)
    d_keys = jnp.einsum('hqk,qhd->khd', widen(d_scores), widen(queries), precision=lax.Precision.HIGHEST)
    soft_round = recomputed.astype(jnp.bfloat16)
    d_values = jnp.einsum('hqk,qhd->khd', widen(soft_round), widen(d_mixed), precision=lax.Precision.HIGHEST)
    return (d_queries, d_keys, d_values)

def one_sequence(weights, inputs):
    input_gain, qkv_weight, output_weight, mlp_gain, expand_weight, contract_weight = weights
    tokens, positions, mask_bias, cotangent = inputs
    length = tokens.shape[0]
    block_count = length // BLOCK
    extent = BLOCK + 2 * HALF
    residual = tokens.astype(jnp.float32)
    normed1, scaled1, xn1 = layer_norm(residual, input_gain)
    projected = jnp.dot(xn1, qkv_weight, preferred_element_type=jnp.float32).reshape(length, 3, HEADS, HEAD_DIM)
    cosine, sine = rope_tables(positions, HEAD_DIM)
    queries = rotate(projected[:, 0], cosine, sine).astype(jnp.bfloat16)
    key_rows = rotate(projected[:, 1], cosine, sine).astype(jnp.bfloat16)
    value_rows = projected[:, 2].astype(jnp.bfloat16)
    window = (jnp.arange(block_count, dtype=jnp.int32)[:, None] * BLOCK + jnp.arange(extent, dtype=jnp.int32)[None, :]).astype(jnp.int32)
    key_pad = jnp.pad(key_rows, ((HALF, HALF), (0, 0), (0, 0)))
    value_pad = jnp.pad(value_rows, ((HALF, HALF), (0, 0), (0, 0)))
    key_window = key_pad[window]
    value_window = value_pad[window]
    query_blocks = queries.reshape(block_count, BLOCK, HEADS, HEAD_DIM)
    bias_blocks = mask_bias.reshape(block_count, BLOCK, extent)
    mixed, log_total = jax.vmap(attend)(query_blocks, key_window, value_window, bias_blocks)
    attention = mixed.reshape(length, D)
    hidden = residual + jnp.dot(attention, output_weight, preferred_element_type=jnp.float32)
    normed2, scaled2, xn2 = layer_norm(hidden, mlp_gain)
    lifted = jnp.dot(xn2, expand_weight, preferred_element_type=jnp.float32)
    gelu_input = lifted[:, :FF]
    gate_part = lifted[:, FF:]
    activated = jax.nn.gelu(gelu_input, approximate=False)
    gated = (activated * gate_part).astype(jnp.bfloat16)
    layer_out = (hidden + jnp.dot(gated, contract_weight.T, preferred_element_type=jnp.float32)).astype(jnp.bfloat16)
    grad_out = cotangent.astype(jnp.float32)
    contract_grad = jnp.dot(cotangent.T, gated, preferred_element_type=jnp.float32)
    d_gated = jnp.dot(cotangent, contract_weight, preferred_element_type=jnp.float32)
    d_lifted = jnp.concatenate([d_gated * gate_part * gelu_slope(gelu_input), d_gated * activated], axis=1).astype(jnp.bfloat16)
    expand_grad = jnp.dot(xn2.T, d_lifted, preferred_element_type=jnp.float32)
    d_xn2 = jnp.dot(d_lifted, expand_weight.T, preferred_element_type=jnp.float32)
    d_norm2, mlp_gain_grad = layer_norm_back(d_xn2, normed2, scaled2, mlp_gain)
    d_hidden = grad_out + d_norm2
    d_proj = d_hidden.astype(jnp.bfloat16)
    output_grad = jnp.dot(attention.T, d_proj, preferred_element_type=jnp.float32)
    d_attention = jnp.dot(d_proj, output_weight.T, preferred_element_type=jnp.float32).astype(jnp.bfloat16)
    d_queries, d_key_win, d_value_win = jax.vmap(attend_back)(query_blocks, key_window, value_window, bias_blocks, log_total, d_attention.reshape(block_count, BLOCK, HEADS, HEAD_DIM))
    d_keys = jnp.zeros((length + 2 * HALF, HEADS, HEAD_DIM), jnp.float32).at[window].add(d_key_win)[HALF:HALF + length]
    d_values = jnp.zeros((length + 2 * HALF, HEADS, HEAD_DIM), jnp.float32).at[window].add(d_value_win)[HALF:HALF + length]
    d_queries = rotate_back(d_queries.reshape(length, HEADS, HEAD_DIM), cosine, sine)
    d_keys = rotate_back(d_keys, cosine, sine)
    d_projected = jnp.concatenate([d_queries.reshape(length, D), d_keys.reshape(length, D), d_values.reshape(length, D)], axis=1).astype(jnp.bfloat16)
    qkv_grad = jnp.dot(xn1.T, d_projected, preferred_element_type=jnp.float32)
    d_xn1 = jnp.dot(d_projected, qkv_weight.T, preferred_element_type=jnp.float32)
    d_norm1, input_gain_grad = layer_norm_back(d_xn1, normed1, scaled1, input_gain)
    input_grad = (d_hidden + d_norm1).astype(jnp.bfloat16)
    return ((layer_out, input_grad), (input_gain_grad, qkv_grad, output_grad, mlp_gain_grad, expand_grad, contract_grad))

def reference(tokens, input_gain, qkv_weight, output_weight, mlp_gain, expand_weight, contract_weight, positions, mask_bias, cotangent):
    weights = (input_gain, qkv_weight, output_weight, mlp_gain, expand_weight, contract_weight)
    starting = jax.tree.map(lambda weight: jnp.zeros(weight.shape, jnp.float32), weights)

    def scan_step(running, inputs):
        outputs, grads = one_sequence(weights, inputs)
        return (jax.tree.map(lambda one, two: one + two, running, grads), outputs)
    summed, outputs = lax.scan(scan_step, starting, (tokens, positions, mask_bias, cotangent))
    layer_out, input_grad = outputs
    return (layer_out, input_grad, summed[0], summed[1], summed[2], summed[3], summed[4], summed[5])
```

```python
import math

import jax
import jax.numpy as jnp
from jax import lax
from jax.sharding import PartitionSpec as P

HEAD_DIM = 64
HALF = 64


EPS = 1e-05
THETA = 10000.0


def extended_2(cells, sides, width):
    for axis, dim in sides:
        count = lax.axis_size(axis)
        ends = count - 1
        head = lax.slice_in_dim(cells, 0, width, axis=dim)
        tail = lax.slice_in_dim(cells, cells.shape[dim] - width, cells.shape[dim], axis=dim)
        cells = jnp.concatenate(
            [
                lax.ppermute(tail, axis, [(i, (i + 1) % count) for i in range(ends)]),
                cells,
                lax.ppermute(head, axis, [((i + 1) % count, i) for i in range(ends)]),
            ],
            axis=dim,
        )
    return cells


def from_behind(value, axis, steps):
    count = lax.axis_size(axis)
    first, last = (max(0, -steps), min(count, count - steps))
    return lax.ppermute(value, axis, [(source, source + steps) for source in range(first, last)])


def layer_norm(values, gain):
    center = values - jnp.mean(values, axis=-1, keepdims=True)
    variance = jnp.mean(center * center, axis=-1, keepdims=True)
    scaled = lax.rsqrt(variance + EPS)
    normed = center * scaled
    return (normed, scaled, (normed * gain.astype(jnp.float32)).astype(jnp.bfloat16))


def layer_norm_back(incoming, normed, scaled, gain):
    weighted = incoming * gain.astype(jnp.float32)
    gain_grad = jnp.sum(incoming * normed, axis=0)
    mean_one = jnp.mean(weighted, axis=-1, keepdims=True)
    mean_two = jnp.mean(weighted * normed, axis=-1, keepdims=True)
    return (scaled * (weighted - mean_one - normed * mean_two), gain_grad)


def rope_tables(positions, head_size):
    half_dim = head_size // 2
    exponent = jnp.arange(half_dim, dtype=jnp.float32) * (2.0 / head_size)
    frequency = jnp.exp(-math.log(THETA) * exponent)
    angles = positions.astype(jnp.float32)[:, None] * frequency[None, :]
    return (jnp.cos(angles)[:, None, :], jnp.sin(angles)[:, None, :])


def rotate(values, cosine, sine):
    half_dim = values.shape[-1] // 2
    lower_half, upper_half = (values[..., :half_dim], values[..., half_dim:])
    return jnp.concatenate(
        [lower_half * cosine - upper_half * sine, upper_half * cosine + lower_half * sine], axis=-1
    )


def rotate_back(values, cosine, sine):
    half_dim = values.shape[-1] // 2
    lower_half, upper_half = (values[..., :half_dim], values[..., half_dim:])
    return jnp.concatenate(
        [lower_half * cosine + upper_half * sine, upper_half * cosine - lower_half * sine], axis=-1
    )


def gelu_slope(values):
    cdf_part = 0.5 * (1.0 + jax.scipy.special.erf(values * (1.0 / math.sqrt(2.0))))
    density = jnp.exp(-0.5 * values * values) * (1.0 / math.sqrt(2.0 * math.pi))
    return cdf_part + values * density


def block_scores(queries, key_rows, additive):
    factor = 1.0 / math.sqrt(queries.shape[-1])
    scores = jnp.einsum("qhd,khd->hqk", queries, key_rows, preferred_element_type=jnp.float32)
    return scores * factor + additive[None]


def attend(queries, key_rows, value_rows, additive):
    scores = block_scores(queries, key_rows, additive)
    row_peak = jnp.max(scores, axis=-1, keepdims=True)
    exponent = jnp.exp(scores - row_peak)
    row_total = jnp.sum(exponent, axis=-1, keepdims=True)
    soft_weights = (exponent / row_total).astype(jnp.bfloat16)
    mixed = jnp.einsum("hqk,khd->qhd", soft_weights, value_rows, preferred_element_type=jnp.float32)
    return (mixed.astype(jnp.bfloat16), row_peak[..., 0] + jnp.log(row_total[..., 0]))


def attend_back(queries, key_rows, value_rows, additive, log_total, d_mixed):
    factor = 1.0 / math.sqrt(queries.shape[-1])
    scores = block_scores(queries, key_rows, additive)
    recomputed = jnp.exp(scores - log_total[..., None])
    d_soft = jnp.einsum("qhd,khd->hqk", d_mixed, value_rows, preferred_element_type=jnp.float32)
    center = jnp.sum(recomputed * d_soft, axis=-1, keepdims=True)
    d_scores = (recomputed * (d_soft - center) * factor).astype(jnp.bfloat16)
    d_queries = jnp.einsum("hqk,khd->qhd", d_scores, key_rows, preferred_element_type=jnp.float32)
    d_keys = jnp.einsum("hqk,qhd->khd", d_scores, queries, preferred_element_type=jnp.float32)
    d_values = jnp.einsum(
        "hqk,qhd->khd", recomputed.astype(jnp.bfloat16), d_mixed, preferred_element_type=jnp.float32
    )
    return (d_queries, d_keys, d_values)


def body_generic(
    tokens,
    input_gain,
    qkv_weight,
    output_weight,
    mlp_gain,
    expand_weight,
    contract_weight,
    positions,
    mask_bias,
    cotangent,
):
    gathered = (
        lax.all_gather(input_gain, ("fsdp", "ctx"), axis=0, tiled=True),
        lax.all_gather(qkv_weight, ("fsdp", "ctx"), axis=0, tiled=True),
        lax.all_gather(output_weight, ("fsdp", "ctx"), axis=0, tiled=True),
        lax.all_gather(mlp_gain, ("fsdp", "ctx"), axis=0, tiled=True),
        lax.all_gather(expand_weight, ("fsdp", "ctx"), axis=0, tiled=True),
        lax.all_gather(contract_weight, ("fsdp", "ctx"), axis=0, tiled=True),
    )
    full_input_gain, full_qkv, full_output, full_mlp_gain, full_expand, full_contract = gathered
    residual = tokens[0].astype(jnp.float32)
    row_count, model_width = residual.shape
    head_count = model_width // HEAD_DIM
    cosine, sine = rope_tables(positions[0], HEAD_DIM)
    normed1, scaled1, xn1 = layer_norm(residual, full_input_gain)
    projected = jnp.dot(xn1, full_qkv, preferred_element_type=jnp.float32).reshape(
        row_count, 3, head_count, HEAD_DIM
    )
    queries = rotate(projected[:, 0], cosine, sine).astype(jnp.bfloat16)
    key_rows = rotate(projected[:, 1], cosine, sine).astype(jnp.bfloat16)
    value_rows = projected[:, 2].astype(jnp.bfloat16)
    packed = jnp.concatenate(
        [key_rows.reshape(row_count, model_width), value_rows.reshape(row_count, model_width)],
        axis=1,
    )
    extended = extended_2(packed, (("ctx", 0),), HALF)
    extent = extended.shape[0]
    key_ext = extended[:, :model_width].reshape(extent, head_count, HEAD_DIM)
    value_ext = extended[:, model_width:].reshape(extent, head_count, HEAD_DIM)
    additive = mask_bias[0]
    mixed, log_total = attend(queries, key_ext, value_ext, additive)
    attention = mixed.reshape(row_count, model_width)
    hidden = residual + jnp.dot(attention, full_output, preferred_element_type=jnp.float32)
    normed2, scaled2, xn2 = layer_norm(hidden, full_mlp_gain)
    lifted = jnp.dot(xn2, full_expand, preferred_element_type=jnp.float32)
    ff_width = lifted.shape[1] // 2
    gelu_input = lifted[:, :ff_width]
    gate_part = lifted[:, ff_width:]
    activated = jax.nn.gelu(gelu_input, approximate=False)
    gated = (activated * gate_part).astype(jnp.bfloat16)
    down_out = jnp.einsum("tf,jf->tj", gated, full_contract, preferred_element_type=jnp.float32)
    layer_out = (hidden + down_out).astype(jnp.bfloat16)
    back_input_gain, back_qkv, back_output, back_mlp_gain, back_expand, back_contract = gathered
    grad_out = cotangent[0]
    d_gated = jnp.dot(grad_out, back_contract, preferred_element_type=jnp.float32)
    d_lifted = jnp.concatenate(
        [d_gated * gate_part * gelu_slope(gelu_input), d_gated * activated], axis=1
    ).astype(jnp.bfloat16)
    d_xn2 = jnp.einsum("tc,dc->td", d_lifted, back_expand, preferred_element_type=jnp.float32)
    d_norm2, mlp_gain_term = layer_norm_back(d_xn2, normed2, scaled2, back_mlp_gain)
    d_hidden = grad_out.astype(jnp.float32) + d_norm2
    d_proj = d_hidden.astype(jnp.bfloat16)
    d_attention = jnp.einsum(
        "tj,ij->ti", d_proj, back_output, preferred_element_type=jnp.float32
    ).astype(jnp.bfloat16)
    d_queries, d_key_ext, d_value_ext = attend_back(
        queries,
        key_ext,
        value_ext,
        additive,
        log_total,
        d_attention.reshape(row_count, head_count, HEAD_DIM),
    )
    grad_ext = jnp.concatenate(
        [d_key_ext.reshape(extent, model_width), d_value_ext.reshape(extent, model_width)], axis=1
    )
    from_next = from_behind(grad_ext[:HALF], "ctx", -1)
    from_prev = from_behind(grad_ext[row_count + HALF :], "ctx", 1)
    grad_kv = grad_ext[HALF : HALF + row_count]
    grad_kv = grad_kv + jnp.pad(from_prev, ((0, row_count - HALF), (0, 0)))
    grad_kv = grad_kv + jnp.pad(from_next, ((row_count - HALF, 0), (0, 0)))
    d_keys = rotate_back(
        grad_kv[:, :model_width].reshape(row_count, head_count, HEAD_DIM), cosine, sine
    )
    d_values = grad_kv[:, model_width:]
    d_queries = rotate_back(d_queries, cosine, sine)
    d_projected = jnp.concatenate(
        [
            d_queries.reshape(row_count, model_width),
            d_keys.reshape(row_count, model_width),
            d_values,
        ],
        axis=1,
    ).astype(jnp.bfloat16)
    d_xn1 = jnp.einsum("tc,dc->td", d_projected, back_qkv, preferred_element_type=jnp.float32)
    d_norm1, input_gain_term = layer_norm_back(d_xn1, normed1, scaled1, back_input_gain)
    input_grad = (d_hidden + d_norm1).astype(jnp.bfloat16)
    left_one, left_two, left_three, left_four = (xn1, attention, xn2, grad_out)
    gain_one, gain_two = (input_gain_term, mlp_gain_term)
    qkv_term = jnp.einsum("ti,tj->ij", left_one, d_projected, preferred_element_type=jnp.float32)
    output_term = jnp.einsum("ti,tj->ij", left_two, d_proj, preferred_element_type=jnp.float32)
    expand_term = jnp.einsum("ti,tj->ij", left_three, d_lifted, preferred_element_type=jnp.float32)
    contract_term = jnp.einsum("ti,tj->ij", left_four, gated, preferred_element_type=jnp.float32)
    first_gain = gain_one[:, None]
    second_gain = gain_two[:, None]
    shares = lax.psum_scatter(
        jnp.concatenate(
            [qkv_term, output_term, expand_term, contract_term, first_gain, second_gain], axis=1
        ),
        ("fsdp", "ctx"),
        scatter_dimension=0,
        tiled=True,
    )
    result = lax.psum(shares, "replica")
    qkv_cols = 3 * model_width
    expand_cols = 2 * ff_width
    qkv_grad = result[:, :qkv_cols]
    output_grad = result[:, qkv_cols : qkv_cols + model_width]
    offset = qkv_cols + model_width
    expand_grad = result[:, offset : offset + expand_cols]
    offset = offset + expand_cols
    contract_grad = result[:, offset : offset + ff_width]
    offset = offset + ff_width
    input_gain_grad = result[:, offset]
    mlp_gain_grad = result[:, offset + 1]
    return (
        layer_out[None],
        input_grad[None],
        input_gain_grad,
        qkv_grad,
        output_grad,
        mlp_gain_grad,
        expand_grad,
        contract_grad,
    )


X_BIT, CORE_BIT, Y_BIT = (1, 2, 4)
PLANE = ("fsdp", "ctx")
PLANE_SIZE = 8


def swap(value, bit):
    return lax.ppermute(value, PLANE, [(i, i ^ bit) for i in range(PLANE_SIZE)])


def reorder(values, me):
    width = values.shape[1] // PLANE_SIZE
    return jnp.concatenate(
        [
            lax.dynamic_slice_in_dim(values, (me ^ block) * width, width, axis=1)
            for block in range(PLANE_SIZE)
        ],
        axis=1,
    )


def gather_rows(own, after=None):
    if after is not None:
        own, _ = lax.optimization_barrier((own, after))
    half = own.shape[0] // 2
    over_x = swap(own, X_BIT)
    over_y = swap(own, Y_BIT)
    corner = jnp.concatenate([swap(over_x[:half], Y_BIT), swap(over_y[half:], X_BIT)], axis=0)
    first = [own, over_x, over_y, corner]
    second = [swap(part, CORE_BIT) for part in first]
    full = jnp.concatenate(
        [first[0], first[1], second[0], second[1], first[2], first[3], second[2], second[3]], axis=0
    )
    return (full, (over_x, over_y))


def line_sum(part):
    first = lax.ppermute(part.astype(jnp.bfloat16), "replica", [(0, 1), (3, 2)])
    pair = (part + first.astype(jnp.float32)).astype(jnp.bfloat16)
    other = lax.ppermute(pair, "replica", [(1, 2), (2, 1)])
    total = (pair.astype(jnp.float32) + other.astype(jnp.float32)).astype(jnp.bfloat16)
    back = lax.ppermute(total, "replica", [(1, 0), (2, 3)])
    place = lax.axis_index("replica")
    middle = (place == 1) | (place == 2)
    return jnp.where(middle, total, back).astype(jnp.float32)


def grad_rows(left, right, gather_bit, sum_bit):
    rows = left.shape[0]
    width = left.shape[1] // PLANE_SIZE
    cols = right.shape[1]
    block = lambda values, o: values[:, o * width : (o + 1) * width]
    keep = [0, CORE_BIT, sum_bit, CORE_BIT | sum_bit]
    packed = jnp.concatenate([right] + [block(left, o | gather_bit) for o in keep], axis=1)
    mine = jnp.concatenate([right] + [block(left, o) for o in keep], axis=1)
    both = jnp.concatenate([mine, swap(packed, gather_bit)], axis=0)
    tail = lambda k: both[:, cols + k * width : cols + (k + 1) * width]
    other = swap(jnp.concatenate([both[:, :cols], tail(1), tail(3)], axis=1), CORE_BIT)
    rights = jnp.concatenate([both[:, :cols], other[:, :cols]], axis=0)
    lefts = [
        jnp.concatenate([tail(0), other[:, cols : cols + width]], axis=0),
        jnp.concatenate([tail(2), other[:, cols + width :]], axis=0),
    ]
    product = lambda one: jnp.einsum("ti,tj->ij", one, rights, preferred_element_type=jnp.float32)
    sent = swap(product(lefts[1]).astype(jnp.bfloat16), sum_bit)
    return line_sum(product(lefts[0]) + sent.astype(jnp.float32))


def halo_rows(values):
    place = lax.axis_index("ctx")
    head, tail = (values[:HALF], values[values.shape[0] - HALF :])
    got = swap(jnp.where(place == 0, tail, head), X_BIT)
    none = jnp.zeros_like(got)
    return jnp.concatenate(
        [jnp.where(place == 0, none, got), values, jnp.where(place == 0, got, none)], axis=0
    )


def halo_sum(values, row_count):
    place = lax.axis_index("ctx")
    head, tail = (values[:HALF], values[row_count + HALF :])
    got = swap(jnp.where(place == 0, tail, head), X_BIT)
    none = jnp.zeros((row_count - HALF, values.shape[1]), values.dtype)
    return values[HALF : HALF + row_count] + jnp.where(
        place == 0, jnp.concatenate([none, got], axis=0), jnp.concatenate([got, none], axis=0)
    )


def body_plane(
    tokens,
    input_gain,
    qkv_weight,
    output_weight,
    mlp_gain,
    expand_weight,
    contract_weight,
    positions,
    mask_bias,
    cotangent,
):
    me = lax.axis_index(PLANE)
    shard, qkv_cols = qkv_weight.shape
    gains = jnp.stack([input_gain, mlp_gain], axis=1)
    gains = jnp.pad(gains, ((0, 0), (0, 126)))
    packed_one, arrived = gather_rows(jnp.concatenate([qkv_weight, output_weight, gains], axis=1))
    full_expand, arrived = gather_rows(expand_weight, arrived)
    full_contract, arrived = gather_rows(contract_weight, arrived)
    residual = tokens[0].astype(jnp.float32)
    row_count, model_width = residual.shape
    full_qkv = packed_one[:, :qkv_cols]
    full_output = packed_one[:, qkv_cols : qkv_cols + model_width]
    both_gains = packed_one[:, qkv_cols + model_width :][:, :2].T
    both_gains = reorder(both_gains, me)
    full_input_gain, full_mlp_gain = (both_gains[0], both_gains[1])
    head_count = model_width // HEAD_DIM
    cosine, sine = rope_tables(positions[0], HEAD_DIM)
    normed1, scaled1, xn1 = layer_norm(residual, full_input_gain)
    xn1 = reorder(xn1, me)
    projected = jnp.dot(xn1, full_qkv, preferred_element_type=jnp.float32).reshape(
        row_count, 3, head_count, HEAD_DIM
    )
    queries = rotate(projected[:, 0], cosine, sine).astype(jnp.bfloat16)
    key_rows = rotate(projected[:, 1], cosine, sine).astype(jnp.bfloat16)
    value_rows = projected[:, 2].astype(jnp.bfloat16)
    packed = jnp.concatenate(
        [key_rows.reshape(row_count, model_width), value_rows.reshape(row_count, model_width)],
        axis=1,
    )
    extended = halo_rows(packed)
    extent = extended.shape[0]
    key_ext = extended[:, :model_width].reshape(extent, head_count, HEAD_DIM)
    value_ext = extended[:, model_width:].reshape(extent, head_count, HEAD_DIM)
    additive = mask_bias[0]
    mixed, log_total = attend(queries, key_ext, value_ext, additive)
    attention = reorder(mixed.reshape(row_count, model_width), me)
    hidden = residual + jnp.dot(attention, full_output, preferred_element_type=jnp.float32)
    normed2, scaled2, xn2 = layer_norm(hidden, full_mlp_gain)
    xn2 = reorder(xn2, me)
    lifted = jnp.dot(xn2, full_expand, preferred_element_type=jnp.float32)
    ff_width = lifted.shape[1] // 2
    gelu_input = lifted[:, :ff_width]
    gate_part = lifted[:, ff_width:]
    activated = jax.nn.gelu(gelu_input, approximate=False)
    gated = (activated * gate_part).astype(jnp.bfloat16)
    grad_out = cotangent[0]
    grad_local = reorder(grad_out, me)
    contract_grad = grad_rows(grad_local, gated, X_BIT, Y_BIT)
    down_out = jnp.einsum("tf,jf->tj", gated, full_contract, preferred_element_type=jnp.float32)
    layer_out = (hidden + reorder(down_out, me)).astype(jnp.bfloat16)
    d_gated = jnp.dot(grad_local, full_contract, preferred_element_type=jnp.float32)
    d_first = (d_gated * gate_part * gelu_slope(gelu_input)).astype(jnp.bfloat16)
    d_second = (d_gated * activated).astype(jnp.bfloat16)
    expand_first = grad_rows(xn2, d_first, Y_BIT, X_BIT)
    expand_second = grad_rows(xn2, d_second, X_BIT, Y_BIT)
    d_xn2 = jnp.einsum(
        "tc,dc->td",
        jnp.concatenate([d_first, d_second], axis=1),
        full_expand,
        preferred_element_type=jnp.float32,
    )
    d_norm2, mlp_gain_term = layer_norm_back(reorder(d_xn2, me), normed2, scaled2, full_mlp_gain)
    d_hidden = grad_out.astype(jnp.float32) + d_norm2
    d_proj = d_hidden.astype(jnp.bfloat16)
    output_grad = grad_rows(attention, d_proj, Y_BIT, X_BIT)
    d_attention = jnp.einsum("tj,ij->ti", d_proj, full_output, preferred_element_type=jnp.float32)
    d_attention = reorder(d_attention.astype(jnp.bfloat16), me)
    d_queries, d_key_ext, d_value_ext = attend_back(
        queries,
        key_ext,
        value_ext,
        additive,
        log_total,
        d_attention.reshape(row_count, head_count, HEAD_DIM),
    )
    grad_ext = jnp.concatenate(
        [d_key_ext.reshape(extent, model_width), d_value_ext.reshape(extent, model_width)], axis=1
    )
    grad_kv = halo_sum(grad_ext, row_count)
    d_keys = rotate_back(
        grad_kv[:, :model_width].reshape(row_count, head_count, HEAD_DIM), cosine, sine
    )
    d_values = grad_kv[:, model_width:]
    d_queries = rotate_back(d_queries, cosine, sine)
    d_projected = jnp.concatenate(
        [
            d_queries.reshape(row_count, model_width),
            d_keys.reshape(row_count, model_width),
            d_values,
        ],
        axis=1,
    ).astype(jnp.bfloat16)
    middle = d_projected.shape[1] // 2
    qkv_first = grad_rows(xn1, d_projected[:, :middle], X_BIT, Y_BIT)
    qkv_second = grad_rows(xn1, d_projected[:, middle:], Y_BIT, X_BIT)
    d_xn1 = jnp.einsum("tc,dc->td", d_projected, full_qkv, preferred_element_type=jnp.float32)
    d_norm1, input_gain_term = layer_norm_back(reorder(d_xn1, me), normed1, scaled1, full_input_gain)
    input_grad = (d_hidden + d_norm1).astype(jnp.bfloat16)
    gain_sums = lax.psum(jnp.stack([input_gain_term, mlp_gain_term]), ("replica", "fsdp", "ctx"))
    gain_rows = lax.dynamic_slice_in_dim(gain_sums, me * shard, shard, axis=1)
    return (
        layer_out[None],
        input_grad[None],
        gain_rows[0],
        jnp.concatenate([qkv_first, qkv_second], axis=1),
        output_grad,
        gain_rows[1],
        jnp.concatenate([expand_first, expand_second], axis=1),
        contract_grad,
    )


def solution(mesh):
    in_specs = (
        P(("replica", "fsdp"), "ctx", None),
        P(("fsdp", "ctx")),
        P(("fsdp", "ctx"), None),
        P(("fsdp", "ctx"), None),
        P(("fsdp", "ctx")),
        P(("fsdp", "ctx"), None),
        P(("fsdp", "ctx"), None),
        P(("replica", "fsdp"), "ctx"),
        P(("replica", "fsdp"), "ctx", None),
        P(("replica", "fsdp"), "ctx", None),
    )
    out_specs = (
        P(("replica", "fsdp"), "ctx", None),
        P(("replica", "fsdp"), "ctx", None),
        P(("fsdp", "ctx")),
        P(("fsdp", "ctx"), None),
        P(("fsdp", "ctx"), None),
        P(("fsdp", "ctx")),
        P(("fsdp", "ctx"), None),
        P(("fsdp", "ctx"), None),
    )
    sizes = (mesh.shape["replica"], mesh.shape["fsdp"], mesh.shape["ctx"])
    body = body_plane if sizes == (4, 4, 2) else body_generic
    return jax.shard_map(body, mesh=mesh, in_specs=in_specs, out_specs=out_specs, check_vma=False)
```

```python
import math

import jax
import jax.numpy as jnp
from jax import lax
from jax.experimental import pallas as pl
from jax.experimental.pallas import tpu as pltpu
from jax.sharding import PartitionSpec as P

HEAD_DIM = 64
HALF = 64


EPS = 1e-05
THETA = 10000.0


def extended_2(cells, sides, width):
    for axis, dim in sides:
        count = lax.axis_size(axis)
        ends = count - 1
        head = lax.slice_in_dim(cells, 0, width, axis=dim)
        tail = lax.slice_in_dim(cells, cells.shape[dim] - width, cells.shape[dim], axis=dim)
        cells = jnp.concatenate(
            [
                lax.ppermute(tail, axis, [(i, (i + 1) % count) for i in range(ends)]),
                cells,
                lax.ppermute(head, axis, [((i + 1) % count, i) for i in range(ends)]),
            ],
            axis=dim,
        )
    return cells


def from_behind(value, axis, steps):
    count = lax.axis_size(axis)
    first, last = (max(0, -steps), min(count, count - steps))
    return lax.ppermute(value, axis, [(source, source + steps) for source in range(first, last)])


def layer_norm(values, gain):
    center = values - jnp.mean(values, axis=-1, keepdims=True)
    variance = jnp.mean(center * center, axis=-1, keepdims=True)
    scaled = lax.rsqrt(variance + EPS)
    normed = center * scaled
    return (normed, scaled, (normed * gain.astype(jnp.float32)).astype(jnp.bfloat16))


def layer_norm_back(incoming, normed, scaled, gain):
    weighted = incoming * gain.astype(jnp.float32)
    gain_grad = jnp.sum(incoming * normed, axis=0)
    mean_one = jnp.mean(weighted, axis=-1, keepdims=True)
    mean_two = jnp.mean(weighted * normed, axis=-1, keepdims=True)
    return (scaled * (weighted - mean_one - normed * mean_two), gain_grad)


def rope_tables(positions, head_size):
    half_dim = head_size // 2
    exponent = jnp.arange(half_dim, dtype=jnp.float32) * (2.0 / head_size)
    frequency = jnp.exp(-math.log(THETA) * exponent)
    angles = positions.astype(jnp.float32)[:, None] * frequency[None, :]
    return (jnp.cos(angles)[:, None, :], jnp.sin(angles)[:, None, :])


def rotate(values, cosine, sine):
    half_dim = values.shape[-1] // 2
    lower_half, upper_half = (values[..., :half_dim], values[..., half_dim:])
    return jnp.concatenate(
        [lower_half * cosine - upper_half * sine, upper_half * cosine + lower_half * sine], axis=-1
    )


def rotate_back(values, cosine, sine):
    half_dim = values.shape[-1] // 2
    lower_half, upper_half = (values[..., :half_dim], values[..., half_dim:])
    return jnp.concatenate(
        [lower_half * cosine + upper_half * sine, upper_half * cosine - lower_half * sine], axis=-1
    )


def gelu_slope(values):
    cdf_part = 0.5 * (1.0 + jax.scipy.special.erf(values * (1.0 / math.sqrt(2.0))))
    density = jnp.exp(-0.5 * values * values) * (1.0 / math.sqrt(2.0 * math.pi))
    return cdf_part + values * density


def block_scores(queries, key_rows, additive):
    factor = 1.0 / math.sqrt(queries.shape[-1])
    scores = jnp.einsum("qhd,khd->hqk", queries, key_rows, preferred_element_type=jnp.float32)
    return scores * factor + additive[None]


def attend(queries, key_rows, value_rows, additive):
    scores = block_scores(queries, key_rows, additive)
    row_peak = jnp.max(scores, axis=-1, keepdims=True)
    exponent = jnp.exp(scores - row_peak)
    row_total = jnp.sum(exponent, axis=-1, keepdims=True)
    soft_weights = (exponent / row_total).astype(jnp.bfloat16)
    mixed = jnp.einsum("hqk,khd->qhd", soft_weights, value_rows, preferred_element_type=jnp.float32)
    return (mixed.astype(jnp.bfloat16), row_peak[..., 0] + jnp.log(row_total[..., 0]))


def attend_back(queries, key_rows, value_rows, additive, log_total, d_mixed):
    factor = 1.0 / math.sqrt(queries.shape[-1])
    scores = block_scores(queries, key_rows, additive)
    recomputed = jnp.exp(scores - log_total[..., None])
    d_soft = jnp.einsum("qhd,khd->hqk", d_mixed, value_rows, preferred_element_type=jnp.float32)
    center = jnp.sum(recomputed * d_soft, axis=-1, keepdims=True)
    d_scores = (recomputed * (d_soft - center) * factor).astype(jnp.bfloat16)
    d_queries = jnp.einsum("hqk,khd->qhd", d_scores, key_rows, preferred_element_type=jnp.float32)
    d_keys = jnp.einsum("hqk,qhd->khd", d_scores, queries, preferred_element_type=jnp.float32)
    d_values = jnp.einsum(
        "hqk,qhd->khd", recomputed.astype(jnp.bfloat16), d_mixed, preferred_element_type=jnp.float32
    )
    return (d_queries, d_keys, d_values)


def body_generic(
    tokens,
    input_gain,
    qkv_weight,
    output_weight,
    mlp_gain,
    expand_weight,
    contract_weight,
    positions,
    mask_bias,
    cotangent,
):
    gathered = (
        lax.all_gather(input_gain, ("fsdp", "ctx"), axis=0, tiled=True),
        lax.all_gather(qkv_weight, ("fsdp", "ctx"), axis=0, tiled=True),
        lax.all_gather(output_weight, ("fsdp", "ctx"), axis=0, tiled=True),
        lax.all_gather(mlp_gain, ("fsdp", "ctx"), axis=0, tiled=True),
        lax.all_gather(expand_weight, ("fsdp", "ctx"), axis=0, tiled=True),
        lax.all_gather(contract_weight, ("fsdp", "ctx"), axis=0, tiled=True),
    )
    full_input_gain, full_qkv, full_output, full_mlp_gain, full_expand, full_contract = gathered
    residual = tokens[0].astype(jnp.float32)
    row_count, model_width = residual.shape
    head_count = model_width // HEAD_DIM
    cosine, sine = rope_tables(positions[0], HEAD_DIM)
    normed1, scaled1, xn1 = layer_norm(residual, full_input_gain)
    projected = jnp.dot(xn1, full_qkv, preferred_element_type=jnp.float32).reshape(
        row_count, 3, head_count, HEAD_DIM
    )
    queries = rotate(projected[:, 0], cosine, sine).astype(jnp.bfloat16)
    key_rows = rotate(projected[:, 1], cosine, sine).astype(jnp.bfloat16)
    value_rows = projected[:, 2].astype(jnp.bfloat16)
    packed = jnp.concatenate(
        [key_rows.reshape(row_count, model_width), value_rows.reshape(row_count, model_width)],
        axis=1,
    )
    extended = extended_2(packed, (("ctx", 0),), HALF)
    extent = extended.shape[0]
    key_ext = extended[:, :model_width].reshape(extent, head_count, HEAD_DIM)
    value_ext = extended[:, model_width:].reshape(extent, head_count, HEAD_DIM)
    additive = mask_bias[0]
    mixed, log_total = attend(queries, key_ext, value_ext, additive)
    attention = mixed.reshape(row_count, model_width)
    hidden = residual + jnp.dot(attention, full_output, preferred_element_type=jnp.float32)
    normed2, scaled2, xn2 = layer_norm(hidden, full_mlp_gain)
    lifted = jnp.dot(xn2, full_expand, preferred_element_type=jnp.float32)
    ff_width = lifted.shape[1] // 2
    gelu_input = lifted[:, :ff_width]
    gate_part = lifted[:, ff_width:]
    activated = jax.nn.gelu(gelu_input, approximate=False)
    gated = (activated * gate_part).astype(jnp.bfloat16)
    down_out = jnp.einsum("tf,jf->tj", gated, full_contract, preferred_element_type=jnp.float32)
    layer_out = (hidden + down_out).astype(jnp.bfloat16)
    back_input_gain, back_qkv, back_output, back_mlp_gain, back_expand, back_contract = gathered
    grad_out = cotangent[0]
    d_gated = jnp.dot(grad_out, back_contract, preferred_element_type=jnp.float32)
    d_lifted = jnp.concatenate(
        [d_gated * gate_part * gelu_slope(gelu_input), d_gated * activated], axis=1
    ).astype(jnp.bfloat16)
    d_xn2 = jnp.einsum("tc,dc->td", d_lifted, back_expand, preferred_element_type=jnp.float32)
    d_norm2, mlp_gain_term = layer_norm_back(d_xn2, normed2, scaled2, back_mlp_gain)
    d_hidden = grad_out.astype(jnp.float32) + d_norm2
    d_proj = d_hidden.astype(jnp.bfloat16)
    d_attention = jnp.einsum(
        "tj,ij->ti", d_proj, back_output, preferred_element_type=jnp.float32
    ).astype(jnp.bfloat16)
    d_queries, d_key_ext, d_value_ext = attend_back(
        queries,
        key_ext,
        value_ext,
        additive,
        log_total,
        d_attention.reshape(row_count, head_count, HEAD_DIM),
    )
    grad_ext = jnp.concatenate(
        [d_key_ext.reshape(extent, model_width), d_value_ext.reshape(extent, model_width)], axis=1
    )
    from_next = from_behind(grad_ext[:HALF], "ctx", -1)
    from_prev = from_behind(grad_ext[row_count + HALF :], "ctx", 1)
    grad_kv = grad_ext[HALF : HALF + row_count]
    grad_kv = grad_kv + jnp.pad(from_prev, ((0, row_count - HALF), (0, 0)))
    grad_kv = grad_kv + jnp.pad(from_next, ((row_count - HALF, 0), (0, 0)))
    d_keys = rotate_back(
        grad_kv[:, :model_width].reshape(row_count, head_count, HEAD_DIM), cosine, sine
    )
    d_values = grad_kv[:, model_width:]
    d_queries = rotate_back(d_queries, cosine, sine)
    d_projected = jnp.concatenate(
        [
            d_queries.reshape(row_count, model_width),
            d_keys.reshape(row_count, model_width),
            d_values,
        ],
        axis=1,
    ).astype(jnp.bfloat16)
    d_xn1 = jnp.einsum("tc,dc->td", d_projected, back_qkv, preferred_element_type=jnp.float32)
    d_norm1, input_gain_term = layer_norm_back(d_xn1, normed1, scaled1, back_input_gain)
    input_grad = (d_hidden + d_norm1).astype(jnp.bfloat16)
    left_one, left_two, left_three, left_four = (xn1, attention, xn2, grad_out)
    gain_one, gain_two = (input_gain_term, mlp_gain_term)
    qkv_term = jnp.einsum("ti,tj->ij", left_one, d_projected, preferred_element_type=jnp.float32)
    output_term = jnp.einsum("ti,tj->ij", left_two, d_proj, preferred_element_type=jnp.float32)
    expand_term = jnp.einsum("ti,tj->ij", left_three, d_lifted, preferred_element_type=jnp.float32)
    contract_term = jnp.einsum("ti,tj->ij", left_four, gated, preferred_element_type=jnp.float32)
    first_gain = gain_one[:, None]
    second_gain = gain_two[:, None]
    shares = lax.psum_scatter(
        jnp.concatenate(
            [qkv_term, output_term, expand_term, contract_term, first_gain, second_gain], axis=1
        ),
        ("fsdp", "ctx"),
        scatter_dimension=0,
        tiled=True,
    )
    result = lax.psum(shares, "replica")
    qkv_cols = 3 * model_width
    expand_cols = 2 * ff_width
    qkv_grad = result[:, :qkv_cols]
    output_grad = result[:, qkv_cols : qkv_cols + model_width]
    offset = qkv_cols + model_width
    expand_grad = result[:, offset : offset + expand_cols]
    offset = offset + expand_cols
    contract_grad = result[:, offset : offset + ff_width]
    offset = offset + ff_width
    input_gain_grad = result[:, offset]
    mlp_gain_grad = result[:, offset + 1]
    return (
        layer_out[None],
        input_grad[None],
        input_gain_grad,
        qkv_grad,
        output_grad,
        mlp_gain_grad,
        expand_grad,
        contract_grad,
    )


X_BIT, CORE_BIT, Y_BIT = (1, 2, 4)
PLANE = ("fsdp", "ctx")
PLANE_SIZE = 8
PIECES = 10
VMEM_BYTES = 50 * 1024 * 1024
F32, BF16 = (jnp.float32, jnp.bfloat16)


def swap(value, bit):
    return lax.ppermute(value, PLANE, [(i, i ^ bit) for i in range(PLANE_SIZE)])


def gather_pieces(own, after=None):
    if after is not None:
        own, _ = lax.optimization_barrier((own, after))
    half = own.shape[0] // 2
    over_x = swap(own, X_BIT)
    over_y = swap(own, Y_BIT)
    first = [own, over_x, over_y, swap(over_x[:half], Y_BIT), swap(over_y[half:], X_BIT)]
    second = [swap(part, CORE_BIT) for part in first]
    return (first + second, (over_x, over_y))


def fill(pieces, target, sems, me, columns=None):
    shard = target.shape[0] // PLANE_SIZE
    half = shard // 2
    corner = X_BIT | Y_BIT
    places = [(0, 0, shard), (X_BIT, 0, shard), (Y_BIT, 0, shard), (corner, 0, half), (corner, half, half)]
    places = places + [(offset | CORE_BIT, start, rows) for offset, start, rows in places]
    copies = []
    for index, (piece, (offset, start, rows)) in enumerate(zip(pieces, places)):
        row = pl.multiple_of((me ^ offset) * shard + start, half)
        source = piece if columns is None else piece.at[:, columns]
        copies.append(pltpu.make_async_copy(source, target.at[pl.ds(row, rows)], sems.at[index]))
    for copy in copies:
        copy.start()
    return copies


def wait_all(copies):
    for copy in copies:
        copy.wait()


def pack(keep, send, left, right, gather_bit, sum_bit, me):
    width = left.shape[1] // PLANE_SIZE
    for slot, offset in enumerate([0, CORE_BIT, sum_bit, CORE_BIT | sum_bit]):
        for target, flip in ((keep, 0), (send, gather_bit)):
            source = pl.multiple_of((me ^ (offset | flip)) * width, width)
            target[:, slot * width : (slot + 1) * width] = left[:, pl.ds(source, width)]
    keep[:, 4 * width :] = right
    send[:, 4 * width :] = right


def turn(values, cosine, sine):
    lane = lax.broadcasted_iota(jnp.int32, values.shape, 1)
    low = lane % HEAD_DIM < HEAD_DIM // 2
    other = jnp.where(
        low,
        pltpu.roll(values, values.shape[1] - HEAD_DIM // 2, 1),
        pltpu.roll(values, HEAD_DIM // 2, 1),
    )
    return values * cosine + other * sine


def dot_tt(one, two):
    return lax.dot_general(one, two, (((0,), (0,)), ((), ())), preferred_element_type=F32)


def dot_nt(one, two):
    return lax.dot_general(one, two, (((1,), (1,)), ((), ())), preferred_element_type=F32)


def dot_nn(one, two):
    return jnp.dot(one, two, preferred_element_type=F32)


def norm_parts(values):
    center = values - jnp.mean(values, axis=-1, keepdims=True)
    variance = jnp.mean(center * center, axis=-1, keepdims=True)
    scaled = lax.rsqrt(variance + EPS)
    return (center * scaled, scaled)


def norm_back(incoming, normed, scaled, gain):
    weighted = incoming * gain
    gain_grad = jnp.sum(incoming * normed, axis=0, keepdims=True)
    mean_one = jnp.mean(weighted, axis=-1, keepdims=True)
    mean_two = jnp.mean(weighted * normed, axis=-1, keepdims=True)
    return (scaled * (weighted - mean_one - normed * mean_two), gain_grad)


def front_kernel(place, tokens, cosine, sine, *refs):
    pieces, (queries, keys_values, edge, xn1, gains, weight, sems) = (refs[:PIECES], refs[PIECES:])
    me, along = (place[0], place[1])
    copies = fill(pieces, weight, sems, me)
    normed, _ = norm_parts(tokens[...].astype(F32))
    width = tokens.shape[1]
    wait_all(copies)
    turned = weight[:, 4 * width :].astype(F32).T
    gains[...] = turned[: gains.shape[0]]
    rounded = (normed * gains[0:1, :]).astype(BF16)
    xn1[...] = rounded
    pair = cosine.shape[1]
    projected = dot_nn(rounded, weight[:, : 3 * width])
    for start in range(0, width, pair):
        part = projected[:, start : start + pair]
        queries[:, start : start + pair] = turn(part, cosine[...], sine[...]).astype(BF16)
        part = projected[:, width + start : width + start + pair]
        keys_values[:, start : start + pair] = turn(part, cosine[...], sine[...]).astype(BF16)
    keys_values[:, width:] = projected[:, 2 * width :].astype(BF16)
    rows = edge.shape[0]
    edge[...] = keys_values[pl.ds(pl.multiple_of((1 - along) * rows, rows), rows), :]


def head_masks(shape):
    lane = lax.broadcasted_iota(jnp.int32, shape, 1)
    return lane < HEAD_DIM


def attend_kernel(place, queries, keys_values, edge, bias, tokens, gains, *refs):
    pieces, (attention, totals, hidden, xn2, weight, sems) = (refs[:PIECES], refs[PIECES:])
    width = tokens.shape[1]
    copies = fill(pieces, weight, sems, place[0], pl.ds(3 * width, width))
    pair = 2 * HEAD_DIM
    factor = 1.0 / math.sqrt(HEAD_DIM)
    rows = queries.shape[0]
    is_first = head_masks((rows, pair))
    lane = lax.broadcasted_iota(jnp.int32, totals.shape, 1)
    logs = jnp.zeros(totals.shape, F32)
    for start in range(0, width, pair):
        two = queries[:, start : start + pair]
        keys = jnp.concatenate([keys_values[:, start : start + pair], edge[:, start : start + pair]], axis=0)
        vals = jnp.concatenate(
            [keys_values[:, width + start : width + start + pair], edge[:, width + start : width + start + pair]],
            axis=0,
        )
        outs = []
        for which in range(2):
            mask = is_first if which == 0 else jnp.logical_not(is_first)
            one = jnp.where(mask, two, jnp.zeros_like(two))
            scores = dot_nt(one, keys) * factor + bias[...]
            peak = jnp.max(scores, axis=-1, keepdims=True)
            exponent = jnp.exp(scores - peak)
            total = jnp.sum(exponent, axis=-1, keepdims=True)
            soft = (exponent / total).astype(BF16)
            outs.append(dot_nn(soft, vals))
            logs = jnp.where(lane == 2 * (start // pair) + which, peak + jnp.log(total), logs)
        attention[:, start : start + pair] = jnp.where(is_first, outs[0], outs[1]).astype(BF16)
    totals[...] = logs
    wait_all(copies)
    result = tokens[...].astype(F32) + dot_nn(attention[...], weight[...])
    hidden[...] = result
    normed, _ = norm_parts(result)
    xn2[...] = (normed * gains[1:2, :]).astype(BF16)


def lift_kernel(place, xn2, grad_out, *refs):
    first, second, rest = (refs[:PIECES], refs[PIECES : 2 * PIECES], refs[2 * PIECES :])
    keep, send, slope_gate, active, gelu_weight, gate_weight, sems_one, sems_two = rest
    me = place[0]
    copies = fill(first, gelu_weight, sems_one, me)
    others = fill(second, gate_weight, sems_two, me)
    wait_all(copies)
    gelu_input = dot_nn(xn2[...], gelu_weight[...])
    wait_all(others)
    gate_part = dot_nn(xn2[...], gate_weight[...])
    cdf_part = 0.5 * (1.0 + lax.erf(gelu_input * (1.0 / math.sqrt(2.0))))
    density = jnp.exp(-0.5 * gelu_input * gelu_input) * (1.0 / math.sqrt(2.0 * math.pi))
    activated = gelu_input * cdf_part
    active[...] = activated
    slope_gate[...] = gate_part * (cdf_part + gelu_input * density)
    pack(keep, send, grad_out, (activated * gate_part).astype(BF16), X_BIT, Y_BIT, me)


def contract_kernel(place, gated_pack, grad_out, xn2, hidden, slope_gate, active, *refs):
    pieces, rest = (refs[:PIECES], refs[PIECES:])
    layer_out, keep_one, send_one, keep_two, send_two, weight, sems = rest
    me = place[0]
    wait_all(fill(pieces, weight, sems, me))
    d_gated = dot_nn(grad_out[...], weight[...])
    pack(keep_one, send_one, xn2, (d_gated * slope_gate[...]).astype(BF16), Y_BIT, X_BIT, me)
    pack(keep_two, send_two, xn2, (d_gated * active[...]).astype(BF16), X_BIT, Y_BIT, me)
    gated = gated_pack[:, xn2.shape[1] // 2 :]
    layer_out[...] = (hidden[...] + dot_nt(gated, weight[...])).astype(BF16)


def hidden_back_kernel(place, pack_one, pack_two, grad_out, hidden, gains, attention, *refs):
    first, second, third = (refs[:PIECES], refs[PIECES : 2 * PIECES], refs[2 * PIECES : 3 * PIECES])
    keep, send, d_hidden, d_attention, gain_grad = refs[3 * PIECES : 3 * PIECES + 5]
    gelu_weight, gate_weight, weight, sems_one, sems_two, sems_three = refs[3 * PIECES + 5 :]
    me = place[0]
    width = hidden.shape[1]
    copies = fill(first, gelu_weight, sems_one, me)
    others = fill(second, gate_weight, sems_two, me)
    lasts = fill(third, weight, sems_three, me, pl.ds(3 * width, width))
    normed, scaled = norm_parts(hidden[...])
    wait_all(copies)
    d_xn2 = dot_nt(pack_one[:, width // 2 :], gelu_weight[...])
    wait_all(others)
    d_xn2 = d_xn2 + dot_nt(pack_two[:, width // 2 :], gate_weight[...])
    d_norm, gain_term = norm_back(d_xn2, normed, scaled, gains[1:2, :])
    gain_grad[...] = gain_term
    total = grad_out[...].astype(F32) + d_norm
    d_hidden[...] = total
    rounded = total.astype(BF16)
    wait_all(lasts)
    d_attention[...] = dot_nt(rounded, weight[...]).astype(BF16)
    pack(keep, send, attention, rounded, Y_BIT, X_BIT, me)


def attend_back_kernel(
    place, queries, keys_values, edge, bias, totals, d_attention, cosine, sine, xn1, keep, send, d_keys_values, d_edge, d_turned
):
    width = queries.shape[1]
    pair = 2 * HEAD_DIM
    factor = 1.0 / math.sqrt(HEAD_DIM)
    rows = queries.shape[0]
    is_first = head_masks((rows, pair))
    is_first_key = head_masks((rows + edge.shape[0], pair))
    for start in range(0, width, pair):
        here = slice(start, start + pair)
        there = slice(width + start, width + start + pair)
        two = queries[:, here]
        d_two = d_attention[:, here]
        keys = jnp.concatenate([keys_values[:, here], edge[:, here]], axis=0)
        vals = jnp.concatenate([keys_values[:, there], edge[:, there]], axis=0)
        d_queries, d_keys, d_vals = ([], [], [])
        for which in range(2):
            mask = is_first if which == 0 else jnp.logical_not(is_first)
            one = jnp.where(mask, two, jnp.zeros_like(two))
            d_one = jnp.where(mask, d_two, jnp.zeros_like(d_two))
            head = 2 * (start // pair) + which
            scores = dot_nt(one, keys) * factor + bias[...]
            recomputed = jnp.exp(scores - totals[:, head : head + 1])
            d_soft = dot_nt(d_one, vals)
            center = jnp.sum(recomputed * d_soft, axis=-1, keepdims=True)
            d_scores = (recomputed * (d_soft - center) * factor).astype(BF16)
            d_queries.append(dot_nn(d_scores, keys))
            d_keys.append(dot_tt(d_scores, two))
            d_vals.append(dot_tt(recomputed.astype(BF16), d_two))
        d_query = jnp.where(is_first, d_queries[0], d_queries[1])
        d_turned[:, here] = turn(d_query, cosine[...], -sine[...]).astype(BF16)
        d_key = jnp.where(is_first_key, d_keys[0], d_keys[1])
        d_val = jnp.where(is_first_key, d_vals[0], d_vals[1])
        d_keys_values[:, here] = d_key[:rows]
        d_keys_values[:, there] = d_val[:rows]
        d_edge[:, here] = d_key[rows:].astype(BF16)
        d_edge[:, there] = d_val[rows:].astype(BF16)
    pack(keep, send, xn1, d_turned[...], X_BIT, Y_BIT, place[0])


def keys_back_kernel(
    place, d_keys_values, arrived, cosine, sine, xn1, keep_one, send_one, keep_two, send_two, summed, d_turned
):
    me, along = (place[0], place[1])
    width = xn1.shape[1]
    pair = 2 * HEAD_DIM
    rows = arrived.shape[0]
    summed[...] = d_keys_values[...]
    where = pl.ds(pl.multiple_of((1 - along) * rows, rows), rows)
    summed[where, :] = summed[where, :] + arrived[...].astype(F32)
    for start in range(0, width, pair):
        here = slice(start, start + pair)
        d_turned[:, here] = turn(summed[:, here], cosine[...], -sine[...]).astype(BF16)
    pack(keep_one, send_one, xn1, d_turned[...], Y_BIT, X_BIT, me)
    pack(keep_two, send_two, xn1, summed[:, width:].astype(BF16), X_BIT, Y_BIT, me)


def tokens_back_kernel(place, pack_q, pack_k, pack_v, tokens, d_hidden, gains, *refs):
    pieces, (input_grad, gain_grad, weight, sems) = (refs[:PIECES], refs[PIECES:])
    width = tokens.shape[1]
    copies = fill(pieces, weight, sems, place[0], pl.ds(0, 3 * width))
    normed, scaled = norm_parts(tokens[...].astype(F32))
    wait_all(copies)
    d_xn1 = dot_nt(pack_q[:, width // 2 :], weight[:, :width])
    d_xn1 = d_xn1 + dot_nt(pack_k[:, width // 2 :], weight[:, width : 2 * width])
    d_xn1 = d_xn1 + dot_nt(pack_v[:, width // 2 :], weight[:, 2 * width :])
    d_norm, gain_term = norm_back(d_xn1, normed, scaled, gains[0:1, :])
    gain_grad[...] = gain_term
    input_grad[...] = (d_hidden[...] + d_norm).astype(BF16)


def product_kernel(width, mine, over_link, core_mine, core_link, own, sent, joined, sems):
    rows = mine.shape[0]
    copies = []
    for index, part in enumerate((mine, over_link, core_mine, core_link)):
        copies.append(pltpu.make_async_copy(part, joined.at[pl.ds(index * rows, rows)], sems.at[index]))
    for copy in copies:
        copy.start()
    wait_all(copies)
    block = lambda top, k: joined[2 * rows * top : 2 * rows * (top + 1), k * width : (k + 1) * width]
    right = joined[:, 4 * width :]
    left = jnp.concatenate([block(0, 2), block(1, 3)], axis=0)
    sent[...] = dot_tt(left, right).astype(BF16)
    left = jnp.concatenate([block(0, 0), block(1, 1)], axis=0)
    own[...] = dot_tt(left, right)


def call(kernel, outs, operands, scratch=(), smem=1, anywhere=(), flops=0, size=0):
    specs = []
    for index in range(len(operands)):
        if index < smem:
            specs.append(pl.BlockSpec(memory_space=pltpu.SMEM))
        elif index in anywhere:
            specs.append(pl.BlockSpec(memory_space=pl.ANY))
        else:
            specs.append(pl.BlockSpec(memory_space=pltpu.VMEM))
    return pl.pallas_call(
        kernel,
        out_shape=[jax.ShapeDtypeStruct(shape, kind) for shape, kind in outs],
        in_specs=specs,
        out_specs=[pl.BlockSpec(memory_space=pltpu.VMEM)] * len(outs),
        scratch_shapes=list(scratch),
        cost_estimate=pl.CostEstimate(flops=flops, bytes_accessed=size, transcendentals=0),
        compiler_params=pltpu.CompilerParams(vmem_limit_bytes=VMEM_BYTES),
    )(*operands)


def grad_rows(keep, send, gather_bit, sum_bit, width):
    rows, cols = (keep.shape[0], keep.shape[1] - 4 * width)
    over_link = swap(send, gather_bit)
    core_mine = swap(keep, CORE_BIT)
    core_link = swap(over_link, CORE_BIT)
    own, sent = call(
        lambda *refs: product_kernel(width, *refs),
        [((width, cols), F32), ((width, cols), BF16)],
        [keep, over_link, core_mine, core_link],
        [pltpu.VMEM((4 * rows, 4 * width + cols), BF16), pltpu.SemaphoreType.DMA((4,))],
        smem=0,
        anywhere=(0, 1, 2, 3),
        flops=16 * rows * width * cols,
        size=4 * rows * (4 * width + cols) * 2 + 6 * width * cols,
    )
    return own + swap(sent, sum_bit).astype(F32)


def line_sum(part):
    first = lax.ppermute(part.astype(BF16), "replica", [(0, 1), (3, 2)])
    pair = (part + first.astype(F32)).astype(BF16)
    other = lax.ppermute(pair, "replica", [(1, 2), (2, 1)])
    total = (pair.astype(F32) + other.astype(F32)).astype(BF16)
    back = lax.ppermute(total, "replica", [(1, 0), (2, 3)])
    place = lax.axis_index("replica")
    middle = (place == 1) | (place == 2)
    return jnp.where(middle, total, back).astype(F32)


def sum_everywhere(values):
    for bit in (CORE_BIT, X_BIT, Y_BIT):
        values = values + swap(values, bit)
    for bit in (1, 2):
        values = values + lax.ppermute(values, "replica", [(i, i ^ bit) for i in range(4)])
    return values


def body_plane(
    tokens,
    input_gain,
    qkv_weight,
    output_weight,
    mlp_gain,
    expand_weight,
    contract_weight,
    positions,
    mask_bias,
    cotangent,
):
    me = lax.axis_index(PLANE)
    along = lax.axis_index("ctx")
    place = jnp.stack([me, along]).astype(jnp.int32)
    shard = qkv_weight.shape[0]
    ff_width = expand_weight.shape[1] // 2
    source, grad_out = (tokens[0], cotangent[0])
    rows, width = source.shape
    gains = jnp.stack([input_gain, mlp_gain], axis=1)
    gains = jnp.pad(gains, ((0, 0), (0, 126)))
    front = jnp.concatenate([qkv_weight, output_weight, gains], axis=1)
    packed, arrived = gather_pieces(front)
    gelu_pieces, arrived = gather_pieces(expand_weight[:, :ff_width], arrived)
    gate_pieces, arrived = gather_pieces(expand_weight[:, ff_width:], arrived)
    contract_pieces, arrived = gather_pieces(contract_weight, arrived)
    cosine, sine = rope_tables(positions[0], HEAD_DIM)
    cosine = jnp.concatenate([cosine[:, 0]] * 4, axis=1)
    sine = jnp.concatenate([-sine[:, 0], sine[:, 0]] * 2, axis=1)
    bias = mask_bias[0]
    bias = jnp.concatenate(
        [bias[:, HALF : HALF + rows], jnp.where(along == 0, bias[:, HALF + rows :], bias[:, :HALF])], axis=1
    )
    sems = pltpu.SemaphoreType.DMA((PIECES,))
    front_cols = front.shape[1]
    queries, keys_values, edge, xn1, full_gains = call(
        front_kernel,
        [((rows, width), BF16), ((rows, 2 * width), BF16), ((HALF, 2 * width), BF16), ((rows, width), BF16), ((8, width), F32)],
        [place, source, cosine, sine] + packed,
        [pltpu.VMEM((width, front_cols), BF16), sems],
        anywhere=range(4, 4 + PIECES),
        flops=6 * rows * width * width,
        size=2 * width * front_cols,
    )
    edge = swap(edge, X_BIT)
    attention, totals, hidden, xn2 = call(
        attend_kernel,
        [((rows, width), BF16), ((rows, 128), F32), ((rows, width), F32), ((rows, width), BF16)],
        [place, queries, keys_values, edge, bias, source, full_gains] + packed,
        [pltpu.VMEM((width, width), BF16), sems],
        anywhere=range(7, 7 + PIECES),
        flops=12 * rows * width * width,
        size=4 * width * width,
    )
    half = 4 * shard
    keep_c, send_c, slope_gate, active = call(
        lift_kernel,
        [((rows, half + ff_width), BF16)] * 2 + [((rows, ff_width), F32)] * 2,
        [place, xn2, grad_out] + gelu_pieces + gate_pieces,
        [pltpu.VMEM((width, ff_width), BF16)] * 2 + [sems] * 2,
        anywhere=range(3, 3 + 2 * PIECES),
        flops=4 * rows * width * ff_width,
        size=4 * width * ff_width,
    )
    contract_part = grad_rows(keep_c, send_c, X_BIT, Y_BIT, shard)
    layer_out, keep_g, send_g, keep_u, send_u = call(
        contract_kernel,
        [((rows, width), BF16)] + [((rows, half + ff_width), BF16)] * 4,
        [place, keep_c, grad_out, xn2, hidden, slope_gate, active] + contract_pieces,
        [pltpu.VMEM((width, ff_width), BF16), sems],
        anywhere=range(7, 7 + PIECES),
        flops=4 * rows * width * ff_width,
        size=2 * width * ff_width,
    )
    gelu_part = grad_rows(keep_g, send_g, Y_BIT, X_BIT, shard)
    gate_part = grad_rows(keep_u, send_u, X_BIT, Y_BIT, shard)
    keep_o, send_o, d_hidden, d_attention, mlp_term = call(
        hidden_back_kernel,
        [((rows, half + width), BF16)] * 2 + [((rows, width), F32), ((rows, width), BF16), ((1, width), F32)],
        [place, keep_g, keep_u, grad_out, hidden, full_gains, attention] + gelu_pieces + gate_pieces + packed,
        [pltpu.VMEM((width, ff_width), BF16)] * 2 + [pltpu.VMEM((width, width), BF16)] + [sems] * 3,
        anywhere=range(7, 7 + 3 * PIECES),
        flops=6 * rows * width * ff_width,
        size=6 * width * ff_width,
    )
    output_part = grad_rows(keep_o, send_o, Y_BIT, X_BIT, shard)
    keep_q, send_q, d_keys_values, d_edge = call(
        attend_back_kernel,
        [((rows, half + width), BF16)] * 2 + [((rows, 2 * width), F32), ((HALF, 2 * width), BF16)],
        [place, queries, keys_values, edge, bias, totals, d_attention, cosine, sine, xn1],
        [pltpu.VMEM((rows, width), BF16)],
        flops=20 * rows * width * width,
        size=4 * width * width,
    )
    query_part = grad_rows(keep_q, send_q, X_BIT, Y_BIT, shard)
    keep_k, send_k, keep_v, send_v = call(
        keys_back_kernel,
        [((rows, half + width), BF16)] * 4,
        [place, d_keys_values, swap(d_edge, X_BIT), cosine, sine, xn1],
        [pltpu.VMEM((rows, 2 * width), F32), pltpu.VMEM((rows, width), BF16)],
        flops=rows * width,
        size=8 * rows * width,
    )
    key_part = grad_rows(keep_k, send_k, Y_BIT, X_BIT, shard)
    value_part = grad_rows(keep_v, send_v, X_BIT, Y_BIT, shard)
    input_grad, input_term = call(
        tokens_back_kernel,
        [((rows, width), BF16), ((1, width), F32)],
        [place, keep_q, keep_k, keep_v, source, d_hidden, full_gains] + packed,
        [pltpu.VMEM((width, 3 * width), BF16), sems],
        anywhere=range(7, 7 + PIECES),
        flops=6 * rows * width * width,
        size=6 * width * width,
    )
    gain_sums = sum_everywhere(jnp.concatenate([input_term, mlp_term], axis=0))
    gain_rows = lax.dynamic_slice_in_dim(gain_sums, me * shard, shard, axis=1)
    contract_grad = line_sum(contract_part)
    gelu_grad = line_sum(gelu_part)
    gate_grad = line_sum(gate_part)
    early_grad = line_sum(jnp.concatenate([output_part, query_part], axis=1))
    late_grad = line_sum(jnp.concatenate([key_part, value_part], axis=1))
    return (
        layer_out[None],
        input_grad[None],
        gain_rows[0],
        jnp.concatenate([early_grad[:, width:], late_grad], axis=1),
        early_grad[:, :width],
        gain_rows[1],
        jnp.concatenate([gelu_grad, gate_grad], axis=1),
        contract_grad,
    )


def solution(mesh):
    in_specs = (
        P(("replica", "fsdp"), "ctx", None),
        P(("fsdp", "ctx")),
        P(("fsdp", "ctx"), None),
        P(("fsdp", "ctx"), None),
        P(("fsdp", "ctx")),
        P(("fsdp", "ctx"), None),
        P(("fsdp", "ctx"), None),
        P(("replica", "fsdp"), "ctx"),
        P(("replica", "fsdp"), "ctx", None),
        P(("replica", "fsdp"), "ctx", None),
    )
    out_specs = (
        P(("replica", "fsdp"), "ctx", None),
        P(("replica", "fsdp"), "ctx", None),
        P(("fsdp", "ctx")),
        P(("fsdp", "ctx"), None),
        P(("fsdp", "ctx"), None),
        P(("fsdp", "ctx")),
        P(("fsdp", "ctx"), None),
        P(("fsdp", "ctx"), None),
    )
    sizes = (mesh.shape["replica"], mesh.shape["fsdp"], mesh.shape["ctx"])
    body = body_plane if sizes == (4, 4, 2) else body_generic
    return jax.shard_map(body, mesh=mesh, in_specs=in_specs, out_specs=out_specs, check_vma=False)
```

```python
import math

import jax
import jax.numpy as jnp
from jax import lax
from jax.experimental import pallas as pl
from jax.experimental.pallas import tpu as pltpu
from jax.sharding import PartitionSpec as P

HEAD_DIM = 64
HALF = 64


EPS = 1e-05
THETA = 10000.0


def extended_2(cells, sides, width):
    for axis, dim in sides:
        count = lax.axis_size(axis)
        ends = count - 1
        head = lax.slice_in_dim(cells, 0, width, axis=dim)
        tail = lax.slice_in_dim(cells, cells.shape[dim] - width, cells.shape[dim], axis=dim)
        cells = jnp.concatenate(
            [
                lax.ppermute(tail, axis, [(i, (i + 1) % count) for i in range(ends)]),
                cells,
                lax.ppermute(head, axis, [((i + 1) % count, i) for i in range(ends)]),
            ],
            axis=dim,
        )
    return cells


def from_behind(value, axis, steps):
    count = lax.axis_size(axis)
    first, last = (max(0, -steps), min(count, count - steps))
    return lax.ppermute(value, axis, [(source, source + steps) for source in range(first, last)])


def layer_norm(values, gain):
    center = values - jnp.mean(values, axis=-1, keepdims=True)
    variance = jnp.mean(center * center, axis=-1, keepdims=True)
    scaled = lax.rsqrt(variance + EPS)
    normed = center * scaled
    return (normed, scaled, (normed * gain.astype(jnp.float32)).astype(jnp.bfloat16))


def layer_norm_back(incoming, normed, scaled, gain):
    weighted = incoming * gain.astype(jnp.float32)
    gain_grad = jnp.sum(incoming * normed, axis=0)
    mean_one = jnp.mean(weighted, axis=-1, keepdims=True)
    mean_two = jnp.mean(weighted * normed, axis=-1, keepdims=True)
    return (scaled * (weighted - mean_one - normed * mean_two), gain_grad)


def rope_tables(positions, head_size):
    half_dim = head_size // 2
    exponent = jnp.arange(half_dim, dtype=jnp.float32) * (2.0 / head_size)
    frequency = jnp.exp(-math.log(THETA) * exponent)
    angles = positions.astype(jnp.float32)[:, None] * frequency[None, :]
    return (jnp.cos(angles)[:, None, :], jnp.sin(angles)[:, None, :])


def rotate(values, cosine, sine):
    half_dim = values.shape[-1] // 2
    lower_half, upper_half = (values[..., :half_dim], values[..., half_dim:])
    return jnp.concatenate(
        [lower_half * cosine - upper_half * sine, upper_half * cosine + lower_half * sine], axis=-1
    )


def rotate_back(values, cosine, sine):
    half_dim = values.shape[-1] // 2
    lower_half, upper_half = (values[..., :half_dim], values[..., half_dim:])
    return jnp.concatenate(
        [lower_half * cosine + upper_half * sine, upper_half * cosine - lower_half * sine], axis=-1
    )


def gelu_slope(values):
    cdf_part = 0.5 * (1.0 + jax.scipy.special.erf(values * (1.0 / math.sqrt(2.0))))
    density = jnp.exp(-0.5 * values * values) * (1.0 / math.sqrt(2.0 * math.pi))
    return cdf_part + values * density


def block_scores(queries, key_rows, additive):
    factor = 1.0 / math.sqrt(queries.shape[-1])
    scores = jnp.einsum("qhd,khd->hqk", queries, key_rows, preferred_element_type=jnp.float32)
    return scores * factor + additive[None]


def attend(queries, key_rows, value_rows, additive):
    scores = block_scores(queries, key_rows, additive)
    row_peak = jnp.max(scores, axis=-1, keepdims=True)
    exponent = jnp.exp(scores - row_peak)
    row_total = jnp.sum(exponent, axis=-1, keepdims=True)
    soft_weights = (exponent / row_total).astype(jnp.bfloat16)
    mixed = jnp.einsum("hqk,khd->qhd", soft_weights, value_rows, preferred_element_type=jnp.float32)
    return (mixed.astype(jnp.bfloat16), row_peak[..., 0] + jnp.log(row_total[..., 0]))


def attend_back(queries, key_rows, value_rows, additive, log_total, d_mixed):
    factor = 1.0 / math.sqrt(queries.shape[-1])
    scores = block_scores(queries, key_rows, additive)
    recomputed = jnp.exp(scores - log_total[..., None])
    d_soft = jnp.einsum("qhd,khd->hqk", d_mixed, value_rows, preferred_element_type=jnp.float32)
    center = jnp.sum(recomputed * d_soft, axis=-1, keepdims=True)
    d_scores = (recomputed * (d_soft - center) * factor).astype(jnp.bfloat16)
    d_queries = jnp.einsum("hqk,khd->qhd", d_scores, key_rows, preferred_element_type=jnp.float32)
    d_keys = jnp.einsum("hqk,qhd->khd", d_scores, queries, preferred_element_type=jnp.float32)
    d_values = jnp.einsum(
        "hqk,qhd->khd", recomputed.astype(jnp.bfloat16), d_mixed, preferred_element_type=jnp.float32
    )
    return (d_queries, d_keys, d_values)


def body_generic(
    tokens,
    input_gain,
    qkv_weight,
    output_weight,
    mlp_gain,
    expand_weight,
    contract_weight,
    positions,
    mask_bias,
    cotangent,
):
    gathered = (
        lax.all_gather(input_gain, ("fsdp", "ctx"), axis=0, tiled=True),
        lax.all_gather(qkv_weight, ("fsdp", "ctx"), axis=0, tiled=True),
        lax.all_gather(output_weight, ("fsdp", "ctx"), axis=0, tiled=True),
        lax.all_gather(mlp_gain, ("fsdp", "ctx"), axis=0, tiled=True),
        lax.all_gather(expand_weight, ("fsdp", "ctx"), axis=0, tiled=True),
        lax.all_gather(contract_weight, ("fsdp", "ctx"), axis=0, tiled=True),
    )
    full_input_gain, full_qkv, full_output, full_mlp_gain, full_expand, full_contract = gathered
    residual = tokens[0].astype(jnp.float32)
    row_count, model_width = residual.shape
    head_count = model_width // HEAD_DIM
    cosine, sine = rope_tables(positions[0], HEAD_DIM)
    normed1, scaled1, xn1 = layer_norm(residual, full_input_gain)
    projected = jnp.dot(xn1, full_qkv, preferred_element_type=jnp.float32).reshape(
        row_count, 3, head_count, HEAD_DIM
    )
    queries = rotate(projected[:, 0], cosine, sine).astype(jnp.bfloat16)
    key_rows = rotate(projected[:, 1], cosine, sine).astype(jnp.bfloat16)
    value_rows = projected[:, 2].astype(jnp.bfloat16)
    packed = jnp.concatenate(
        [key_rows.reshape(row_count, model_width), value_rows.reshape(row_count, model_width)],
        axis=1,
    )
    extended = extended_2(packed, (("ctx", 0),), HALF)
    extent = extended.shape[0]
    key_ext = extended[:, :model_width].reshape(extent, head_count, HEAD_DIM)
    value_ext = extended[:, model_width:].reshape(extent, head_count, HEAD_DIM)
    additive = mask_bias[0]
    mixed, log_total = attend(queries, key_ext, value_ext, additive)
    attention = mixed.reshape(row_count, model_width)
    hidden = residual + jnp.dot(attention, full_output, preferred_element_type=jnp.float32)
    normed2, scaled2, xn2 = layer_norm(hidden, full_mlp_gain)
    lifted = jnp.dot(xn2, full_expand, preferred_element_type=jnp.float32)
    ff_width = lifted.shape[1] // 2
    gelu_input = lifted[:, :ff_width]
    gate_part = lifted[:, ff_width:]
    activated = jax.nn.gelu(gelu_input, approximate=False)
    gated = (activated * gate_part).astype(jnp.bfloat16)
    down_out = jnp.einsum("tf,jf->tj", gated, full_contract, preferred_element_type=jnp.float32)
    layer_out = (hidden + down_out).astype(jnp.bfloat16)
    back_input_gain, back_qkv, back_output, back_mlp_gain, back_expand, back_contract = gathered
    grad_out = cotangent[0]
    d_gated = jnp.dot(grad_out, back_contract, preferred_element_type=jnp.float32)
    d_lifted = jnp.concatenate(
        [d_gated * gate_part * gelu_slope(gelu_input), d_gated * activated], axis=1
    ).astype(jnp.bfloat16)
    d_xn2 = jnp.einsum("tc,dc->td", d_lifted, back_expand, preferred_element_type=jnp.float32)
    d_norm2, mlp_gain_term = layer_norm_back(d_xn2, normed2, scaled2, back_mlp_gain)
    d_hidden = grad_out.astype(jnp.float32) + d_norm2
    d_proj = d_hidden.astype(jnp.bfloat16)
    d_attention = jnp.einsum(
        "tj,ij->ti", d_proj, back_output, preferred_element_type=jnp.float32
    ).astype(jnp.bfloat16)
    d_queries, d_key_ext, d_value_ext = attend_back(
        queries,
        key_ext,
        value_ext,
        additive,
        log_total,
        d_attention.reshape(row_count, head_count, HEAD_DIM),
    )
    grad_ext = jnp.concatenate(
        [d_key_ext.reshape(extent, model_width), d_value_ext.reshape(extent, model_width)], axis=1
    )
    from_next = from_behind(grad_ext[:HALF], "ctx", -1)
    from_prev = from_behind(grad_ext[row_count + HALF :], "ctx", 1)
    grad_kv = grad_ext[HALF : HALF + row_count]
    grad_kv = grad_kv + jnp.pad(from_prev, ((0, row_count - HALF), (0, 0)))
    grad_kv = grad_kv + jnp.pad(from_next, ((row_count - HALF, 0), (0, 0)))
    d_keys = rotate_back(
        grad_kv[:, :model_width].reshape(row_count, head_count, HEAD_DIM), cosine, sine
    )
    d_values = grad_kv[:, model_width:]
    d_queries = rotate_back(d_queries, cosine, sine)
    d_projected = jnp.concatenate(
        [
            d_queries.reshape(row_count, model_width),
            d_keys.reshape(row_count, model_width),
            d_values,
        ],
        axis=1,
    ).astype(jnp.bfloat16)
    d_xn1 = jnp.einsum("tc,dc->td", d_projected, back_qkv, preferred_element_type=jnp.float32)
    d_norm1, input_gain_term = layer_norm_back(d_xn1, normed1, scaled1, back_input_gain)
    input_grad = (d_hidden + d_norm1).astype(jnp.bfloat16)
    left_one, left_two, left_three, left_four = (xn1, attention, xn2, grad_out)
    gain_one, gain_two = (input_gain_term, mlp_gain_term)
    qkv_term = jnp.einsum("ti,tj->ij", left_one, d_projected, preferred_element_type=jnp.float32)
    output_term = jnp.einsum("ti,tj->ij", left_two, d_proj, preferred_element_type=jnp.float32)
    expand_term = jnp.einsum("ti,tj->ij", left_three, d_lifted, preferred_element_type=jnp.float32)
    contract_term = jnp.einsum("ti,tj->ij", left_four, gated, preferred_element_type=jnp.float32)
    first_gain = gain_one[:, None]
    second_gain = gain_two[:, None]
    shares = lax.psum_scatter(
        jnp.concatenate(
            [qkv_term, output_term, expand_term, contract_term, first_gain, second_gain], axis=1
        ),
        ("fsdp", "ctx"),
        scatter_dimension=0,
        tiled=True,
    )
    result = lax.psum(shares, "replica")
    qkv_cols = 3 * model_width
    expand_cols = 2 * ff_width
    qkv_grad = result[:, :qkv_cols]
    output_grad = result[:, qkv_cols : qkv_cols + model_width]
    offset = qkv_cols + model_width
    expand_grad = result[:, offset : offset + expand_cols]
    offset = offset + expand_cols
    contract_grad = result[:, offset : offset + ff_width]
    offset = offset + ff_width
    input_gain_grad = result[:, offset]
    mlp_gain_grad = result[:, offset + 1]
    return (
        layer_out[None],
        input_grad[None],
        input_gain_grad,
        qkv_grad,
        output_grad,
        mlp_gain_grad,
        expand_grad,
        contract_grad,
    )


X_BIT, CORE_BIT, Y_BIT = (1, 2, 4)
PLANE = ("fsdp", "ctx")
PLANE_SIZE = 8
PIECES = 10
VMEM_BYTES = 50 * 1024 * 1024
F32, BF16 = (jnp.float32, jnp.bfloat16)


def swap(value, bit):
    return lax.ppermute(value, PLANE, [(i, i ^ bit) for i in range(PLANE_SIZE)])


def gather_pieces(own, after=None):
    if after is not None:
        own, _ = lax.optimization_barrier((own, after))
    half = own.shape[0] // 2
    over_x = swap(own, X_BIT)
    over_y = swap(own, Y_BIT)
    first = [own, over_x, over_y, swap(over_x[:half], Y_BIT), swap(over_y[half:], X_BIT)]
    second = [swap(part, CORE_BIT) for part in first]
    return (first + second, (over_x, over_y))


def fill(pieces, target, sems, me, columns=None):
    shard = target.shape[0] // PLANE_SIZE
    half = shard // 2
    corner = X_BIT | Y_BIT
    places = [(0, 0, shard), (X_BIT, 0, shard), (Y_BIT, 0, shard), (corner, 0, half), (corner, half, half)]
    places = places + [(offset | CORE_BIT, start, rows) for offset, start, rows in places]
    copies = []
    for index, (piece, (offset, start, rows)) in enumerate(zip(pieces, places)):
        row = pl.multiple_of((me ^ offset) * shard + start, half)
        source = piece if columns is None else piece.at[:, columns]
        copies.append(pltpu.make_async_copy(source, target.at[pl.ds(row, rows)], sems.at[index]))
    for copy in copies:
        copy.start()
    return copies


def wait_all(copies):
    for copy in copies:
        copy.wait()


def pack(keep, send, left, right, gather_bit, sum_bit, me):
    width = left.shape[1] // PLANE_SIZE
    for slot, offset in enumerate([0, CORE_BIT, sum_bit, CORE_BIT | sum_bit]):
        for target, flip in ((keep, 0), (send, gather_bit)):
            source = pl.multiple_of((me ^ (offset | flip)) * width, width)
            target[:, slot * width : (slot + 1) * width] = left[:, pl.ds(source, width)]
    keep[:, 4 * width :] = right
    send[:, 4 * width :] = right


def turn(values, cosine, sine):
    lane = lax.broadcasted_iota(jnp.int32, values.shape, 1)
    low = lane % HEAD_DIM < HEAD_DIM // 2
    other = jnp.where(
        low,
        pltpu.roll(values, values.shape[1] - HEAD_DIM // 2, 1),
        pltpu.roll(values, HEAD_DIM // 2, 1),
    )
    return values * cosine + other * sine


def dot_tt(one, two):
    return lax.dot_general(one, two, (((0,), (0,)), ((), ())), preferred_element_type=F32)


def dot_nt(one, two):
    return lax.dot_general(one, two, (((1,), (1,)), ((), ())), preferred_element_type=F32)


def dot_nn(one, two):
    return jnp.dot(one, two, preferred_element_type=F32)


def norm_parts(values):
    center = values - jnp.mean(values, axis=-1, keepdims=True)
    variance = jnp.mean(center * center, axis=-1, keepdims=True)
    scaled = lax.rsqrt(variance + EPS)
    return (center * scaled, scaled)


def norm_back(incoming, normed, scaled, gain):
    weighted = incoming * gain
    gain_grad = jnp.sum(incoming * normed, axis=0, keepdims=True)
    mean_one = jnp.mean(weighted, axis=-1, keepdims=True)
    mean_two = jnp.mean(weighted * normed, axis=-1, keepdims=True)
    return (scaled * (weighted - mean_one - normed * mean_two), gain_grad)


def front_kernel(place, tokens, cosine, sine, *refs):
    pieces, (queries, keys_values, edge, xn1, gains, weight, sems) = (refs[:PIECES], refs[PIECES:])
    me, along = (place[0], place[1])
    copies = fill(pieces, weight, sems, me)
    normed, _ = norm_parts(tokens[...].astype(F32))
    width = tokens.shape[1]
    wait_all(copies)
    turned = weight[:, 4 * width :].astype(F32).T
    gains[...] = turned[: gains.shape[0]]
    rounded = (normed * gains[0:1, :]).astype(BF16)
    xn1[...] = rounded
    pair = cosine.shape[1]
    projected = dot_nn(rounded, weight[:, : 3 * width])
    for start in range(0, width, pair):
        part = projected[:, start : start + pair]
        queries[:, start : start + pair] = turn(part, cosine[...], sine[...]).astype(BF16)
        part = projected[:, width + start : width + start + pair]
        keys_values[:, start : start + pair] = turn(part, cosine[...], sine[...]).astype(BF16)
    keys_values[:, width:] = projected[:, 2 * width :].astype(BF16)
    rows = edge.shape[0]
    edge[...] = keys_values[pl.ds(pl.multiple_of((1 - along) * rows, rows), rows), :]


def head_masks(shape):
    lane = lax.broadcasted_iota(jnp.int32, shape, 1)
    return lane < HEAD_DIM


def attend_kernel(place, queries, keys_values, edge, bias, tokens, gains, *refs):
    pieces, (attention, totals, hidden, xn2, weight, sems) = (refs[:PIECES], refs[PIECES:])
    width = tokens.shape[1]
    copies = fill(pieces, weight, sems, place[0], pl.ds(3 * width, width))
    pair = 2 * HEAD_DIM
    factor = 1.0 / math.sqrt(HEAD_DIM)
    rows = queries.shape[0]
    is_first = head_masks((rows, pair))
    lane = lax.broadcasted_iota(jnp.int32, totals.shape, 1)
    logs = jnp.zeros(totals.shape, F32)
    for start in range(0, width, pair):
        two = queries[:, start : start + pair]
        keys = jnp.concatenate([keys_values[:, start : start + pair], edge[:, start : start + pair]], axis=0)
        vals = jnp.concatenate(
            [keys_values[:, width + start : width + start + pair], edge[:, width + start : width + start + pair]],
            axis=0,
        )
        outs = []
        for which in range(2):
            mask = is_first if which == 0 else jnp.logical_not(is_first)
            one = jnp.where(mask, two, jnp.zeros_like(two))
            scores = dot_nt(one, keys) * factor + bias[...]
            peak = jnp.max(scores, axis=-1, keepdims=True)
            exponent = jnp.exp(scores - peak)
            total = jnp.sum(exponent, axis=-1, keepdims=True)
            soft = (exponent / total).astype(BF16)
            outs.append(dot_nn(soft, vals))
            logs = jnp.where(lane == 2 * (start // pair) + which, peak + jnp.log(total), logs)
        attention[:, start : start + pair] = jnp.where(is_first, outs[0], outs[1]).astype(BF16)
    totals[...] = logs
    wait_all(copies)
    result = tokens[...].astype(F32) + dot_nn(attention[...], weight[...])
    hidden[...] = result
    normed, _ = norm_parts(result)
    xn2[...] = (normed * gains[1:2, :]).astype(BF16)


def lift_kernel(place, xn2, grad_out, *refs):
    pieces, (keep, send, slope_gate, active, weight, sems) = (refs[:PIECES], refs[PIECES:])
    me = place[0]
    cols = active.shape[1]
    wait_all(fill(pieces, weight, sems, me))
    gelu_input = dot_nn(xn2[...], weight[:, :cols])
    gate_part = dot_nn(xn2[...], weight[:, cols:])
    cdf_part = 0.5 * (1.0 + lax.erf(gelu_input * (1.0 / math.sqrt(2.0))))
    density = jnp.exp(-0.5 * gelu_input * gelu_input) * (1.0 / math.sqrt(2.0 * math.pi))
    activated = gelu_input * cdf_part
    active[...] = activated
    slope_gate[...] = gate_part * (cdf_part + gelu_input * density)
    pack(keep, send, grad_out, (activated * gate_part).astype(BF16), X_BIT, Y_BIT, me)


def contract_kernel(place, gated_pack, grad_out, xn2, hidden, slope_gate, active, *refs):
    pieces, rest = (refs[:PIECES], refs[PIECES:])
    layer_out, keep_one, send_one, keep_two, send_two, weight, sems = rest
    me = place[0]
    wait_all(fill(pieces, weight, sems, me))
    d_gated = dot_nn(grad_out[...], weight[...])
    pack(keep_one, send_one, xn2, (d_gated * slope_gate[...]).astype(BF16), Y_BIT, X_BIT, me)
    pack(keep_two, send_two, xn2, (d_gated * active[...]).astype(BF16), X_BIT, Y_BIT, me)
    gated = gated_pack[:, xn2.shape[1] // 2 :]
    layer_out[...] = (hidden[...] + dot_nt(gated, weight[...])).astype(BF16)


def hidden_back_kernel(place, pack_one, pack_two, grad_out, hidden, gains, attention, *refs):
    first, third = (refs[:PIECES], refs[PIECES : 2 * PIECES])
    keep, send, d_hidden, d_attention, gain_grad, lift_weight, weight, sems, sems_three = refs[2 * PIECES :]
    me = place[0]
    width = hidden.shape[1]
    copies = fill(first, lift_weight, sems, me)
    lasts = fill(third, weight, sems_three, me, pl.ds(3 * width, width))
    normed, scaled = norm_parts(hidden[...])
    wait_all(copies)
    cols = lift_weight.shape[1] // 2
    d_xn2 = dot_nt(pack_one[:, width // 2 :], lift_weight[:, :cols])
    d_xn2 = d_xn2 + dot_nt(pack_two[:, width // 2 :], lift_weight[:, cols:])
    d_norm, gain_term = norm_back(d_xn2, normed, scaled, gains[1:2, :])
    gain_grad[...] = gain_term
    total = grad_out[...].astype(F32) + d_norm
    d_hidden[...] = total
    rounded = total.astype(BF16)
    wait_all(lasts)
    d_attention[...] = dot_nt(rounded, weight[...]).astype(BF16)
    pack(keep, send, attention, rounded, Y_BIT, X_BIT, me)


def attend_back_kernel(
    place, queries, keys_values, edge, bias, totals, d_attention, cosine, sine, xn1, keep, send, d_keys_values, d_edge, d_turned
):
    width = queries.shape[1]
    pair = 2 * HEAD_DIM
    factor = 1.0 / math.sqrt(HEAD_DIM)
    rows = queries.shape[0]
    is_first = head_masks((rows, pair))
    is_first_key = head_masks((rows + edge.shape[0], pair))
    for start in range(0, width, pair):
        here = slice(start, start + pair)
        there = slice(width + start, width + start + pair)
        two = queries[:, here]
        d_two = d_attention[:, here]
        keys = jnp.concatenate([keys_values[:, here], edge[:, here]], axis=0)
        vals = jnp.concatenate([keys_values[:, there], edge[:, there]], axis=0)
        d_queries, d_keys, d_vals = ([], [], [])
        for which in range(2):
            mask = is_first if which == 0 else jnp.logical_not(is_first)
            one = jnp.where(mask, two, jnp.zeros_like(two))
            d_one = jnp.where(mask, d_two, jnp.zeros_like(d_two))
            head = 2 * (start // pair) + which
            scores = dot_nt(one, keys) * factor + bias[...]
            recomputed = jnp.exp(scores - totals[:, head : head + 1])
            d_soft = dot_nt(d_one, vals)
            center = jnp.sum(recomputed * d_soft, axis=-1, keepdims=True)
            d_scores = (recomputed * (d_soft - center) * factor).astype(BF16)
            d_queries.append(dot_nn(d_scores, keys))
            d_keys.append(dot_tt(d_scores, two))
            d_vals.append(dot_tt(recomputed.astype(BF16), d_two))
        d_query = jnp.where(is_first, d_queries[0], d_queries[1])
        d_turned[:, here] = turn(d_query, cosine[...], -sine[...]).astype(BF16)
        d_key = jnp.where(is_first_key, d_keys[0], d_keys[1])
        d_val = jnp.where(is_first_key, d_vals[0], d_vals[1])
        d_keys_values[:, here] = d_key[:rows]
        d_keys_values[:, there] = d_val[:rows]
        d_edge[:, here] = d_key[rows:].astype(BF16)
        d_edge[:, there] = d_val[rows:].astype(BF16)
    pack(keep, send, xn1, d_turned[...], X_BIT, Y_BIT, place[0])


def keys_back_kernel(
    place, d_keys_values, arrived, cosine, sine, xn1, keep_one, send_one, keep_two, send_two, summed, d_turned
):
    me, along = (place[0], place[1])
    width = xn1.shape[1]
    pair = 2 * HEAD_DIM
    rows = arrived.shape[0]
    summed[...] = d_keys_values[...]
    where = pl.ds(pl.multiple_of((1 - along) * rows, rows), rows)
    summed[where, :] = summed[where, :] + arrived[...].astype(F32)
    for start in range(0, width, pair):
        here = slice(start, start + pair)
        d_turned[:, here] = turn(summed[:, here], cosine[...], -sine[...]).astype(BF16)
    pack(keep_one, send_one, xn1, d_turned[...], Y_BIT, X_BIT, me)
    pack(keep_two, send_two, xn1, summed[:, width:].astype(BF16), X_BIT, Y_BIT, me)


def tokens_back_kernel(place, pack_q, pack_k, pack_v, tokens, d_hidden, gains, *refs):
    pieces, (input_grad, gain_grad, weight, sems) = (refs[:PIECES], refs[PIECES:])
    width = tokens.shape[1]
    copies = fill(pieces, weight, sems, place[0], pl.ds(0, 3 * width))
    normed, scaled = norm_parts(tokens[...].astype(F32))
    wait_all(copies)
    d_xn1 = dot_nt(pack_q[:, width // 2 :], weight[:, :width])
    d_xn1 = d_xn1 + dot_nt(pack_k[:, width // 2 :], weight[:, width : 2 * width])
    d_xn1 = d_xn1 + dot_nt(pack_v[:, width // 2 :], weight[:, 2 * width :])
    d_norm, gain_term = norm_back(d_xn1, normed, scaled, gains[0:1, :])
    gain_grad[...] = gain_term
    input_grad[...] = (d_hidden[...] + d_norm).astype(BF16)


def product_kernel(width, mine, over_link, core_mine, core_link, own, sent, joined, sems):
    rows = mine.shape[0]
    copies = []
    for index, part in enumerate((mine, over_link, core_mine, core_link)):
        copies.append(pltpu.make_async_copy(part, joined.at[pl.ds(index * rows, rows)], sems.at[index]))
    for copy in copies:
        copy.start()
    wait_all(copies)
    block = lambda top, k: joined[2 * rows * top : 2 * rows * (top + 1), k * width : (k + 1) * width]
    right = joined[:, 4 * width :]
    left = jnp.concatenate([block(0, 2), block(1, 3)], axis=0)
    sent[...] = dot_tt(left, right).astype(BF16)
    left = jnp.concatenate([block(0, 0), block(1, 1)], axis=0)
    own[...] = dot_tt(left, right)


def call(kernel, outs, operands, scratch=(), smem=1, anywhere=(), flops=0, size=0):
    specs = []
    for index in range(len(operands)):
        if index < smem:
            specs.append(pl.BlockSpec(memory_space=pltpu.SMEM))
        elif index in anywhere:
            specs.append(pl.BlockSpec(memory_space=pltpu.HBM))
        else:
            specs.append(pl.BlockSpec(memory_space=pltpu.VMEM))
    return pl.pallas_call(
        kernel,
        out_shape=[jax.ShapeDtypeStruct(shape, kind) for shape, kind in outs],
        in_specs=specs,
        out_specs=[pl.BlockSpec(memory_space=pltpu.VMEM)] * len(outs),
        scratch_shapes=list(scratch),
        cost_estimate=pl.CostEstimate(flops=flops, bytes_accessed=size, transcendentals=0),
        compiler_params=pltpu.CompilerParams(vmem_limit_bytes=VMEM_BYTES),
    )(*operands)


def grad_rows(keep, send, gather_bit, sum_bit, width):
    rows, cols = (keep.shape[0], keep.shape[1] - 4 * width)
    over_link = swap(send, gather_bit)
    core_mine = swap(keep, CORE_BIT)
    core_link = swap(over_link, CORE_BIT)
    own, sent = call(
        lambda *refs: product_kernel(width, *refs),
        [((width, cols), F32), ((width, cols), BF16)],
        [keep, over_link, core_mine, core_link],
        [pltpu.VMEM((4 * rows, 4 * width + cols), BF16), pltpu.SemaphoreType.DMA((4,))],
        smem=0,
        anywhere=(0, 1, 2, 3),
        flops=16 * rows * width * cols,
        size=4 * rows * (4 * width + cols) * 2 + 6 * width * cols,
    )
    return (own + swap(sent, sum_bit).astype(F32), sent)


def line_sum(part):
    first = lax.ppermute(part.astype(BF16), "replica", [(0, 1), (3, 2)])
    pair = (part + first.astype(F32)).astype(BF16)
    other = lax.ppermute(pair, "replica", [(1, 2), (2, 1)])
    total = (pair.astype(F32) + other.astype(F32)).astype(BF16)
    back = lax.ppermute(total, "replica", [(1, 0), (2, 3)])
    place = lax.axis_index("replica")
    middle = (place == 1) | (place == 2)
    return jnp.where(middle, total, back).astype(F32)


def sum_everywhere(values):
    for bit in (CORE_BIT, X_BIT, Y_BIT):
        values = values + swap(values, bit)
    for bit in (1, 2):
        values = values + lax.ppermute(values, "replica", [(i, i ^ bit) for i in range(4)])
    return values


def body_plane(
    tokens,
    input_gain,
    qkv_weight,
    output_weight,
    mlp_gain,
    expand_weight,
    contract_weight,
    positions,
    mask_bias,
    cotangent,
):
    me = lax.axis_index(PLANE)
    along = lax.axis_index("ctx")
    place = jnp.stack([me, along]).astype(jnp.int32)
    shard = qkv_weight.shape[0]
    true_width = expand_weight.shape[1] // 2
    fill_cols = -true_width % 128
    ff_width = true_width + fill_cols
    source, grad_out = (tokens[0], cotangent[0])
    rows, width = source.shape
    gains = jnp.stack([input_gain, mlp_gain], axis=1)
    gains = jnp.pad(gains, ((0, 0), (0, 126)))
    front = jnp.concatenate([qkv_weight, output_weight, gains], axis=1)
    widened = lambda values: jnp.pad(values, ((0, 0), (0, fill_cols)))
    lift = jnp.concatenate(
        [widened(expand_weight[:, :true_width]), widened(expand_weight[:, true_width:])], axis=1
    )
    packed, arrived = gather_pieces(front)
    lift_pieces, arrived = gather_pieces(lift, arrived)
    contract_pieces, arrived = gather_pieces(widened(contract_weight), arrived)
    cosine, sine = rope_tables(positions[0], HEAD_DIM)
    cosine = jnp.concatenate([cosine[:, 0]] * 4, axis=1)
    sine = jnp.concatenate([-sine[:, 0], sine[:, 0]] * 2, axis=1)
    bias = mask_bias[0]
    bias = jnp.concatenate(
        [bias[:, HALF : HALF + rows], jnp.where(along == 0, bias[:, HALF + rows :], bias[:, :HALF])], axis=1
    )
    sems = pltpu.SemaphoreType.DMA((PIECES,))
    front_cols = front.shape[1]
    queries, keys_values, edge, xn1, full_gains = call(
        front_kernel,
        [((rows, width), BF16), ((rows, 2 * width), BF16), ((HALF, 2 * width), BF16), ((rows, width), BF16), ((8, width), F32)],
        [place, source, cosine, sine] + packed,
        [pltpu.VMEM((width, front_cols), BF16), sems],
        anywhere=range(4, 4 + PIECES),
        flops=6 * rows * width * width,
        size=2 * width * front_cols,
    )
    edge = swap(edge, X_BIT)
    attention, totals, hidden, xn2 = call(
        attend_kernel,
        [((rows, width), BF16), ((rows, 128), F32), ((rows, width), F32), ((rows, width), BF16)],
        [place, queries, keys_values, edge, bias, source, full_gains] + packed,
        [pltpu.VMEM((width, width), BF16), sems],
        anywhere=range(7, 7 + PIECES),
        flops=12 * rows * width * width,
        size=4 * width * width,
    )
    half = 4 * shard
    keep_c, send_c, slope_gate, active = call(
        lift_kernel,
        [((rows, half + ff_width), BF16)] * 2 + [((rows, ff_width), F32)] * 2,
        [place, xn2, grad_out] + lift_pieces,
        [pltpu.VMEM((width, 2 * ff_width), BF16), sems],
        anywhere=range(3, 3 + PIECES),
        flops=4 * rows * width * ff_width,
        size=4 * width * ff_width,
    )
    contract_part, contract_sent = grad_rows(keep_c, send_c, X_BIT, Y_BIT, shard)
    layer_out, keep_g, send_g, keep_u, send_u = call(
        contract_kernel,
        [((rows, width), BF16)] + [((rows, half + ff_width), BF16)] * 4,
        [place, keep_c, grad_out, xn2, hidden, slope_gate, active] + contract_pieces,
        [pltpu.VMEM((width, ff_width), BF16), sems],
        anywhere=range(7, 7 + PIECES),
        flops=4 * rows * width * ff_width,
        size=2 * width * ff_width,
    )
    gelu_part, gelu_sent = grad_rows(keep_g, send_g, Y_BIT, X_BIT, shard)
    gate_part, gate_sent = grad_rows(keep_u, send_u, X_BIT, Y_BIT, shard)
    keep_o, send_o, d_hidden, d_attention, mlp_term = call(
        hidden_back_kernel,
        [((rows, half + width), BF16)] * 2 + [((rows, width), F32), ((rows, width), BF16), ((1, width), F32)],
        [place, keep_g, keep_u, grad_out, hidden, full_gains, attention] + lift_pieces + packed,
        [pltpu.VMEM((width, 2 * ff_width), BF16), pltpu.VMEM((width, width), BF16), sems, sems],
        anywhere=range(7, 7 + 2 * PIECES),
        flops=6 * rows * width * ff_width,
        size=6 * width * ff_width,
    )
    output_part, output_sent = grad_rows(keep_o, send_o, Y_BIT, X_BIT, shard)
    d_attention, _ = lax.optimization_barrier((d_attention, contract_sent))
    keep_q, send_q, d_keys_values, d_edge = call(
        attend_back_kernel,
        [((rows, half + width), BF16)] * 2 + [((rows, 2 * width), F32), ((HALF, 2 * width), BF16)],
        [place, queries, keys_values, edge, bias, totals, d_attention, cosine, sine, xn1],
        [pltpu.VMEM((rows, width), BF16)],
        flops=20 * rows * width * width,
        size=4 * width * width,
    )
    d_keys_values, _ = lax.optimization_barrier((d_keys_values, (gelu_sent, gate_sent)))
    query_part, query_sent = grad_rows(keep_q, send_q, X_BIT, Y_BIT, shard)
    keep_k, send_k, keep_v, send_v = call(
        keys_back_kernel,
        [((rows, half + width), BF16)] * 4,
        [place, d_keys_values, swap(d_edge, X_BIT), cosine, sine, xn1],
        [pltpu.VMEM((rows, 2 * width), F32), pltpu.VMEM((rows, width), BF16)],
        flops=rows * width,
        size=8 * rows * width,
    )
    key_part, _ = grad_rows(keep_k, send_k, Y_BIT, X_BIT, shard)
    value_part, _ = grad_rows(keep_v, send_v, X_BIT, Y_BIT, shard)
    d_hidden, _ = lax.optimization_barrier((d_hidden, (contract_part, output_sent)))
    input_grad, input_term = call(
        tokens_back_kernel,
        [((rows, width), BF16), ((1, width), F32)],
        [place, keep_q, keep_k, keep_v, source, d_hidden, full_gains] + packed,
        [pltpu.VMEM((width, 3 * width), BF16), sems],
        anywhere=range(7, 7 + PIECES),
        flops=6 * rows * width * width,
        size=6 * width * width,
    )
    gain_sums = sum_everywhere(jnp.concatenate([input_term, mlp_term], axis=0))
    gain_rows = lax.dynamic_slice_in_dim(gain_sums, me * shard, shard, axis=1)
    contract_grad = line_sum(contract_part)
    gelu_grad = line_sum(gelu_part)
    gate_grad = line_sum(gate_part)
    early_grad = line_sum(jnp.concatenate([output_part, query_part], axis=1))
    late_grad = line_sum(jnp.concatenate([key_part, value_part], axis=1))
    return (
        layer_out[None],
        input_grad[None],
        gain_rows[0],
        jnp.concatenate([early_grad[:, width:], late_grad], axis=1),
        early_grad[:, :width],
        gain_rows[1],
        jnp.concatenate([gelu_grad[:, :true_width], gate_grad[:, :true_width]], axis=1),
        contract_grad[:, :true_width],
    )


def solution(mesh):
    in_specs = (
        P(("replica", "fsdp"), "ctx", None),
        P(("fsdp", "ctx")),
        P(("fsdp", "ctx"), None),
        P(("fsdp", "ctx"), None),
        P(("fsdp", "ctx")),
        P(("fsdp", "ctx"), None),
        P(("fsdp", "ctx"), None),
        P(("replica", "fsdp"), "ctx"),
        P(("replica", "fsdp"), "ctx", None),
        P(("replica", "fsdp"), "ctx", None),
    )
    out_specs = (
        P(("replica", "fsdp"), "ctx", None),
        P(("replica", "fsdp"), "ctx", None),
        P(("fsdp", "ctx")),
        P(("fsdp", "ctx"), None),
        P(("fsdp", "ctx"), None),
        P(("fsdp", "ctx")),
        P(("fsdp", "ctx"), None),
        P(("fsdp", "ctx"), None),
    )
    sizes = (mesh.shape["replica"], mesh.shape["fsdp"], mesh.shape["ctx"])
    body = body_plane if sizes == (4, 4, 2) else body_generic
    return jax.shard_map(body, mesh=mesh, in_specs=in_specs, out_specs=out_specs, check_vma=False)
```

```python
import math

import jax
import jax.numpy as jnp
from jax import lax
from jax.experimental import pallas as pl
from jax.experimental.pallas import tpu as pltpu
from jax.sharding import PartitionSpec as P

HEAD_DIM = 64
HALF = 64


EPS = 1e-05
THETA = 10000.0


def extended_2(cells, sides, width):
    for axis, dim in sides:
        count = lax.axis_size(axis)
        ends = count - 1
        head = lax.slice_in_dim(cells, 0, width, axis=dim)
        tail = lax.slice_in_dim(cells, cells.shape[dim] - width, cells.shape[dim], axis=dim)
        cells = jnp.concatenate(
            [
                lax.ppermute(tail, axis, [(i, (i + 1) % count) for i in range(ends)]),
                cells,
                lax.ppermute(head, axis, [((i + 1) % count, i) for i in range(ends)]),
            ],
            axis=dim,
        )
    return cells


def from_behind(value, axis, steps):
    count = lax.axis_size(axis)
    first, last = (max(0, -steps), min(count, count - steps))
    return lax.ppermute(value, axis, [(source, source + steps) for source in range(first, last)])


def layer_norm(values, gain):
    center = values - jnp.mean(values, axis=-1, keepdims=True)
    variance = jnp.mean(center * center, axis=-1, keepdims=True)
    scaled = lax.rsqrt(variance + EPS)
    normed = center * scaled
    return (normed, scaled, (normed * gain.astype(jnp.float32)).astype(jnp.bfloat16))


def layer_norm_back(incoming, normed, scaled, gain):
    weighted = incoming * gain.astype(jnp.float32)
    gain_grad = jnp.sum(incoming * normed, axis=0)
    mean_one = jnp.mean(weighted, axis=-1, keepdims=True)
    mean_two = jnp.mean(weighted * normed, axis=-1, keepdims=True)
    return (scaled * (weighted - mean_one - normed * mean_two), gain_grad)


def rope_tables(positions, head_size):
    half_dim = head_size // 2
    exponent = jnp.arange(half_dim, dtype=jnp.float32) * (2.0 / head_size)
    frequency = jnp.exp(-math.log(THETA) * exponent)
    angles = positions.astype(jnp.float32)[:, None] * frequency[None, :]
    return (jnp.cos(angles)[:, None, :], jnp.sin(angles)[:, None, :])


def rotate(values, cosine, sine):
    half_dim = values.shape[-1] // 2
    lower_half, upper_half = (values[..., :half_dim], values[..., half_dim:])
    return jnp.concatenate(
        [lower_half * cosine - upper_half * sine, upper_half * cosine + lower_half * sine], axis=-1
    )


def rotate_back(values, cosine, sine):
    half_dim = values.shape[-1] // 2
    lower_half, upper_half = (values[..., :half_dim], values[..., half_dim:])
    return jnp.concatenate(
        [lower_half * cosine + upper_half * sine, upper_half * cosine - lower_half * sine], axis=-1
    )


def gelu_slope(values):
    cdf_part = 0.5 * (1.0 + jax.scipy.special.erf(values * (1.0 / math.sqrt(2.0))))
    density = jnp.exp(-0.5 * values * values) * (1.0 / math.sqrt(2.0 * math.pi))
    return cdf_part + values * density


def block_scores(queries, key_rows, additive):
    factor = 1.0 / math.sqrt(queries.shape[-1])
    scores = jnp.einsum("qhd,khd->hqk", queries, key_rows, preferred_element_type=jnp.float32)
    return scores * factor + additive[None]


def attend(queries, key_rows, value_rows, additive):
    scores = block_scores(queries, key_rows, additive)
    row_peak = jnp.max(scores, axis=-1, keepdims=True)
    exponent = jnp.exp(scores - row_peak)
    row_total = jnp.sum(exponent, axis=-1, keepdims=True)
    soft_weights = (exponent / row_total).astype(jnp.bfloat16)
    mixed = jnp.einsum("hqk,khd->qhd", soft_weights, value_rows, preferred_element_type=jnp.float32)
    return (mixed.astype(jnp.bfloat16), row_peak[..., 0] + jnp.log(row_total[..., 0]))


def attend_back(queries, key_rows, value_rows, additive, log_total, d_mixed):
    factor = 1.0 / math.sqrt(queries.shape[-1])
    scores = block_scores(queries, key_rows, additive)
    recomputed = jnp.exp(scores - log_total[..., None])
    d_soft = jnp.einsum("qhd,khd->hqk", d_mixed, value_rows, preferred_element_type=jnp.float32)
    center = jnp.sum(recomputed * d_soft, axis=-1, keepdims=True)
    d_scores = (recomputed * (d_soft - center) * factor).astype(jnp.bfloat16)
    d_queries = jnp.einsum("hqk,khd->qhd", d_scores, key_rows, preferred_element_type=jnp.float32)
    d_keys = jnp.einsum("hqk,qhd->khd", d_scores, queries, preferred_element_type=jnp.float32)
    d_values = jnp.einsum(
        "hqk,qhd->khd", recomputed.astype(jnp.bfloat16), d_mixed, preferred_element_type=jnp.float32
    )
    return (d_queries, d_keys, d_values)


def body_generic(
    tokens,
    input_gain,
    qkv_weight,
    output_weight,
    mlp_gain,
    expand_weight,
    contract_weight,
    positions,
    mask_bias,
    cotangent,
):
    gathered = (
        lax.all_gather(input_gain, ("fsdp", "ctx"), axis=0, tiled=True),
        lax.all_gather(qkv_weight, ("fsdp", "ctx"), axis=0, tiled=True),
        lax.all_gather(output_weight, ("fsdp", "ctx"), axis=0, tiled=True),
        lax.all_gather(mlp_gain, ("fsdp", "ctx"), axis=0, tiled=True),
        lax.all_gather(expand_weight, ("fsdp", "ctx"), axis=0, tiled=True),
        lax.all_gather(contract_weight, ("fsdp", "ctx"), axis=0, tiled=True),
    )
    full_input_gain, full_qkv, full_output, full_mlp_gain, full_expand, full_contract = gathered
    residual = tokens[0].astype(jnp.float32)
    row_count, model_width = residual.shape
    head_count = model_width // HEAD_DIM
    cosine, sine = rope_tables(positions[0], HEAD_DIM)
    normed1, scaled1, xn1 = layer_norm(residual, full_input_gain)
    projected = jnp.dot(xn1, full_qkv, preferred_element_type=jnp.float32).reshape(
        row_count, 3, head_count, HEAD_DIM
    )
    queries = rotate(projected[:, 0], cosine, sine).astype(jnp.bfloat16)
    key_rows = rotate(projected[:, 1], cosine, sine).astype(jnp.bfloat16)
    value_rows = projected[:, 2].astype(jnp.bfloat16)
    packed = jnp.concatenate(
        [key_rows.reshape(row_count, model_width), value_rows.reshape(row_count, model_width)],
        axis=1,
    )
    extended = extended_2(packed, (("ctx", 0),), HALF)
    extent = extended.shape[0]
    key_ext = extended[:, :model_width].reshape(extent, head_count, HEAD_DIM)
    value_ext = extended[:, model_width:].reshape(extent, head_count, HEAD_DIM)
    additive = mask_bias[0]
    mixed, log_total = attend(queries, key_ext, value_ext, additive)
    attention = mixed.reshape(row_count, model_width)
    hidden = residual + jnp.dot(attention, full_output, preferred_element_type=jnp.float32)
    normed2, scaled2, xn2 = layer_norm(hidden, full_mlp_gain)
    lifted = jnp.dot(xn2, full_expand, preferred_element_type=jnp.float32)
    ff_width = lifted.shape[1] // 2
    gelu_input = lifted[:, :ff_width]
    gate_part = lifted[:, ff_width:]
    activated = jax.nn.gelu(gelu_input, approximate=False)
    gated = (activated * gate_part).astype(jnp.bfloat16)
    down_out = jnp.einsum("tf,jf->tj", gated, full_contract, preferred_element_type=jnp.float32)
    layer_out = (hidden + down_out).astype(jnp.bfloat16)
    back_input_gain, back_qkv, back_output, back_mlp_gain, back_expand, back_contract = gathered
    grad_out = cotangent[0]
    d_gated = jnp.dot(grad_out, back_contract, preferred_element_type=jnp.float32)
    d_lifted = jnp.concatenate(
        [d_gated * gate_part * gelu_slope(gelu_input), d_gated * activated], axis=1
    ).astype(jnp.bfloat16)
    d_xn2 = jnp.einsum("tc,dc->td", d_lifted, back_expand, preferred_element_type=jnp.float32)
    d_norm2, mlp_gain_term = layer_norm_back(d_xn2, normed2, scaled2, back_mlp_gain)
    d_hidden = grad_out.astype(jnp.float32) + d_norm2
    d_proj = d_hidden.astype(jnp.bfloat16)
    d_attention = jnp.einsum(
        "tj,ij->ti", d_proj, back_output, preferred_element_type=jnp.float32
    ).astype(jnp.bfloat16)
    d_queries, d_key_ext, d_value_ext = attend_back(
        queries,
        key_ext,
        value_ext,
        additive,
        log_total,
        d_attention.reshape(row_count, head_count, HEAD_DIM),
    )
    grad_ext = jnp.concatenate(
        [d_key_ext.reshape(extent, model_width), d_value_ext.reshape(extent, model_width)], axis=1
    )
    from_next = from_behind(grad_ext[:HALF], "ctx", -1)
    from_prev = from_behind(grad_ext[row_count + HALF :], "ctx", 1)
    grad_kv = grad_ext[HALF : HALF + row_count]
    grad_kv = grad_kv + jnp.pad(from_prev, ((0, row_count - HALF), (0, 0)))
    grad_kv = grad_kv + jnp.pad(from_next, ((row_count - HALF, 0), (0, 0)))
    d_keys = rotate_back(
        grad_kv[:, :model_width].reshape(row_count, head_count, HEAD_DIM), cosine, sine
    )
    d_values = grad_kv[:, model_width:]
    d_queries = rotate_back(d_queries, cosine, sine)
    d_projected = jnp.concatenate(
        [
            d_queries.reshape(row_count, model_width),
            d_keys.reshape(row_count, model_width),
            d_values,
        ],
        axis=1,
    ).astype(jnp.bfloat16)
    d_xn1 = jnp.einsum("tc,dc->td", d_projected, back_qkv, preferred_element_type=jnp.float32)
    d_norm1, input_gain_term = layer_norm_back(d_xn1, normed1, scaled1, back_input_gain)
    input_grad = (d_hidden + d_norm1).astype(jnp.bfloat16)
    left_one, left_two, left_three, left_four = (xn1, attention, xn2, grad_out)
    gain_one, gain_two = (input_gain_term, mlp_gain_term)
    qkv_term = jnp.einsum("ti,tj->ij", left_one, d_projected, preferred_element_type=jnp.float32)
    output_term = jnp.einsum("ti,tj->ij", left_two, d_proj, preferred_element_type=jnp.float32)
    expand_term = jnp.einsum("ti,tj->ij", left_three, d_lifted, preferred_element_type=jnp.float32)
    contract_term = jnp.einsum("ti,tj->ij", left_four, gated, preferred_element_type=jnp.float32)
    first_gain = gain_one[:, None]
    second_gain = gain_two[:, None]
    shares = lax.psum_scatter(
        jnp.concatenate(
            [qkv_term, output_term, expand_term, contract_term, first_gain, second_gain], axis=1
        ),
        ("fsdp", "ctx"),
        scatter_dimension=0,
        tiled=True,
    )
    result = lax.psum(shares, "replica")
    qkv_cols = 3 * model_width
    expand_cols = 2 * ff_width
    qkv_grad = result[:, :qkv_cols]
    output_grad = result[:, qkv_cols : qkv_cols + model_width]
    offset = qkv_cols + model_width
    expand_grad = result[:, offset : offset + expand_cols]
    offset = offset + expand_cols
    contract_grad = result[:, offset : offset + ff_width]
    offset = offset + ff_width
    input_gain_grad = result[:, offset]
    mlp_gain_grad = result[:, offset + 1]
    return (
        layer_out[None],
        input_grad[None],
        input_gain_grad,
        qkv_grad,
        output_grad,
        mlp_gain_grad,
        expand_grad,
        contract_grad,
    )


X_BIT, CORE_BIT, Y_BIT = (1, 2, 4)
PLANE = ("fsdp", "ctx")
PLANE_SIZE = 8
PIECES = 10
VMEM_BYTES = 50 * 1024 * 1024
F32, BF16 = (jnp.float32, jnp.bfloat16)


def swap(value, bit):
    return lax.ppermute(value, PLANE, [(i, i ^ bit) for i in range(PLANE_SIZE)])


def later(value, *others):
    return lax.optimization_barrier((value, others))[0]


def gather_pieces(own, after=()):
    own = later(own, after)
    half = own.shape[0] // 2
    over_x = swap(own, X_BIT)
    over_y = swap(own, Y_BIT)
    first = [own, over_x, over_y, swap(over_x[:half], Y_BIT), swap(over_y[half:], X_BIT)]
    second = [swap(part, CORE_BIT) for part in first]
    return (first + second, tuple(first[3:]))


def fill(pieces, target, sems, me, columns=None):
    shard = target.shape[0] // PLANE_SIZE
    half = shard // 2
    corner = X_BIT | Y_BIT
    places = [(0, 0, shard), (X_BIT, 0, shard), (Y_BIT, 0, shard), (corner, 0, half), (corner, half, half)]
    places = places + [(offset | CORE_BIT, start, rows) for offset, start, rows in places]
    copies = []
    for index, (piece, (offset, start, rows)) in enumerate(zip(pieces, places)):
        row = pl.multiple_of((me ^ offset) * shard + start, half)
        source = piece if columns is None else piece.at[:, columns]
        copies.append(pltpu.make_async_copy(source, target.at[pl.ds(row, rows)], sems.at[index]))
    for copy in copies:
        copy.start()
    return copies


def wait_all(copies):
    for copy in copies:
        copy.wait()


def pack(keep, send, left, right, gather_bit, sum_bit, me):
    rows, width = (left.shape[0], left.shape[1] // PLANE_SIZE)
    for slot, offset in enumerate([0, CORE_BIT, sum_bit, CORE_BIT | sum_bit]):
        for target, flip in ((keep, 0), (send, gather_bit)):
            source = pl.multiple_of((me ^ (offset | flip)) * width, width)
            target[:rows, slot * width : (slot + 1) * width] = left[:, pl.ds(source, width)]
    keep[:rows, 4 * width :] = right
    send[:rows, 4 * width :] = right


def turn(values, cosine, sine):
    lane = lax.broadcasted_iota(jnp.int32, values.shape, 1)
    low = lane % HEAD_DIM < HEAD_DIM // 2
    other = jnp.where(
        low,
        pltpu.roll(values, values.shape[1] - HEAD_DIM // 2, 1),
        pltpu.roll(values, HEAD_DIM // 2, 1),
    )
    return values * cosine + other * sine


def dot_tt(one, two):
    return lax.dot_general(one, two, (((0,), (0,)), ((), ())), preferred_element_type=F32)


def dot_nt(one, two):
    return lax.dot_general(one, two, (((1,), (1,)), ((), ())), preferred_element_type=F32)


def dot_nn(one, two):
    return jnp.dot(one, two, preferred_element_type=F32)


def norm_parts(values):
    center = values - jnp.mean(values, axis=-1, keepdims=True)
    variance = jnp.mean(center * center, axis=-1, keepdims=True)
    scaled = lax.rsqrt(variance + EPS)
    return (center * scaled, scaled)


def norm_back(incoming, normed, scaled, gain):
    weighted = incoming * gain
    gain_grad = jnp.sum(incoming * normed, axis=0, keepdims=True)
    mean_one = jnp.mean(weighted, axis=-1, keepdims=True)
    mean_two = jnp.mean(weighted * normed, axis=-1, keepdims=True)
    return (scaled * (weighted - mean_one - normed * mean_two), gain_grad)


def front_kernel(place, tokens, cosine, sine, *refs):
    pieces, (queries, keys_values, edge, xn1, gains, weight, sems) = (refs[:PIECES], refs[PIECES:])
    me, along = (place[0], place[1])
    copies = fill(pieces, weight, sems, me)
    normed, _ = norm_parts(tokens[...].astype(F32))
    width = tokens.shape[1]
    wait_all(copies)
    turned = weight[:, 4 * width :].astype(F32).T
    gains[...] = turned[: gains.shape[0]]
    rounded = (normed * gains[0:1, :]).astype(BF16)
    xn1[...] = rounded
    pair = cosine.shape[1]
    projected = dot_nn(rounded, weight[:, : 3 * width])
    for start in range(0, width, pair):
        part = projected[:, start : start + pair]
        queries[:, start : start + pair] = turn(part, cosine[...], sine[...]).astype(BF16)
        part = projected[:, width + start : width + start + pair]
        keys_values[:, start : start + pair] = turn(part, cosine[...], sine[...]).astype(BF16)
    keys_values[:, width:] = projected[:, 2 * width :].astype(BF16)
    rows = edge.shape[0]
    edge[...] = keys_values[pl.ds(pl.multiple_of((1 - along) * rows, rows), rows), :]


def head_masks(shape):
    lane = lax.broadcasted_iota(jnp.int32, shape, 1)
    return lane < HEAD_DIM


def attend_kernel(place, queries, keys_values, edge, bias, tokens, gains, *refs):
    pieces, (attention, totals, hidden, xn2, weight, sems) = (refs[:PIECES], refs[PIECES:])
    width = tokens.shape[1]
    copies = fill(pieces, weight, sems, place[0], pl.ds(3 * width, width))
    pair = 2 * HEAD_DIM
    factor = 1.0 / math.sqrt(HEAD_DIM)
    rows = queries.shape[0]
    is_first = head_masks((rows, pair))
    lane = lax.broadcasted_iota(jnp.int32, totals.shape, 1)
    logs = jnp.zeros(totals.shape, F32)
    for start in range(0, width, pair):
        two = queries[:, start : start + pair]
        keys = jnp.concatenate([keys_values[:, start : start + pair], edge[:, start : start + pair]], axis=0)
        vals = jnp.concatenate(
            [keys_values[:, width + start : width + start + pair], edge[:, width + start : width + start + pair]],
            axis=0,
        )
        outs = []
        for which in range(2):
            mask = is_first if which == 0 else jnp.logical_not(is_first)
            one = jnp.where(mask, two, jnp.zeros_like(two))
            scores = dot_nt(one, keys) * factor + bias[...]
            peak = jnp.max(scores, axis=-1, keepdims=True)
            exponent = jnp.exp(scores - peak)
            total = jnp.sum(exponent, axis=-1, keepdims=True)
            soft = (exponent / total).astype(BF16)
            outs.append(dot_nn(soft, vals))
            logs = jnp.where(lane == 2 * (start // pair) + which, peak + jnp.log(total), logs)
        attention[:, start : start + pair] = jnp.where(is_first, outs[0], outs[1]).astype(BF16)
    totals[...] = logs
    wait_all(copies)
    result = tokens[...].astype(F32) + dot_nn(attention[...], weight[...])
    hidden[...] = result
    normed, _ = norm_parts(result)
    xn2[...] = (normed * gains[1:2, :]).astype(BF16)


def lift_kernel(place, xn2, grad_out, *refs):
    pieces, (keep, send, slope_gate, active, weight, sems) = (refs[:PIECES], refs[PIECES:])
    me = place[0]
    cols = active.shape[1]
    wait_all(fill(pieces, weight, sems, me, pl.ds(0, 2 * cols)))
    gelu_input = dot_nn(xn2[...], weight[:, :cols])
    gate_part = dot_nn(xn2[...], weight[:, cols:])
    cdf_part = 0.5 * (1.0 + lax.erf(gelu_input * (1.0 / math.sqrt(2.0))))
    density = jnp.exp(-0.5 * gelu_input * gelu_input) * (1.0 / math.sqrt(2.0 * math.pi))
    activated = gelu_input * cdf_part
    active[...] = activated
    slope_gate[...] = gate_part * (cdf_part + gelu_input * density)
    pack(keep, send, grad_out, (activated * gate_part).astype(BF16), X_BIT, Y_BIT, me)


def contract_kernel(place, gated_pack, grad_out, xn2, hidden, slope_gate, active, *refs):
    pieces, rest = (refs[:PIECES], refs[PIECES:])
    layer_out, keep_one, send_one, keep_two, send_two, weight, sems = rest
    me = place[0]
    cols = weight.shape[1]
    wait_all(fill(pieces, weight, sems, me, pl.ds(2 * cols, cols)))
    d_gated = dot_nn(grad_out[...], weight[...])
    pack(keep_one, send_one, xn2, (d_gated * slope_gate[...]).astype(BF16), Y_BIT, X_BIT, me)
    pack(keep_two, send_two, xn2, (d_gated * active[...]).astype(BF16), X_BIT, Y_BIT, me)
    gated = gated_pack[:, xn2.shape[1] // 2 :]
    layer_out[...] = (hidden[...] + dot_nt(gated, weight[...])).astype(BF16)


def hidden_back_kernel(place, pack_one, pack_two, grad_out, hidden, gains, attention, *refs):
    first, third = (refs[:PIECES], refs[PIECES : 2 * PIECES])
    keep, send, d_hidden, d_attention, gain_grad, lift_weight, weight, sems, sems_three = refs[2 * PIECES :]
    me = place[0]
    width = hidden.shape[1]
    copies = fill(first, lift_weight, sems, me, pl.ds(0, lift_weight.shape[1]))
    lasts = fill(third, weight, sems_three, me, pl.ds(3 * width, width))
    normed, scaled = norm_parts(hidden[...])
    wait_all(copies)
    cols = lift_weight.shape[1] // 2
    d_xn2 = dot_nt(pack_one[:, width // 2 :], lift_weight[:, :cols])
    d_xn2 = d_xn2 + dot_nt(pack_two[:, width // 2 :], lift_weight[:, cols:])
    d_norm, gain_term = norm_back(d_xn2, normed, scaled, gains[1:2, :])
    gain_grad[...] = gain_term
    total = grad_out[...].astype(F32) + d_norm
    d_hidden[...] = total
    rounded = total.astype(BF16)
    wait_all(lasts)
    d_attention[...] = dot_nt(rounded, weight[...]).astype(BF16)
    pack(keep, send, attention, rounded, Y_BIT, X_BIT, me)


def attend_back_kernel(
    place, queries, keys_values, edge, bias, totals, d_attention, cosine, sine, d_turned, d_keys_values, d_edge
):
    width = queries.shape[1]
    pair = 2 * HEAD_DIM
    factor = 1.0 / math.sqrt(HEAD_DIM)
    rows = queries.shape[0]
    is_first = head_masks((rows, pair))
    is_first_key = head_masks((rows + edge.shape[0], pair))
    for start in range(0, width, pair):
        here = slice(start, start + pair)
        there = slice(width + start, width + start + pair)
        two = queries[:, here]
        d_two = d_attention[:, here]
        keys = jnp.concatenate([keys_values[:, here], edge[:, here]], axis=0)
        vals = jnp.concatenate([keys_values[:, there], edge[:, there]], axis=0)
        d_queries, d_keys, d_vals = ([], [], [])
        for which in range(2):
            mask = is_first if which == 0 else jnp.logical_not(is_first)
            one = jnp.where(mask, two, jnp.zeros_like(two))
            d_one = jnp.where(mask, d_two, jnp.zeros_like(d_two))
            head = 2 * (start // pair) + which
            scores = dot_nt(one, keys) * factor + bias[...]
            recomputed = jnp.exp(scores - totals[:, head : head + 1])
            d_soft = dot_nt(d_one, vals)
            center = jnp.sum(recomputed * d_soft, axis=-1, keepdims=True)
            d_scores = (recomputed * (d_soft - center) * factor).astype(BF16)
            d_queries.append(dot_nn(d_scores, keys))
            d_keys.append(dot_tt(d_scores, two))
            d_vals.append(dot_tt(recomputed.astype(BF16), d_two))
        d_query = jnp.where(is_first, d_queries[0], d_queries[1])
        d_turned[:, here] = turn(d_query, cosine[...], -sine[...]).astype(BF16)
        d_key = jnp.where(is_first_key, d_keys[0], d_keys[1])
        d_val = jnp.where(is_first_key, d_vals[0], d_vals[1])
        d_keys_values[:, here] = d_key[:rows]
        d_keys_values[:, there] = d_val[:rows]
        d_edge[:, here] = d_key[rows:].astype(BF16)
        d_edge[:, there] = d_val[rows:].astype(BF16)


def keys_back_kernel(
    place, d_keys_values, arrived, cosine, sine, xn1, keep_one, send_one, keep_two, send_two, summed, d_turned
):
    me, along = (place[0], place[1])
    width = xn1.shape[1]
    pair = 2 * HEAD_DIM
    rows = arrived.shape[0]
    summed[...] = d_keys_values[...]
    where = pl.ds(pl.multiple_of((1 - along) * rows, rows), rows)
    summed[where, :] = summed[where, :] + arrived[...].astype(F32)
    for start in range(0, width, pair):
        here = slice(start, start + pair)
        d_turned[:, here] = turn(summed[:, here], cosine[...], -sine[...]).astype(BF16)
    pack(keep_one, send_one, xn1, d_turned[...], Y_BIT, X_BIT, me)
    pack(keep_two, send_two, xn1, summed[:, width:].astype(BF16), X_BIT, Y_BIT, me)


def tokens_back_kernel(place, d_queries, pack_k, pack_v, tokens, xn1, d_hidden, gains, mlp_term, *refs):
    pieces, (keep, send, input_grad, weight, sems) = (refs[:PIECES], refs[PIECES:])
    rows = tokens.shape[0]
    width = tokens.shape[1]
    copies = fill(pieces, weight, sems, place[0], pl.ds(0, 3 * width))
    normed, scaled = norm_parts(tokens[...].astype(F32))
    wait_all(copies)
    d_xn1 = dot_nt(d_queries[...], weight[:, :width])
    d_xn1 = d_xn1 + dot_nt(pack_k[:, width // 2 :], weight[:, width : 2 * width])
    d_xn1 = d_xn1 + dot_nt(pack_v[:, width // 2 :], weight[:, 2 * width :])
    d_norm, gain_term = norm_back(d_xn1, normed, scaled, gains[0:1, :])
    pack(keep, send, xn1, d_queries[...], X_BIT, Y_BIT, place[0])
    extra = keep.shape[0] - rows
    line = lax.broadcasted_iota(jnp.int32, (extra, width), 0)
    terms = jnp.where(line == 0, mlp_term[...], jnp.where(line == 1, gain_term, 0.0)).astype(BF16)
    for target in (keep, send):
        target[rows:, : width // 2] = jnp.zeros((extra, width // 2), BF16)
        target[rows:, width // 2 :] = terms
    input_grad[...] = (d_hidden[...] + d_norm).astype(BF16)


def product_kernel(width, rows, mine, over_link, core_mine, core_link, own, sent, joined, *refs):
    terms, sems = (refs[0] if len(refs) > 1 else None, refs[-1])
    copies = []
    for index, part in enumerate((mine, over_link, core_mine, core_link)):
        source = part if terms is None else part.at[pl.ds(0, rows)]
        copies.append(pltpu.make_async_copy(source, joined.at[pl.ds(index * rows, rows)], sems.at[index]))
        if terms is not None:
            extra = terms.shape[1]
            copies.append(
                pltpu.make_async_copy(part.at[pl.ds(rows, extra)], terms.at[index], sems.at[4 + index])
            )
    for copy in copies:
        copy.start()
    wait_all(copies)
    block = lambda top, k: joined[2 * rows * top : 2 * rows * (top + 1), k * width : (k + 1) * width]
    right = joined[:, 4 * width :]
    left = jnp.concatenate([block(0, 2), block(1, 3)], axis=0)
    sent[:width] = dot_tt(left, right).astype(BF16)
    left = jnp.concatenate([block(0, 0), block(1, 1)], axis=0)
    own[:width] = dot_tt(left, right)
    if terms is not None:
        total = sum(terms[index, :, 4 * width :].astype(F32) for index in range(4))
        own[width:] = total
        sent[width:] = total.astype(BF16)


def call(kernel, outs, operands, scratch=(), smem=1, anywhere=(), flops=0, size=0):
    specs = []
    for index in range(len(operands)):
        if index < smem:
            specs.append(pl.BlockSpec(memory_space=pltpu.SMEM))
        elif index in anywhere:
            specs.append(pl.BlockSpec(memory_space=pltpu.HBM))
        else:
            specs.append(pl.BlockSpec(memory_space=pltpu.VMEM))
    return pl.pallas_call(
        kernel,
        out_shape=[jax.ShapeDtypeStruct(shape, kind) for shape, kind in outs],
        in_specs=specs,
        out_specs=[pl.BlockSpec(memory_space=pltpu.VMEM)] * len(outs),
        scratch_shapes=list(scratch),
        cost_estimate=pl.CostEstimate(flops=flops, bytes_accessed=size, transcendentals=0),
        compiler_params=pltpu.CompilerParams(vmem_limit_bytes=VMEM_BYTES),
    )(*operands)


def grad_rows(keep, send, gather_bit, sum_bit, width, after=()):
    rows = keep.shape[0] // 128 * 128
    extra = keep.shape[0] - rows
    cols = keep.shape[1] - 4 * width
    over_link = swap(send, gather_bit)
    keep, over_link = later((keep, over_link), after)
    core_mine = swap(keep, CORE_BIT)
    core_link = swap(over_link, CORE_BIT)
    scratch = [pltpu.VMEM((4 * rows, 4 * width + cols), BF16)]
    if extra:
        scratch.append(pltpu.VMEM((4, extra, 4 * width + cols), BF16))
    own, sent = call(
        lambda *refs: product_kernel(width, rows, *refs),
        [((width + extra, cols), F32), ((width + extra, cols), BF16)],
        [keep, over_link, core_mine, core_link],
        scratch + [pltpu.SemaphoreType.DMA((8,))],
        smem=0,
        anywhere=(0, 1, 2, 3),
        flops=16 * rows * width * cols,
        size=4 * rows * (4 * width + cols) * 2 + 6 * width * cols,
    )
    return (own + swap(sent, sum_bit).astype(F32), sent)


def line_sum(part):
    first = lax.ppermute(part.astype(BF16), "replica", [(0, 1), (3, 2)])
    pair = (part + first.astype(F32)).astype(BF16)
    other = lax.ppermute(pair, "replica", [(1, 2), (2, 1)])
    total = (pair.astype(F32) + other.astype(F32)).astype(BF16)
    back = lax.ppermute(total, "replica", [(1, 0), (2, 3)])
    place = lax.axis_index("replica")
    middle = (place == 1) | (place == 2)
    return jnp.where(middle, total, back).astype(F32)


def cross_sum(part):
    half = part.shape[1] // 2
    even = lax.axis_index("replica") % 2 == 0
    step = lambda value, bit: lax.ppermute(value, "replica", [(i, i ^ bit) for i in range(4)])
    low, high = (part[:, :half], part[:, half:])
    got = step(jnp.where(even, high, low).astype(BF16), 1)
    pair = (jnp.where(even, low, high) + got.astype(F32)).astype(BF16)
    total = (pair.astype(F32) + step(pair, 2).astype(F32)).astype(BF16)
    back = step(total, 1)
    return jnp.concatenate([jnp.where(even, total, back), jnp.where(even, back, total)], axis=1).astype(F32)


def body_plane(
    tokens,
    input_gain,
    qkv_weight,
    output_weight,
    mlp_gain,
    expand_weight,
    contract_weight,
    positions,
    mask_bias,
    cotangent,
):
    me = lax.axis_index(PLANE)
    along = lax.axis_index("ctx")
    place = jnp.stack([me, along]).astype(jnp.int32)
    shard = qkv_weight.shape[0]
    true_width = expand_weight.shape[1] // 2
    fill_cols = -true_width % 128
    ff_width = true_width + fill_cols
    source, grad_out = (tokens[0], cotangent[0])
    rows, width = source.shape
    gains = jnp.stack([input_gain, mlp_gain], axis=1)
    gains = jnp.pad(gains, ((0, 0), (0, 126)))
    front = jnp.concatenate([qkv_weight, output_weight, gains], axis=1)
    widened = lambda values: jnp.pad(values, ((0, 0), (0, fill_cols)))
    feed = jnp.concatenate(
        [
            widened(expand_weight[:, :true_width]),
            widened(expand_weight[:, true_width:]),
            widened(contract_weight),
        ],
        axis=1,
    )
    packed, arrived = gather_pieces(front)
    feed_pieces, arrived = gather_pieces(feed, arrived)
    cosine, sine = rope_tables(positions[0], HEAD_DIM)
    cosine = jnp.concatenate([cosine[:, 0]] * 4, axis=1)
    sine = jnp.concatenate([-sine[:, 0], sine[:, 0]] * 2, axis=1)
    bias = mask_bias[0]
    bias = jnp.concatenate(
        [bias[:, HALF : HALF + rows], jnp.where(along == 0, bias[:, HALF + rows :], bias[:, :HALF])], axis=1
    )
    sems = pltpu.SemaphoreType.DMA((PIECES,))
    front_cols = front.shape[1]
    queries, keys_values, edge, xn1, full_gains = call(
        front_kernel,
        [((rows, width), BF16), ((rows, 2 * width), BF16), ((HALF, 2 * width), BF16), ((rows, width), BF16), ((8, width), F32)],
        [place, source, cosine, sine] + packed,
        [pltpu.VMEM((width, front_cols), BF16), sems],
        anywhere=range(4, 4 + PIECES),
        flops=6 * rows * width * width,
        size=2 * width * front_cols,
    )
    edge = swap(edge, X_BIT)
    attention, totals, hidden, xn2 = call(
        attend_kernel,
        [((rows, width), BF16), ((rows, 128), F32), ((rows, width), F32), ((rows, width), BF16)],
        [place, queries, keys_values, edge, bias, source, full_gains] + packed,
        [pltpu.VMEM((width, width), BF16), sems],
        anywhere=range(7, 7 + PIECES),
        flops=12 * rows * width * width,
        size=4 * width * width,
    )
    half = 4 * shard
    keep_c, send_c, slope_gate, active = call(
        lift_kernel,
        [((rows, half + ff_width), BF16)] * 2 + [((rows, ff_width), F32)] * 2,
        [place, xn2, grad_out] + feed_pieces,
        [pltpu.VMEM((width, 2 * ff_width), BF16), sems],
        anywhere=range(3, 3 + PIECES),
        flops=4 * rows * width * ff_width,
        size=4 * width * ff_width,
    )
    layer_out, keep_g, send_g, keep_u, send_u = call(
        contract_kernel,
        [((rows, width), BF16)] + [((rows, half + ff_width), BF16)] * 4,
        [place, keep_c, grad_out, xn2, hidden, slope_gate, active] + feed_pieces,
        [pltpu.VMEM((width, ff_width), BF16), sems],
        anywhere=range(7, 7 + PIECES),
        flops=4 * rows * width * ff_width,
        size=2 * width * ff_width,
    )
    keep_o, send_o, d_hidden, d_attention, mlp_term = call(
        hidden_back_kernel,
        [((rows, half + width), BF16)] * 2 + [((rows, width), F32), ((rows, width), BF16), ((1, width), F32)],
        [place, keep_g, keep_u, grad_out, hidden, full_gains, attention] + feed_pieces + packed,
        [pltpu.VMEM((width, 2 * ff_width), BF16), pltpu.VMEM((width, width), BF16), sems, sems],
        anywhere=range(7, 7 + 2 * PIECES),
        flops=6 * rows * width * ff_width,
        size=6 * width * ff_width,
    )
    contract_part, contract_sent = grad_rows(keep_c, send_c, X_BIT, Y_BIT, shard, d_attention)
    d_attention = later(d_attention, contract_sent)
    d_queries, d_keys_values, d_edge = call(
        attend_back_kernel,
        [((rows, width), BF16), ((rows, 2 * width), F32), ((HALF, 2 * width), BF16)],
        [place, queries, keys_values, edge, bias, totals, d_attention, cosine, sine],
        flops=20 * rows * width * width,
        size=4 * width * width,
    )
    gelu_part, gelu_sent = grad_rows(keep_g, send_g, Y_BIT, X_BIT, shard, d_edge)
    gate_part, gate_sent = grad_rows(keep_u, send_u, X_BIT, Y_BIT, shard, d_edge)
    keep_k, send_k, keep_v, send_v = call(
        keys_back_kernel,
        [((rows, half + width), BF16)] * 4,
        [place, d_keys_values, swap(d_edge, X_BIT), cosine, sine, xn1],
        [pltpu.VMEM((rows, 2 * width), F32), pltpu.VMEM((rows, width), BF16)],
        flops=rows * width,
        size=8 * rows * width,
    )
    key_part, _ = grad_rows(keep_k, send_k, Y_BIT, X_BIT, shard)
    value_part, _ = grad_rows(keep_v, send_v, X_BIT, Y_BIT, shard)
    d_hidden = later(d_hidden, contract_part, gelu_sent, gate_sent)
    keep_q, send_q, input_grad = call(
        tokens_back_kernel,
        [((rows + 16, half + width), BF16)] * 2 + [((rows, width), BF16)],
        [place, d_queries, keep_k, keep_v, source, xn1, d_hidden, full_gains, mlp_term] + packed,
        [pltpu.VMEM((width, 3 * width), BF16), sems],
        anywhere=range(9, 9 + PIECES),
        flops=6 * rows * width * width,
        size=6 * width * width,
    )
    output_part, _ = grad_rows(keep_o, send_o, Y_BIT, X_BIT, shard, keep_k)
    query_part, _ = grad_rows(keep_q, send_q, X_BIT, Y_BIT, shard)
    contract_grad = line_sum(contract_part)
    gelu_grad = line_sum(gelu_part)
    gate_grad = line_sum(gate_part)
    late_grad = cross_sum(jnp.concatenate([key_part, value_part], axis=1))
    early_grad = line_sum(jnp.concatenate([output_part, query_part], axis=0))
    query_grad = early_grad[shard : 2 * shard]
    gain_rows = lax.dynamic_slice_in_dim(early_grad[2 * shard : 2 * shard + 2], me * shard, shard, axis=1)
    return (
        layer_out[None],
        input_grad[None],
        gain_rows[1],
        jnp.concatenate([query_grad, late_grad], axis=1),
        early_grad[:shard],
        gain_rows[0],
        jnp.concatenate([gelu_grad[:, :true_width], gate_grad[:, :true_width]], axis=1),
        contract_grad[:, :true_width],
    )


def solution(mesh):
    in_specs = (
        P(("replica", "fsdp"), "ctx", None),
        P(("fsdp", "ctx")),
        P(("fsdp", "ctx"), None),
        P(("fsdp", "ctx"), None),
        P(("fsdp", "ctx")),
        P(("fsdp", "ctx"), None),
        P(("fsdp", "ctx"), None),
        P(("replica", "fsdp"), "ctx"),
        P(("replica", "fsdp"), "ctx", None),
        P(("replica", "fsdp"), "ctx", None),
    )
    out_specs = (
        P(("replica", "fsdp"), "ctx", None),
        P(("replica", "fsdp"), "ctx", None),
        P(("fsdp", "ctx")),
        P(("fsdp", "ctx"), None),
        P(("fsdp", "ctx"), None),
        P(("fsdp", "ctx")),
        P(("fsdp", "ctx"), None),
        P(("fsdp", "ctx"), None),
    )
    sizes = (mesh.shape["replica"], mesh.shape["fsdp"], mesh.shape["ctx"])
    body = body_plane if sizes == (4, 4, 2) else body_generic
    return jax.shard_map(body, mesh=mesh, in_specs=in_specs, out_specs=out_specs, check_vma=False)
```

```python
import math

import jax
import jax.numpy as jnp
from jax import lax
from jax.experimental import pallas as pl
from jax.experimental.pallas import tpu as pltpu
from jax.sharding import PartitionSpec as P

HEAD_DIM = 64
HALF = 64


EPS = 1e-05
THETA = 10000.0


def extended_2(cells, sides, width):
    for axis, dim in sides:
        count = lax.axis_size(axis)
        ends = count - 1
        head = lax.slice_in_dim(cells, 0, width, axis=dim)
        tail = lax.slice_in_dim(cells, cells.shape[dim] - width, cells.shape[dim], axis=dim)
        cells = jnp.concatenate(
            [
                lax.ppermute(tail, axis, [(i, (i + 1) % count) for i in range(ends)]),
                cells,
                lax.ppermute(head, axis, [((i + 1) % count, i) for i in range(ends)]),
            ],
            axis=dim,
        )
    return cells


def from_behind(value, axis, steps):
    count = lax.axis_size(axis)
    first, last = (max(0, -steps), min(count, count - steps))
    return lax.ppermute(value, axis, [(source, source + steps) for source in range(first, last)])


def layer_norm(values, gain):
    center = values - jnp.mean(values, axis=-1, keepdims=True)
    variance = jnp.mean(center * center, axis=-1, keepdims=True)
    scaled = lax.rsqrt(variance + EPS)
    normed = center * scaled
    return (normed, scaled, (normed * gain.astype(jnp.float32)).astype(jnp.bfloat16))


def layer_norm_back(incoming, normed, scaled, gain):
    weighted = incoming * gain.astype(jnp.float32)
    gain_grad = jnp.sum(incoming * normed, axis=0)
    mean_one = jnp.mean(weighted, axis=-1, keepdims=True)
    mean_two = jnp.mean(weighted * normed, axis=-1, keepdims=True)
    return (scaled * (weighted - mean_one - normed * mean_two), gain_grad)


def rope_tables(positions, head_size):
    half_dim = head_size // 2
    exponent = jnp.arange(half_dim, dtype=jnp.float32) * (2.0 / head_size)
    frequency = jnp.exp(-math.log(THETA) * exponent)
    angles = positions.astype(jnp.float32)[:, None] * frequency[None, :]
    return (jnp.cos(angles)[:, None, :], jnp.sin(angles)[:, None, :])


def rotate(values, cosine, sine):
    half_dim = values.shape[-1] // 2
    lower_half, upper_half = (values[..., :half_dim], values[..., half_dim:])
    return jnp.concatenate(
        [lower_half * cosine - upper_half * sine, upper_half * cosine + lower_half * sine], axis=-1
    )


def rotate_back(values, cosine, sine):
    half_dim = values.shape[-1] // 2
    lower_half, upper_half = (values[..., :half_dim], values[..., half_dim:])
    return jnp.concatenate(
        [lower_half * cosine + upper_half * sine, upper_half * cosine - lower_half * sine], axis=-1
    )


def gelu_slope(values):
    cdf_part = 0.5 * (1.0 + jax.scipy.special.erf(values * (1.0 / math.sqrt(2.0))))
    density = jnp.exp(-0.5 * values * values) * (1.0 / math.sqrt(2.0 * math.pi))
    return cdf_part + values * density


def block_scores(queries, key_rows, additive):
    factor = 1.0 / math.sqrt(queries.shape[-1])
    scores = jnp.einsum("qhd,khd->hqk", queries, key_rows, preferred_element_type=jnp.float32)
    return scores * factor + additive[None]


def attend(queries, key_rows, value_rows, additive):
    scores = block_scores(queries, key_rows, additive)
    row_peak = jnp.max(scores, axis=-1, keepdims=True)
    exponent = jnp.exp(scores - row_peak)
    row_total = jnp.sum(exponent, axis=-1, keepdims=True)
    soft_weights = (exponent / row_total).astype(jnp.bfloat16)
    mixed = jnp.einsum("hqk,khd->qhd", soft_weights, value_rows, preferred_element_type=jnp.float32)
    return (mixed.astype(jnp.bfloat16), row_peak[..., 0] + jnp.log(row_total[..., 0]))


def attend_back(queries, key_rows, value_rows, additive, log_total, d_mixed):
    factor = 1.0 / math.sqrt(queries.shape[-1])
    scores = block_scores(queries, key_rows, additive)
    recomputed = jnp.exp(scores - log_total[..., None])
    d_soft = jnp.einsum("qhd,khd->hqk", d_mixed, value_rows, preferred_element_type=jnp.float32)
    center = jnp.sum(recomputed * d_soft, axis=-1, keepdims=True)
    d_scores = (recomputed * (d_soft - center) * factor).astype(jnp.bfloat16)
    d_queries = jnp.einsum("hqk,khd->qhd", d_scores, key_rows, preferred_element_type=jnp.float32)
    d_keys = jnp.einsum("hqk,qhd->khd", d_scores, queries, preferred_element_type=jnp.float32)
    d_values = jnp.einsum(
        "hqk,qhd->khd", recomputed.astype(jnp.bfloat16), d_mixed, preferred_element_type=jnp.float32
    )
    return (d_queries, d_keys, d_values)


def body_generic(
    tokens,
    input_gain,
    qkv_weight,
    output_weight,
    mlp_gain,
    expand_weight,
    contract_weight,
    positions,
    mask_bias,
    cotangent,
):
    gathered = (
        lax.all_gather(input_gain, ("fsdp", "ctx"), axis=0, tiled=True),
        lax.all_gather(qkv_weight, ("fsdp", "ctx"), axis=0, tiled=True),
        lax.all_gather(output_weight, ("fsdp", "ctx"), axis=0, tiled=True),
        lax.all_gather(mlp_gain, ("fsdp", "ctx"), axis=0, tiled=True),
        lax.all_gather(expand_weight, ("fsdp", "ctx"), axis=0, tiled=True),
        lax.all_gather(contract_weight, ("fsdp", "ctx"), axis=0, tiled=True),
    )
    full_input_gain, full_qkv, full_output, full_mlp_gain, full_expand, full_contract = gathered
    residual = tokens[0].astype(jnp.float32)
    row_count, model_width = residual.shape
    head_count = model_width // HEAD_DIM
    cosine, sine = rope_tables(positions[0], HEAD_DIM)
    normed1, scaled1, xn1 = layer_norm(residual, full_input_gain)
    projected = jnp.dot(xn1, full_qkv, preferred_element_type=jnp.float32).reshape(
        row_count, 3, head_count, HEAD_DIM
    )
    queries = rotate(projected[:, 0], cosine, sine).astype(jnp.bfloat16)
    key_rows = rotate(projected[:, 1], cosine, sine).astype(jnp.bfloat16)
    value_rows = projected[:, 2].astype(jnp.bfloat16)
    packed = jnp.concatenate(
        [key_rows.reshape(row_count, model_width), value_rows.reshape(row_count, model_width)],
        axis=1,
    )
    extended = extended_2(packed, (("ctx", 0),), HALF)
    extent = extended.shape[0]
    key_ext = extended[:, :model_width].reshape(extent, head_count, HEAD_DIM)
    value_ext = extended[:, model_width:].reshape(extent, head_count, HEAD_DIM)
    additive = mask_bias[0]
    mixed, log_total = attend(queries, key_ext, value_ext, additive)
    attention = mixed.reshape(row_count, model_width)
    hidden = residual + jnp.dot(attention, full_output, preferred_element_type=jnp.float32)
    normed2, scaled2, xn2 = layer_norm(hidden, full_mlp_gain)
    lifted = jnp.dot(xn2, full_expand, preferred_element_type=jnp.float32)
    ff_width = lifted.shape[1] // 2
    gelu_input = lifted[:, :ff_width]
    gate_part = lifted[:, ff_width:]
    activated = jax.nn.gelu(gelu_input, approximate=False)
    gated = (activated * gate_part).astype(jnp.bfloat16)
    down_out = jnp.einsum("tf,jf->tj", gated, full_contract, preferred_element_type=jnp.float32)
    layer_out = (hidden + down_out).astype(jnp.bfloat16)
    back_input_gain, back_qkv, back_output, back_mlp_gain, back_expand, back_contract = gathered
    grad_out = cotangent[0]
    d_gated = jnp.dot(grad_out, back_contract, preferred_element_type=jnp.float32)
    d_lifted = jnp.concatenate(
        [d_gated * gate_part * gelu_slope(gelu_input), d_gated * activated], axis=1
    ).astype(jnp.bfloat16)
    d_xn2 = jnp.einsum("tc,dc->td", d_lifted, back_expand, preferred_element_type=jnp.float32)
    d_norm2, mlp_gain_term = layer_norm_back(d_xn2, normed2, scaled2, back_mlp_gain)
    d_hidden = grad_out.astype(jnp.float32) + d_norm2
    d_proj = d_hidden.astype(jnp.bfloat16)
    d_attention = jnp.einsum(
        "tj,ij->ti", d_proj, back_output, preferred_element_type=jnp.float32
    ).astype(jnp.bfloat16)
    d_queries, d_key_ext, d_value_ext = attend_back(
        queries,
        key_ext,
        value_ext,
        additive,
        log_total,
        d_attention.reshape(row_count, head_count, HEAD_DIM),
    )
    grad_ext = jnp.concatenate(
        [d_key_ext.reshape(extent, model_width), d_value_ext.reshape(extent, model_width)], axis=1
    )
    from_next = from_behind(grad_ext[:HALF], "ctx", -1)
    from_prev = from_behind(grad_ext[row_count + HALF :], "ctx", 1)
    grad_kv = grad_ext[HALF : HALF + row_count]
    grad_kv = grad_kv + jnp.pad(from_prev, ((0, row_count - HALF), (0, 0)))
    grad_kv = grad_kv + jnp.pad(from_next, ((row_count - HALF, 0), (0, 0)))
    d_keys = rotate_back(
        grad_kv[:, :model_width].reshape(row_count, head_count, HEAD_DIM), cosine, sine
    )
    d_values = grad_kv[:, model_width:]
    d_queries = rotate_back(d_queries, cosine, sine)
    d_projected = jnp.concatenate(
        [
            d_queries.reshape(row_count, model_width),
            d_keys.reshape(row_count, model_width),
            d_values,
        ],
        axis=1,
    ).astype(jnp.bfloat16)
    d_xn1 = jnp.einsum("tc,dc->td", d_projected, back_qkv, preferred_element_type=jnp.float32)
    d_norm1, input_gain_term = layer_norm_back(d_xn1, normed1, scaled1, back_input_gain)
    input_grad = (d_hidden + d_norm1).astype(jnp.bfloat16)
    left_one, left_two, left_three, left_four = (xn1, attention, xn2, grad_out)
    gain_one, gain_two = (input_gain_term, mlp_gain_term)
    qkv_term = jnp.einsum("ti,tj->ij", left_one, d_projected, preferred_element_type=jnp.float32)
    output_term = jnp.einsum("ti,tj->ij", left_two, d_proj, preferred_element_type=jnp.float32)
    expand_term = jnp.einsum("ti,tj->ij", left_three, d_lifted, preferred_element_type=jnp.float32)
    contract_term = jnp.einsum("ti,tj->ij", left_four, gated, preferred_element_type=jnp.float32)
    first_gain = gain_one[:, None]
    second_gain = gain_two[:, None]
    shares = lax.psum_scatter(
        jnp.concatenate(
            [qkv_term, output_term, expand_term, contract_term, first_gain, second_gain], axis=1
        ),
        ("fsdp", "ctx"),
        scatter_dimension=0,
        tiled=True,
    )
    result = lax.psum(shares, "replica")
    qkv_cols = 3 * model_width
    expand_cols = 2 * ff_width
    qkv_grad = result[:, :qkv_cols]
    output_grad = result[:, qkv_cols : qkv_cols + model_width]
    offset = qkv_cols + model_width
    expand_grad = result[:, offset : offset + expand_cols]
    offset = offset + expand_cols
    contract_grad = result[:, offset : offset + ff_width]
    offset = offset + ff_width
    input_gain_grad = result[:, offset]
    mlp_gain_grad = result[:, offset + 1]
    return (
        layer_out[None],
        input_grad[None],
        input_gain_grad,
        qkv_grad,
        output_grad,
        mlp_gain_grad,
        expand_grad,
        contract_grad,
    )


X_BIT, CORE_BIT, Y_BIT = (1, 2, 4)
PLANE = ("fsdp", "ctx")
PLANE_SIZE = 8
PIECES = 10
VMEM_BYTES = 50 * 1024 * 1024
F32, BF16 = (jnp.float32, jnp.bfloat16)


def swap(value, bit):
    return lax.ppermute(value, PLANE, [(i, i ^ bit) for i in range(PLANE_SIZE)])


def later(value, *others):
    return lax.optimization_barrier((value, others))[0]


def fetch_pieces(own, after=()):
    own = later(own, after)
    half = own.shape[0] // 2
    over_x = swap(own, X_BIT)
    over_y = swap(own, Y_BIT)
    return [own, over_x, over_y, swap(over_x[:half], Y_BIT), swap(over_y[half:], X_BIT)]


def share_pieces(first, after=()):
    corners = [swap(later(part, after), CORE_BIT) for part in first[3:]]
    return first + [swap(part, CORE_BIT) for part in first[:3]] + corners


def fill(pieces, target, sems, me, columns=None):
    shard = target.shape[0] // PLANE_SIZE
    half = shard // 2
    corner = X_BIT | Y_BIT
    places = [(0, 0, shard), (X_BIT, 0, shard), (Y_BIT, 0, shard), (corner, 0, half), (corner, half, half)]
    places = places + [(offset | CORE_BIT, start, rows) for offset, start, rows in places]
    copies = []
    for index, (piece, (offset, start, rows)) in enumerate(zip(pieces, places)):
        row = pl.multiple_of((me ^ offset) * shard + start, half)
        source = piece if columns is None else piece.at[:, columns]
        copies.append(pltpu.make_async_copy(source, target.at[pl.ds(row, rows)], sems.at[index]))
    for copy in copies:
        copy.start()
    return copies


def wait_all(copies):
    for copy in copies:
        copy.wait()


def pack(keep, send, left, right, gather_bit, sum_bit, me):
    rows, width = (left.shape[0], left.shape[1] // PLANE_SIZE)
    for slot, offset in enumerate([0, CORE_BIT, sum_bit, CORE_BIT | sum_bit]):
        for target, flip in ((keep, 0), (send, gather_bit)):
            source = pl.multiple_of((me ^ (offset | flip)) * width, width)
            target[:rows, slot * width : (slot + 1) * width] = left[:, pl.ds(source, width)]
    keep[:rows, 4 * width :] = right
    send[:rows, 4 * width :] = right


def turn(values, cosine, sine):
    lane = lax.broadcasted_iota(jnp.int32, values.shape, 1)
    low = lane % HEAD_DIM < HEAD_DIM // 2
    other = jnp.where(
        low,
        pltpu.roll(values, values.shape[1] - HEAD_DIM // 2, 1),
        pltpu.roll(values, HEAD_DIM // 2, 1),
    )
    return values * cosine + other * sine


def dot_tt(one, two):
    return lax.dot_general(one, two, (((0,), (0,)), ((), ())), preferred_element_type=F32)


def dot_nt(one, two):
    return lax.dot_general(one, two, (((1,), (1,)), ((), ())), preferred_element_type=F32)


def dot_nn(one, two):
    return jnp.dot(one, two, preferred_element_type=F32)


def norm_parts(values):
    center = values - jnp.mean(values, axis=-1, keepdims=True)
    variance = jnp.mean(center * center, axis=-1, keepdims=True)
    scaled = lax.rsqrt(variance + EPS)
    return (center * scaled, scaled)


def norm_back(incoming, normed, scaled, gain):
    weighted = incoming * gain
    gain_grad = jnp.sum(incoming * normed, axis=0, keepdims=True)
    mean_one = jnp.mean(weighted, axis=-1, keepdims=True)
    mean_two = jnp.mean(weighted * normed, axis=-1, keepdims=True)
    return (scaled * (weighted - mean_one - normed * mean_two), gain_grad)


def front_kernel(place, tokens, cosine, sine, *refs):
    pieces, (queries, keys_values, edge, xn1, gains, weight, sems) = (refs[:PIECES], refs[PIECES:])
    me, along = (place[0], place[1])
    copies = fill(pieces, weight, sems, me)
    normed, _ = norm_parts(tokens[...].astype(F32))
    width = tokens.shape[1]
    wait_all(copies)
    turned = weight[:, 4 * width :].astype(F32).T
    gains[...] = turned[: gains.shape[0]]
    rounded = (normed * gains[0:1, :]).astype(BF16)
    xn1[...] = rounded
    pair = cosine.shape[1]
    projected = dot_nn(rounded, weight[:, : 3 * width])
    for start in range(0, width, pair):
        part = projected[:, start : start + pair]
        queries[:, start : start + pair] = turn(part, cosine[...], sine[...]).astype(BF16)
        part = projected[:, width + start : width + start + pair]
        keys_values[:, start : start + pair] = turn(part, cosine[...], sine[...]).astype(BF16)
    keys_values[:, width:] = projected[:, 2 * width :].astype(BF16)
    rows = edge.shape[0]
    edge[...] = keys_values[pl.ds(pl.multiple_of((1 - along) * rows, rows), rows), :]


def head_masks(shape):
    lane = lax.broadcasted_iota(jnp.int32, shape, 1)
    return lane < HEAD_DIM


def attend_kernel(place, queries, keys_values, edge, bias, tokens, gains, *refs):
    pieces, (attention, totals, hidden, xn2, weight, sems) = (refs[:PIECES], refs[PIECES:])
    width = tokens.shape[1]
    copies = fill(pieces, weight, sems, place[0], pl.ds(3 * width, width))
    pair = 2 * HEAD_DIM
    factor = 1.0 / math.sqrt(HEAD_DIM)
    rows = queries.shape[0]
    is_first = head_masks((rows, pair))
    lane = lax.broadcasted_iota(jnp.int32, totals.shape, 1)
    logs = jnp.zeros(totals.shape, F32)
    for start in range(0, width, pair):
        two = queries[:, start : start + pair]
        keys = jnp.concatenate([keys_values[:, start : start + pair], edge[:, start : start + pair]], axis=0)
        vals = jnp.concatenate(
            [keys_values[:, width + start : width + start + pair], edge[:, width + start : width + start + pair]],
            axis=0,
        )
        outs = []
        for which in range(2):
            mask = is_first if which == 0 else jnp.logical_not(is_first)
            one = jnp.where(mask, two, jnp.zeros_like(two))
            scores = dot_nt(one, keys) * factor + bias[...]
            peak = jnp.max(scores, axis=-1, keepdims=True)
            exponent = jnp.exp(scores - peak)
            total = jnp.sum(exponent, axis=-1, keepdims=True)
            soft = (exponent / total).astype(BF16)
            outs.append(dot_nn(soft, vals))
            logs = jnp.where(lane == 2 * (start // pair) + which, peak + jnp.log(total), logs)
        attention[:, start : start + pair] = jnp.where(is_first, outs[0], outs[1]).astype(BF16)
    totals[...] = logs
    wait_all(copies)
    result = tokens[...].astype(F32) + dot_nn(attention[...], weight[...])
    hidden[...] = result
    normed, _ = norm_parts(result)
    xn2[...] = (normed * gains[1:2, :]).astype(BF16)


def lift_kernel(place, xn2, grad_out, *refs):
    pieces, rest = (refs[:PIECES], refs[PIECES:])
    keep_one, send_one, keep_two, send_two, slope_gate, active, weight, sems = rest
    me = place[0]
    cols = active.shape[1]
    wait_all(fill(pieces, weight, sems, me, pl.ds(0, 2 * cols)))
    gelu_input = dot_nn(xn2[...], weight[:, :cols])
    gate_part = dot_nn(xn2[...], weight[:, cols:])
    cdf_part = 0.5 * (1.0 + lax.erf(gelu_input * (1.0 / math.sqrt(2.0))))
    density = jnp.exp(-0.5 * gelu_input * gelu_input) * (1.0 / math.sqrt(2.0 * math.pi))
    activated = gelu_input * cdf_part
    active[...] = activated
    slope_gate[...] = gate_part * (cdf_part + gelu_input * density)
    gated = (activated * gate_part).astype(BF16)
    cut = keep_one.shape[1] - xn2.shape[1] // 2
    pack(keep_one, send_one, grad_out, gated[:, :cut], X_BIT, Y_BIT, me)
    pack(keep_two, send_two, grad_out, gated[:, cut:], Y_BIT, X_BIT, me)


def contract_kernel(place, gated_one, gated_two, grad_out, xn2, hidden, slope_gate, active, *refs):
    pieces, rest = (refs[:PIECES], refs[PIECES:])
    layer_out, keep_one, send_one, keep_two, send_two, weight, sems = rest
    me = place[0]
    cols = weight.shape[1]
    wait_all(fill(pieces, weight, sems, me, pl.ds(2 * cols, cols)))
    d_gated = dot_nn(grad_out[...], weight[...])
    pack(keep_one, send_one, xn2, (d_gated * slope_gate[...]).astype(BF16), Y_BIT, X_BIT, me)
    pack(keep_two, send_two, xn2, (d_gated * active[...]).astype(BF16), X_BIT, Y_BIT, me)
    skip = xn2.shape[1] // 2
    cut = gated_one.shape[1] - skip
    down = dot_nt(gated_one[:, skip:], weight[:, :cut]) + dot_nt(gated_two[:, skip:], weight[:, cut:])
    layer_out[...] = (hidden[...] + down).astype(BF16)


def hidden_back_kernel(place, pack_one, pack_two, grad_out, hidden, gains, *refs):
    first, third = (refs[:PIECES], refs[PIECES : 2 * PIECES])
    d_hidden, d_attention, gain_grad, lift_weight, weight, sems, sems_three = refs[2 * PIECES :]
    me = place[0]
    width = hidden.shape[1]
    copies = fill(first, lift_weight, sems, me, pl.ds(0, lift_weight.shape[1]))
    lasts = fill(third, weight, sems_three, me, pl.ds(3 * width, width))
    normed, scaled = norm_parts(hidden[...])
    wait_all(copies)
    cols = lift_weight.shape[1] // 2
    d_xn2 = dot_nt(pack_one[:, width // 2 :], lift_weight[:, :cols])
    d_xn2 = d_xn2 + dot_nt(pack_two[:, width // 2 :], lift_weight[:, cols:])
    d_norm, gain_term = norm_back(d_xn2, normed, scaled, gains[1:2, :])
    gain_grad[...] = gain_term
    total = grad_out[...].astype(F32) + d_norm
    d_hidden[...] = total
    rounded = total.astype(BF16)
    wait_all(lasts)
    d_attention[...] = dot_nt(rounded, weight[...]).astype(BF16)


def attend_back_kernel(
    place, queries, keys_values, edge, bias, totals, d_attention, cosine, sine, d_turned, d_keys_values, d_edge
):
    width = queries.shape[1]
    pair = 2 * HEAD_DIM
    factor = 1.0 / math.sqrt(HEAD_DIM)
    rows = queries.shape[0]
    is_first = head_masks((rows, pair))
    is_first_key = head_masks((rows + edge.shape[0], pair))
    for start in range(0, width, pair):
        here = slice(start, start + pair)
        there = slice(width + start, width + start + pair)
        two = queries[:, here]
        d_two = d_attention[:, here]
        keys = jnp.concatenate([keys_values[:, here], edge[:, here]], axis=0)
        vals = jnp.concatenate([keys_values[:, there], edge[:, there]], axis=0)
        d_queries, d_keys, d_vals = ([], [], [])
        for which in range(2):
            mask = is_first if which == 0 else jnp.logical_not(is_first)
            one = jnp.where(mask, two, jnp.zeros_like(two))
            d_one = jnp.where(mask, d_two, jnp.zeros_like(d_two))
            head = 2 * (start // pair) + which
            scores = dot_nt(one, keys) * factor + bias[...]
            recomputed = jnp.exp(scores - totals[:, head : head + 1])
            d_soft = dot_nt(d_one, vals)
            center = jnp.sum(recomputed * d_soft, axis=-1, keepdims=True)
            d_scores = (recomputed * (d_soft - center) * factor).astype(BF16)
            d_queries.append(dot_nn(d_scores, keys))
            d_keys.append(dot_tt(d_scores, two))
            d_vals.append(dot_tt(recomputed.astype(BF16), d_two))
        d_query = jnp.where(is_first, d_queries[0], d_queries[1])
        d_turned[:, here] = turn(d_query, cosine[...], -sine[...]).astype(BF16)
        d_key = jnp.where(is_first_key, d_keys[0], d_keys[1])
        d_val = jnp.where(is_first_key, d_vals[0], d_vals[1])
        d_keys_values[:, here] = d_key[:rows]
        d_keys_values[:, there] = d_val[:rows]
        d_edge[:, here] = d_key[rows:].astype(BF16)
        d_edge[:, there] = d_val[rows:].astype(BF16)


def keys_back_kernel(
    place, d_queries, d_keys_values, arrived, cosine, sine, xn1, keep_one, send_one, keep_two, send_two, summed, d_turned
):
    me, along = (place[0], place[1])
    width = xn1.shape[1]
    pair = 2 * HEAD_DIM
    rows = arrived.shape[0]
    summed[...] = d_keys_values[...]
    where = pl.ds(pl.multiple_of((1 - along) * rows, rows), rows)
    summed[where, :] = summed[where, :] + arrived[...].astype(F32)
    for start in range(0, width, pair):
        here = slice(start, start + pair)
        there = slice(width + start, width + start + pair)
        d_turned[:, there] = turn(summed[:, here], cosine[...], -sine[...]).astype(BF16)
    d_turned[:, :width] = d_queries[...]
    d_turned[:, 2 * width :] = summed[:, width:].astype(BF16)
    middle = d_turned.shape[1] // 2
    pack(keep_one, send_one, xn1, d_turned[:, :middle], X_BIT, Y_BIT, me)
    pack(keep_two, send_two, xn1, d_turned[:, middle:], Y_BIT, X_BIT, me)


def tokens_back_kernel(place, pack_one, pack_two, tokens, attention, d_hidden, gains, mlp_term, *refs):
    pieces, (keep, send, input_grad, weight, sems) = (refs[:PIECES], refs[PIECES:])
    rows = tokens.shape[0]
    width = tokens.shape[1]
    copies = fill(pieces, weight, sems, place[0], pl.ds(0, 3 * width))
    normed, scaled = norm_parts(tokens[...].astype(F32))
    wait_all(copies)
    middle = pack_one.shape[1] - width // 2
    d_xn1 = dot_nt(pack_one[:, width // 2 :], weight[:, :middle])
    d_xn1 = d_xn1 + dot_nt(pack_two[:, width // 2 :], weight[:, middle:])
    d_norm, gain_term = norm_back(d_xn1, normed, scaled, gains[0:1, :])
    pack(keep, send, attention, d_hidden[...].astype(BF16), Y_BIT, X_BIT, place[0])
    extra = keep.shape[0] - rows
    line = lax.broadcasted_iota(jnp.int32, (extra, width), 0)
    terms = jnp.where(line == 0, mlp_term[...], jnp.where(line == 1, gain_term, 0.0)).astype(BF16)
    for target in (keep, send):
        target[rows:, : width // 2] = jnp.zeros((extra, width // 2), BF16)
        target[rows:, width // 2 :] = terms
    input_grad[...] = (d_hidden[...] + d_norm).astype(BF16)


def product_kernel(width, rows, chip, other, own, sent, joined, *refs):
    terms, sems = (refs[0] if len(refs) > 1 else None, refs[-1])
    copies = []
    extra = 0 if terms is None else terms.shape[1]
    for index in range(4):
        part, start = ((chip, other)[index // 2], index % 2 * (rows + extra))
        source = part.at[pl.ds(start, rows)]
        copies.append(pltpu.make_async_copy(source, joined.at[pl.ds(index * rows, rows)], sems.at[index]))
        if terms is not None:
            copies.append(
                pltpu.make_async_copy(part.at[pl.ds(start + rows, extra)], terms.at[index], sems.at[4 + index])
            )
    for copy in copies:
        copy.start()
    wait_all(copies)
    block = lambda top, k: joined[2 * rows * top : 2 * rows * (top + 1), k * width : (k + 1) * width]
    right = joined[:, 4 * width :]
    left = jnp.concatenate([block(0, 2), block(1, 3)], axis=0)
    sent[:width] = dot_tt(left, right).astype(BF16)
    left = jnp.concatenate([block(0, 0), block(1, 1)], axis=0)
    own[:width] = dot_tt(left, right)
    if terms is not None:
        total = sum(terms[index, :, 4 * width :].astype(F32) for index in range(4))
        own[width:] = total
        sent[width:] = total.astype(BF16)


def call(kernel, outs, operands, scratch=(), smem=1, anywhere=(), flops=0, size=0):
    specs = []
    for index in range(len(operands)):
        if index < smem:
            specs.append(pl.BlockSpec(memory_space=pltpu.SMEM))
        elif index in anywhere:
            specs.append(pl.BlockSpec(memory_space=pltpu.HBM))
        else:
            specs.append(pl.BlockSpec(memory_space=pltpu.VMEM))
    return pl.pallas_call(
        kernel,
        out_shape=[jax.ShapeDtypeStruct(shape, kind) for shape, kind in outs],
        in_specs=specs,
        out_specs=[pl.BlockSpec(memory_space=pltpu.VMEM)] * len(outs),
        scratch_shapes=list(scratch),
        cost_estimate=pl.CostEstimate(flops=flops, bytes_accessed=size, transcendentals=0),
        compiler_params=pltpu.CompilerParams(vmem_limit_bytes=VMEM_BYTES),
    )(*operands)


def grad_rows(keep, over_link, width, before=(), after=()):
    return products(share(keep, over_link, before), width, after)


def share(keep, over_link, before=()):
    return jnp.concatenate(later([keep, over_link], before), axis=0)


def products(chip, width, after=()):
    rows = chip.shape[0] // 256 * 128
    extra = chip.shape[0] // 2 - rows
    cols = chip.shape[1] - 4 * width
    other = later(swap(chip, CORE_BIT), after)
    scratch = [pltpu.VMEM((4 * rows, 4 * width + cols), BF16)]
    if extra:
        scratch.append(pltpu.VMEM((4, extra, 4 * width + cols), BF16))
    return call(
        lambda *refs: product_kernel(width, rows, *refs),
        [((width + extra, cols), F32), ((width + extra, cols), BF16)],
        [chip, other],
        scratch + [pltpu.SemaphoreType.DMA((8,))],
        smem=0,
        anywhere=(0, 1),
        flops=16 * rows * width * cols,
        size=4 * rows * (4 * width + cols) * 2 + 6 * width * cols,
    )


def line_first(part):
    return lax.ppermute(part.astype(BF16), "replica", [(0, 1), (3, 2)])


def line_pair(part, first):
    return (part + first.astype(F32)).astype(BF16)


def line_middle(pair):
    return lax.ppermute(pair, "replica", [(1, 2), (2, 1)])


def line_total(pair, other):
    return (pair.astype(F32) + other.astype(F32)).astype(BF16)


def line_back(total):
    return lax.ppermute(total, "replica", [(1, 0), (2, 3)])


def line_end(total, back):
    place = lax.axis_index("replica")
    middle = (place == 1) | (place == 2)
    return jnp.where(middle, total, back).astype(F32)


def body_plane(
    tokens,
    input_gain,
    qkv_weight,
    output_weight,
    mlp_gain,
    expand_weight,
    contract_weight,
    positions,
    mask_bias,
    cotangent,
):
    me = lax.axis_index(PLANE)
    along = lax.axis_index("ctx")
    place = jnp.stack([me, along]).astype(jnp.int32)
    shard = qkv_weight.shape[0]
    true_width = expand_weight.shape[1] // 2
    fill_cols = -true_width % 128
    ff_width = true_width + fill_cols
    source, grad_out = (tokens[0], cotangent[0])
    rows, width = source.shape
    gains = jnp.stack([input_gain, mlp_gain], axis=1)
    gains = jnp.pad(gains, ((0, 0), (0, 126)))
    front = jnp.concatenate([qkv_weight, output_weight, gains], axis=1)
    widened = lambda values: jnp.pad(values, ((0, 0), (0, fill_cols)))
    feed = jnp.concatenate(
        [
            widened(expand_weight[:, :true_width]),
            widened(expand_weight[:, true_width:]),
            widened(contract_weight),
        ],
        axis=1,
    )
    fetched = fetch_pieces(front)
    packed = share_pieces(fetched)
    feed_fetched = fetch_pieces(feed, tuple(fetched[3:]))
    cosine, sine = rope_tables(positions[0], HEAD_DIM)
    cosine = jnp.concatenate([cosine[:, 0]] * 4, axis=1)
    sine = jnp.concatenate([-sine[:, 0], sine[:, 0]] * 2, axis=1)
    bias = mask_bias[0]
    bias = jnp.concatenate(
        [bias[:, HALF : HALF + rows], jnp.where(along == 0, bias[:, HALF + rows :], bias[:, :HALF])], axis=1
    )
    sems = pltpu.SemaphoreType.DMA((PIECES,))
    front_cols = front.shape[1]
    queries, keys_values, edge, xn1, full_gains = call(
        front_kernel,
        [((rows, width), BF16), ((rows, 2 * width), BF16), ((HALF, 2 * width), BF16), ((rows, width), BF16), ((8, width), F32)],
        [place, source, cosine, sine] + packed,
        [pltpu.VMEM((width, front_cols), BF16), sems],
        anywhere=range(4, 4 + PIECES),
        flops=6 * rows * width * width,
        size=2 * width * front_cols,
    )
    edge = swap(edge, X_BIT)
    attention, totals, hidden, xn2 = call(
        attend_kernel,
        [((rows, width), BF16), ((rows, 128), F32), ((rows, width), F32), ((rows, width), BF16)],
        [place, queries, keys_values, edge, bias, source, full_gains] + packed,
        [pltpu.VMEM((width, width), BF16), sems],
        anywhere=range(7, 7 + PIECES),
        flops=12 * rows * width * width,
        size=4 * width * width,
    )
    feed_pieces = share_pieces(feed_fetched, xn2)
    half = 4 * shard
    cut = -(-ff_width // 256) * 128
    cuts = [((rows, half + cut), BF16)] * 2 + [((rows, half + ff_width - cut), BF16)] * 2
    keep_c, send_c, keep_d, send_d, slope_gate, active = call(
        lift_kernel,
        cuts + [((rows, ff_width), F32)] * 2,
        [place, xn2, grad_out] + feed_pieces,
        [pltpu.VMEM((width, 2 * ff_width), BF16), sems],
        anywhere=range(3, 3 + PIECES),
        flops=4 * rows * width * ff_width,
        size=4 * width * ff_width,
    )
    layer_out, keep_g, send_g, keep_u, send_u = call(
        contract_kernel,
        [((rows, width), BF16)] + [((rows, half + ff_width), BF16)] * 4,
        [place, keep_c, keep_d, grad_out, xn2, hidden, slope_gate, active] + feed_pieces,
        [pltpu.VMEM((width, ff_width), BF16), sems],
        anywhere=range(8, 8 + PIECES),
        flops=4 * rows * width * ff_width,
        size=2 * width * ff_width,
    )
    d_hidden, d_attention, mlp_term = call(
        hidden_back_kernel,
        [((rows, width), F32), ((rows, width), BF16), ((1, width), F32)],
        [place, keep_g, keep_u, grad_out, hidden, full_gains] + feed_pieces + packed,
        [pltpu.VMEM((width, 2 * ff_width), BF16), pltpu.VMEM((width, width), BF16), sems, sems],
        anywhere=range(6, 6 + 2 * PIECES),
        flops=6 * rows * width * ff_width,
        size=6 * width * ff_width,
    )
    link_c = swap(send_c, X_BIT)
    link_d = swap(send_d, Y_BIT)
    link_g = swap(send_g, Y_BIT)
    link_u = swap(send_u, X_BIT)
    d_queries, d_keys_values, d_edge = call(
        attend_back_kernel,
        [((rows, width), BF16), ((rows, 2 * width), F32), ((HALF, 2 * width), BF16)],
        [place, queries, keys_values, edge, bias, totals, d_attention, cosine, sine],
        flops=20 * rows * width * width,
        size=4 * width * width,
    )
    first_own, first_sent = grad_rows(keep_c, link_c, shard, keep_g, d_edge)
    second_own, second_sent = grad_rows(keep_d, link_d, shard, keep_g, d_edge)
    first_back = swap(first_sent, Y_BIT)
    second_back = swap(second_sent, X_BIT)
    chip_g = share(keep_g, link_g, (first_sent, second_sent))
    chip_u = share(keep_u, link_u, (first_sent, second_sent))
    first_back, second_back = later((first_back, second_back), chip_g, chip_u)
    contract_part = jnp.concatenate(
        [first_own + first_back.astype(F32), second_own + second_back.astype(F32)], axis=1
    )
    contract_first = line_first(contract_part)
    gelu_own, gelu_sent = products(chip_g, shard, contract_part)
    gelu_back = swap(gelu_sent, X_BIT)
    gate_own, gate_sent = products(chip_u, shard, gelu_sent)
    gate_back = swap(gate_sent, Y_BIT)
    d_keys_values = later(d_keys_values, gate_sent)
    keep_kv, send_kv, keep_vk, send_vk = call(
        keys_back_kernel,
        [((rows, half + 3 * width // 2), BF16)] * 4,
        [place, d_queries, d_keys_values, swap(d_edge, X_BIT), cosine, sine, xn1],
        [pltpu.VMEM((rows, 2 * width), F32), pltpu.VMEM((rows, 3 * width), BF16)],
        flops=rows * width,
        size=8 * rows * width,
    )
    link_kv = swap(send_kv, X_BIT)
    link_vk = swap(send_vk, Y_BIT)
    contract_pair = line_pair(contract_part, later(contract_first, keep_kv))
    contract_other = line_middle(contract_pair)
    gelu_part = gelu_own + later(gelu_back, contract_pair).astype(F32)
    gelu_first = line_first(gelu_part)
    gate_part = gate_own + later(gate_back, gelu_part).astype(F32)
    gate_first = line_first(gate_part)
    contract_total = line_total(contract_pair, later(contract_other, gate_part))
    contract_last = line_back(contract_total)
    gelu_pair = line_pair(gelu_part, later(gelu_first, contract_total))
    gelu_other = line_middle(gelu_pair)
    chip_kv = share(keep_kv, link_kv, gelu_pair)
    chip_vk = share(keep_vk, link_vk, gelu_pair)
    d_hidden = later(d_hidden, chip_kv, chip_vk)
    keep_o, send_o, input_grad = call(
        tokens_back_kernel,
        [((rows + 16, half + width), BF16)] * 2 + [((rows, width), BF16)],
        [place, keep_kv, keep_vk, source, attention, d_hidden, full_gains, mlp_term] + packed,
        [pltpu.VMEM((width, 3 * width), BF16), sems],
        anywhere=range(8, 8 + PIECES),
        flops=6 * rows * width * width,
        size=6 * width * width,
    )
    link_o = swap(send_o, Y_BIT)
    low_own, low_sent = products(chip_kv, shard, keep_o)
    low_back = swap(low_sent, Y_BIT)
    high_own, high_sent = products(chip_vk, shard, low_sent)
    high_back = swap(high_sent, X_BIT)
    gate_pair = line_pair(gate_part, later(gate_first, high_sent))
    gate_other = line_middle(gate_pair)
    out_own, out_sent = grad_rows(keep_o, link_o, shard, gate_pair)
    out_back = swap(out_sent, X_BIT)
    low_part = low_own + later(low_back, out_sent).astype(F32)
    low_first = line_first(low_part)
    high_part = high_own + later(high_back, low_part).astype(F32)
    high_first = line_first(high_part)
    gelu_total = line_total(gelu_pair, later(gelu_other, high_part))
    gelu_last = line_back(gelu_total)
    low_pair = line_pair(low_part, later(low_first, gelu_total))
    low_other = line_middle(low_pair)
    out_part = out_own + later(out_back, low_pair).astype(F32)
    out_first = line_first(out_part)
    gate_total = line_total(gate_pair, later(gate_other, out_part))
    gate_last = line_back(gate_total)
    high_pair = line_pair(high_part, later(high_first, gate_total))
    high_other = line_middle(high_pair)
    low_total = line_total(low_pair, later(low_other, high_pair))
    low_last = line_back(low_total)
    out_pair = line_pair(out_part, later(out_first, low_total))
    out_other = line_middle(out_pair)
    high_total = line_total(high_pair, later(high_other, out_pair))
    high_last = line_back(high_total)
    out_total = line_total(out_pair, later(out_other, high_total))
    out_last = line_back(out_total)
    contract_grad = line_end(contract_total, later(contract_last, high_pair))
    gelu_grad = line_end(gelu_total, later(gelu_last, out_total))
    gate_grad = line_end(gate_total, later(gate_last, out_total))
    all_grad = jnp.concatenate([line_end(low_total, low_last), line_end(high_total, high_last)], axis=1)
    out_grad = line_end(out_total, out_last)
    gain_rows = lax.dynamic_slice_in_dim(out_grad[shard : shard + 2], me * shard, shard, axis=1)
    return (
        layer_out[None],
        input_grad[None],
        gain_rows[1],
        all_grad,
        out_grad[:shard],
        gain_rows[0],
        jnp.concatenate([gelu_grad[:, :true_width], gate_grad[:, :true_width]], axis=1),
        contract_grad[:, :true_width],
    )


def solution(mesh):
    in_specs = (
        P(("replica", "fsdp"), "ctx", None),
        P(("fsdp", "ctx")),
        P(("fsdp", "ctx"), None),
        P(("fsdp", "ctx"), None),
        P(("fsdp", "ctx")),
        P(("fsdp", "ctx"), None),
        P(("fsdp", "ctx"), None),
        P(("replica", "fsdp"), "ctx"),
        P(("replica", "fsdp"), "ctx", None),
        P(("replica", "fsdp"), "ctx", None),
    )
    out_specs = (
        P(("replica", "fsdp"), "ctx", None),
        P(("replica", "fsdp"), "ctx", None),
        P(("fsdp", "ctx")),
        P(("fsdp", "ctx"), None),
        P(("fsdp", "ctx"), None),
        P(("fsdp", "ctx")),
        P(("fsdp", "ctx"), None),
        P(("fsdp", "ctx"), None),
    )
    sizes = (mesh.shape["replica"], mesh.shape["fsdp"], mesh.shape["ctx"])
    body = body_plane if sizes == (4, 4, 2) else body_generic
    return jax.shard_map(body, mesh=mesh, in_specs=in_specs, out_specs=out_specs, check_vma=False)
```

```python
import math

import jax
import jax.numpy as jnp
from jax import lax
from jax.experimental import pallas as pl
from jax.experimental.pallas import tpu as pltpu
from jax.sharding import PartitionSpec as P

HEAD_DIM = 64
HALF = 64


EPS = 1e-05
THETA = 10000.0


def extended_2(cells, sides, width):
    for axis, dim in sides:
        count = lax.axis_size(axis)
        ends = count - 1
        head = lax.slice_in_dim(cells, 0, width, axis=dim)
        tail = lax.slice_in_dim(cells, cells.shape[dim] - width, cells.shape[dim], axis=dim)
        cells = jnp.concatenate(
            [
                lax.ppermute(tail, axis, [(i, (i + 1) % count) for i in range(ends)]),
                cells,
                lax.ppermute(head, axis, [((i + 1) % count, i) for i in range(ends)]),
            ],
            axis=dim,
        )
    return cells


def from_behind(value, axis, steps):
    count = lax.axis_size(axis)
    first, last = (max(0, -steps), min(count, count - steps))
    return lax.ppermute(value, axis, [(source, source + steps) for source in range(first, last)])


def layer_norm(values, gain):
    center = values - jnp.mean(values, axis=-1, keepdims=True)
    variance = jnp.mean(center * center, axis=-1, keepdims=True)
    scaled = lax.rsqrt(variance + EPS)
    normed = center * scaled
    return (normed, scaled, (normed * gain.astype(jnp.float32)).astype(jnp.bfloat16))


def layer_norm_back(incoming, normed, scaled, gain):
    weighted = incoming * gain.astype(jnp.float32)
    gain_grad = jnp.sum(incoming * normed, axis=0)
    mean_one = jnp.mean(weighted, axis=-1, keepdims=True)
    mean_two = jnp.mean(weighted * normed, axis=-1, keepdims=True)
    return (scaled * (weighted - mean_one - normed * mean_two), gain_grad)


def rope_tables(positions, head_size):
    half_dim = head_size // 2
    exponent = jnp.arange(half_dim, dtype=jnp.float32) * (2.0 / head_size)
    frequency = jnp.exp(-math.log(THETA) * exponent)
    angles = positions.astype(jnp.float32)[:, None] * frequency[None, :]
    return (jnp.cos(angles)[:, None, :], jnp.sin(angles)[:, None, :])


def rotate(values, cosine, sine):
    half_dim = values.shape[-1] // 2
    lower_half, upper_half = (values[..., :half_dim], values[..., half_dim:])
    return jnp.concatenate(
        [lower_half * cosine - upper_half * sine, upper_half * cosine + lower_half * sine], axis=-1
    )


def rotate_back(values, cosine, sine):
    half_dim = values.shape[-1] // 2
    lower_half, upper_half = (values[..., :half_dim], values[..., half_dim:])
    return jnp.concatenate(
        [lower_half * cosine + upper_half * sine, upper_half * cosine - lower_half * sine], axis=-1
    )


def gelu_slope(values):
    cdf_part = 0.5 * (1.0 + jax.scipy.special.erf(values * (1.0 / math.sqrt(2.0))))
    density = jnp.exp(-0.5 * values * values) * (1.0 / math.sqrt(2.0 * math.pi))
    return cdf_part + values * density


def block_scores(queries, key_rows, additive):
    factor = 1.0 / math.sqrt(queries.shape[-1])
    scores = jnp.einsum("qhd,khd->hqk", queries, key_rows, preferred_element_type=jnp.float32)
    return scores * factor + additive[None]


def attend(queries, key_rows, value_rows, additive):
    scores = block_scores(queries, key_rows, additive)
    row_peak = jnp.max(scores, axis=-1, keepdims=True)
    exponent = jnp.exp(scores - row_peak)
    row_total = jnp.sum(exponent, axis=-1, keepdims=True)
    soft_weights = (exponent / row_total).astype(jnp.bfloat16)
    mixed = jnp.einsum("hqk,khd->qhd", soft_weights, value_rows, preferred_element_type=jnp.float32)
    return (mixed.astype(jnp.bfloat16), row_peak[..., 0] + jnp.log(row_total[..., 0]))


def attend_back(queries, key_rows, value_rows, additive, log_total, d_mixed):
    factor = 1.0 / math.sqrt(queries.shape[-1])
    scores = block_scores(queries, key_rows, additive)
    recomputed = jnp.exp(scores - log_total[..., None])
    d_soft = jnp.einsum("qhd,khd->hqk", d_mixed, value_rows, preferred_element_type=jnp.float32)
    center = jnp.sum(recomputed * d_soft, axis=-1, keepdims=True)
    d_scores = (recomputed * (d_soft - center) * factor).astype(jnp.bfloat16)
    d_queries = jnp.einsum("hqk,khd->qhd", d_scores, key_rows, preferred_element_type=jnp.float32)
    d_keys = jnp.einsum("hqk,qhd->khd", d_scores, queries, preferred_element_type=jnp.float32)
    d_values = jnp.einsum(
        "hqk,qhd->khd", recomputed.astype(jnp.bfloat16), d_mixed, preferred_element_type=jnp.float32
    )
    return (d_queries, d_keys, d_values)


def body_generic(
    tokens,
    input_gain,
    qkv_weight,
    output_weight,
    mlp_gain,
    expand_weight,
    contract_weight,
    positions,
    mask_bias,
    cotangent,
):
    gathered = (
        lax.all_gather(input_gain, ("fsdp", "ctx"), axis=0, tiled=True),
        lax.all_gather(qkv_weight, ("fsdp", "ctx"), axis=0, tiled=True),
        lax.all_gather(output_weight, ("fsdp", "ctx"), axis=0, tiled=True),
        lax.all_gather(mlp_gain, ("fsdp", "ctx"), axis=0, tiled=True),
        lax.all_gather(expand_weight, ("fsdp", "ctx"), axis=0, tiled=True),
        lax.all_gather(contract_weight, ("fsdp", "ctx"), axis=0, tiled=True),
    )
    full_input_gain, full_qkv, full_output, full_mlp_gain, full_expand, full_contract = gathered
    residual = tokens[0].astype(jnp.float32)
    row_count, model_width = residual.shape
    head_count = model_width // HEAD_DIM
    cosine, sine = rope_tables(positions[0], HEAD_DIM)
    normed1, scaled1, xn1 = layer_norm(residual, full_input_gain)
    projected = jnp.dot(xn1, full_qkv, preferred_element_type=jnp.float32).reshape(
        row_count, 3, head_count, HEAD_DIM
    )
    queries = rotate(projected[:, 0], cosine, sine).astype(jnp.bfloat16)
    key_rows = rotate(projected[:, 1], cosine, sine).astype(jnp.bfloat16)
    value_rows = projected[:, 2].astype(jnp.bfloat16)
    packed = jnp.concatenate(
        [key_rows.reshape(row_count, model_width), value_rows.reshape(row_count, model_width)],
        axis=1,
    )
    extended = extended_2(packed, (("ctx", 0),), HALF)
    extent = extended.shape[0]
    key_ext = extended[:, :model_width].reshape(extent, head_count, HEAD_DIM)
    value_ext = extended[:, model_width:].reshape(extent, head_count, HEAD_DIM)
    additive = mask_bias[0]
    mixed, log_total = attend(queries, key_ext, value_ext, additive)
    attention = mixed.reshape(row_count, model_width)
    hidden = residual + jnp.dot(attention, full_output, preferred_element_type=jnp.float32)
    normed2, scaled2, xn2 = layer_norm(hidden, full_mlp_gain)
    lifted = jnp.dot(xn2, full_expand, preferred_element_type=jnp.float32)
    ff_width = lifted.shape[1] // 2
    gelu_input = lifted[:, :ff_width]
    gate_part = lifted[:, ff_width:]
    activated = jax.nn.gelu(gelu_input, approximate=False)
    gated = (activated * gate_part).astype(jnp.bfloat16)
    down_out = jnp.einsum("tf,jf->tj", gated, full_contract, preferred_element_type=jnp.float32)
    layer_out = (hidden + down_out).astype(jnp.bfloat16)
    back_input_gain, back_qkv, back_output, back_mlp_gain, back_expand, back_contract = gathered
    grad_out = cotangent[0]
    d_gated = jnp.dot(grad_out, back_contract, preferred_element_type=jnp.float32)
    d_lifted = jnp.concatenate(
        [d_gated * gate_part * gelu_slope(gelu_input), d_gated * activated], axis=1
    ).astype(jnp.bfloat16)
    d_xn2 = jnp.einsum("tc,dc->td", d_lifted, back_expand, preferred_element_type=jnp.float32)
    d_norm2, mlp_gain_term = layer_norm_back(d_xn2, normed2, scaled2, back_mlp_gain)
    d_hidden = grad_out.astype(jnp.float32) + d_norm2
    d_proj = d_hidden.astype(jnp.bfloat16)
    d_attention = jnp.einsum(
        "tj,ij->ti", d_proj, back_output, preferred_element_type=jnp.float32
    ).astype(jnp.bfloat16)
    d_queries, d_key_ext, d_value_ext = attend_back(
        queries,
        key_ext,
        value_ext,
        additive,
        log_total,
        d_attention.reshape(row_count, head_count, HEAD_DIM),
    )
    grad_ext = jnp.concatenate(
        [d_key_ext.reshape(extent, model_width), d_value_ext.reshape(extent, model_width)], axis=1
    )
    from_next = from_behind(grad_ext[:HALF], "ctx", -1)
    from_prev = from_behind(grad_ext[row_count + HALF :], "ctx", 1)
    grad_kv = grad_ext[HALF : HALF + row_count]
    grad_kv = grad_kv + jnp.pad(from_prev, ((0, row_count - HALF), (0, 0)))
    grad_kv = grad_kv + jnp.pad(from_next, ((row_count - HALF, 0), (0, 0)))
    d_keys = rotate_back(
        grad_kv[:, :model_width].reshape(row_count, head_count, HEAD_DIM), cosine, sine
    )
    d_values = grad_kv[:, model_width:]
    d_queries = rotate_back(d_queries, cosine, sine)
    d_projected = jnp.concatenate(
        [
            d_queries.reshape(row_count, model_width),
            d_keys.reshape(row_count, model_width),
            d_values,
        ],
        axis=1,
    ).astype(jnp.bfloat16)
    d_xn1 = jnp.einsum("tc,dc->td", d_projected, back_qkv, preferred_element_type=jnp.float32)
    d_norm1, input_gain_term = layer_norm_back(d_xn1, normed1, scaled1, back_input_gain)
    input_grad = (d_hidden + d_norm1).astype(jnp.bfloat16)
    left_one, left_two, left_three, left_four = (xn1, attention, xn2, grad_out)
    gain_one, gain_two = (input_gain_term, mlp_gain_term)
    qkv_term = jnp.einsum("ti,tj->ij", left_one, d_projected, preferred_element_type=jnp.float32)
    output_term = jnp.einsum("ti,tj->ij", left_two, d_proj, preferred_element_type=jnp.float32)
    expand_term = jnp.einsum("ti,tj->ij", left_three, d_lifted, preferred_element_type=jnp.float32)
    contract_term = jnp.einsum("ti,tj->ij", left_four, gated, preferred_element_type=jnp.float32)
    first_gain = gain_one[:, None]
    second_gain = gain_two[:, None]
    shares = lax.psum_scatter(
        jnp.concatenate(
            [qkv_term, output_term, expand_term, contract_term, first_gain, second_gain], axis=1
        ),
        ("fsdp", "ctx"),
        scatter_dimension=0,
        tiled=True,
    )
    result = lax.psum(shares, "replica")
    qkv_cols = 3 * model_width
    expand_cols = 2 * ff_width
    qkv_grad = result[:, :qkv_cols]
    output_grad = result[:, qkv_cols : qkv_cols + model_width]
    offset = qkv_cols + model_width
    expand_grad = result[:, offset : offset + expand_cols]
    offset = offset + expand_cols
    contract_grad = result[:, offset : offset + ff_width]
    offset = offset + ff_width
    input_gain_grad = result[:, offset]
    mlp_gain_grad = result[:, offset + 1]
    return (
        layer_out[None],
        input_grad[None],
        input_gain_grad,
        qkv_grad,
        output_grad,
        mlp_gain_grad,
        expand_grad,
        contract_grad,
    )


X_BIT, CORE_BIT, Y_BIT = (1, 2, 4)
PLANE = ("fsdp", "ctx")
PLANE_SIZE = 8
PIECES = 10
VMEM_BYTES = 50 * 1024 * 1024
F32, BF16 = (jnp.float32, jnp.bfloat16)


def swap(value, bit):
    return lax.ppermute(value, PLANE, [(i, i ^ bit) for i in range(PLANE_SIZE)])


def later(value, *others):
    return lax.optimization_barrier((value, others))[0]


def fetch_pieces(own, after=()):
    own = later(own, after)
    half = own.shape[0] // 2
    over_x = swap(own, X_BIT)
    over_y = swap(own, Y_BIT)
    return [own, over_x, over_y, swap(over_x[:half], Y_BIT), swap(over_y[half:], X_BIT)]


def share_pieces(first, after=()):
    corners = [swap(later(part, after), CORE_BIT) for part in first[3:]]
    return first + [swap(part, CORE_BIT) for part in first[:3]] + corners


def fill(pieces, target, sems, me, columns=None):
    shard = target.shape[0] // PLANE_SIZE
    half = shard // 2
    corner = X_BIT | Y_BIT
    places = [(0, 0, shard), (X_BIT, 0, shard), (Y_BIT, 0, shard), (corner, 0, half), (corner, half, half)]
    places = places + [(offset | CORE_BIT, start, rows) for offset, start, rows in places]
    copies = []
    for index, (piece, (offset, start, rows)) in enumerate(zip(pieces, places)):
        row = pl.multiple_of((me ^ offset) * shard + start, half)
        source = piece if columns is None else piece.at[:, columns]
        copies.append(pltpu.make_async_copy(source, target.at[pl.ds(row, rows)], sems.at[index]))
    for copy in copies:
        copy.start()
    return copies


def wait_all(copies):
    for copy in copies:
        copy.wait()


def pack(keep, send, left, right, gather_bit, sum_bit, me):
    rows, width = (left.shape[0], left.shape[1] // PLANE_SIZE)
    for slot, offset in enumerate([0, CORE_BIT, sum_bit, CORE_BIT | sum_bit]):
        for target, flip in ((keep, 0), (send, gather_bit)):
            source = pl.multiple_of((me ^ (offset | flip)) * width, width)
            target[:rows, slot * width : (slot + 1) * width] = left[:, pl.ds(source, width)]
    keep[:rows, 4 * width :] = right
    send[:rows, 4 * width :] = right


def turn(values, cosine, sine):
    lane = lax.broadcasted_iota(jnp.int32, values.shape, 1)
    low = lane % HEAD_DIM < HEAD_DIM // 2
    other = jnp.where(
        low,
        pltpu.roll(values, values.shape[1] - HEAD_DIM // 2, 1),
        pltpu.roll(values, HEAD_DIM // 2, 1),
    )
    return values * cosine + other * sine


def dot_tt(one, two):
    return lax.dot_general(one, two, (((0,), (0,)), ((), ())), preferred_element_type=F32)


def dot_nt(one, two):
    return lax.dot_general(one, two, (((1,), (1,)), ((), ())), preferred_element_type=F32)


def dot_nn(one, two):
    return jnp.dot(one, two, preferred_element_type=F32)


def norm_parts(values):
    center = values - jnp.mean(values, axis=-1, keepdims=True)
    variance = jnp.mean(center * center, axis=-1, keepdims=True)
    scaled = lax.rsqrt(variance + EPS)
    return (center * scaled, scaled)


def norm_back(incoming, normed, scaled, gain):
    weighted = incoming * gain
    gain_grad = jnp.sum(incoming * normed, axis=0, keepdims=True)
    mean_one = jnp.mean(weighted, axis=-1, keepdims=True)
    mean_two = jnp.mean(weighted * normed, axis=-1, keepdims=True)
    return (scaled * (weighted - mean_one - normed * mean_two), gain_grad)


def front_kernel(place, tokens, cosine, sine, *refs):
    pieces, (queries, keys_values, edge, xn1, gains, weight, sems) = (refs[:PIECES], refs[PIECES:])
    me, along = (place[0], place[1])
    copies = fill(pieces, weight, sems, me)
    normed, _ = norm_parts(tokens[...].astype(F32))
    width = tokens.shape[1]
    wait_all(copies)
    turned = weight[:, 4 * width :].astype(F32).T
    gains[...] = turned[: gains.shape[0]]
    rounded = (normed * gains[0:1, :]).astype(BF16)
    xn1[...] = rounded
    pair = cosine.shape[1]
    projected = dot_nn(rounded, weight[:, : 3 * width])
    for start in range(0, width, pair):
        part = projected[:, start : start + pair]
        queries[:, start : start + pair] = turn(part, cosine[...], sine[...]).astype(BF16)
        part = projected[:, width + start : width + start + pair]
        keys_values[:, start : start + pair] = turn(part, cosine[...], sine[...]).astype(BF16)
    keys_values[:, width:] = projected[:, 2 * width :].astype(BF16)
    rows = edge.shape[0]
    edge[...] = keys_values[pl.ds(pl.multiple_of((1 - along) * rows, rows), rows), :]


def head_masks(shape):
    lane = lax.broadcasted_iota(jnp.int32, shape, 1)
    return lane < HEAD_DIM


def attend_kernel(place, queries, keys_values, edge, bias, tokens, gains, *refs):
    pieces, (attention, totals, hidden, xn2, weight, sems) = (refs[:PIECES], refs[PIECES:])
    width = tokens.shape[1]
    copies = fill(pieces, weight, sems, place[0], pl.ds(3 * width, width))
    pair = 2 * HEAD_DIM
    factor = 1.0 / math.sqrt(HEAD_DIM)
    rows = queries.shape[0]
    is_first = head_masks((rows, pair))
    lane = lax.broadcasted_iota(jnp.int32, totals.shape, 1)
    logs = jnp.zeros(totals.shape, F32)
    for start in range(0, width, pair):
        two = queries[:, start : start + pair]
        keys = jnp.concatenate([keys_values[:, start : start + pair], edge[:, start : start + pair]], axis=0)
        vals = jnp.concatenate(
            [keys_values[:, width + start : width + start + pair], edge[:, width + start : width + start + pair]],
            axis=0,
        )
        outs = []
        for which in range(2):
            mask = is_first if which == 0 else jnp.logical_not(is_first)
            one = jnp.where(mask, two, jnp.zeros_like(two))
            scores = dot_nt(one, keys) * factor + bias[...]
            peak = jnp.max(scores, axis=-1, keepdims=True)
            exponent = jnp.exp(scores - peak)
            total = jnp.sum(exponent, axis=-1, keepdims=True)
            soft = (exponent / total).astype(BF16)
            outs.append(dot_nn(soft, vals))
            logs = jnp.where(lane == 2 * (start // pair) + which, peak + jnp.log(total), logs)
        attention[:, start : start + pair] = jnp.where(is_first, outs[0], outs[1]).astype(BF16)
    totals[...] = logs
    wait_all(copies)
    result = tokens[...].astype(F32) + dot_nn(attention[...], weight[...])
    hidden[...] = result
    normed, _ = norm_parts(result)
    xn2[...] = (normed * gains[1:2, :]).astype(BF16)


def lift_kernel(place, xn2, grad_out, *refs):
    pieces, rest = (refs[:PIECES], refs[PIECES:])
    keep_one, send_one, keep_two, send_two, slope_gate, active, weight, sems = rest
    me = place[0]
    cols = active.shape[1]
    wait_all(fill(pieces, weight, sems, me, pl.ds(0, 2 * cols)))
    gelu_input = dot_nn(xn2[...], weight[:, :cols])
    gate_part = dot_nn(xn2[...], weight[:, cols:])
    cdf_part = 0.5 * (1.0 + lax.erf(gelu_input * (1.0 / math.sqrt(2.0))))
    density = jnp.exp(-0.5 * gelu_input * gelu_input) * (1.0 / math.sqrt(2.0 * math.pi))
    activated = gelu_input * cdf_part
    active[...] = activated
    slope_gate[...] = gate_part * (cdf_part + gelu_input * density)
    gated = (activated * gate_part).astype(BF16)
    cut = keep_one.shape[1] - xn2.shape[1] // 2
    pack(keep_one, send_one, grad_out, gated[:, :cut], X_BIT, Y_BIT, me)
    pack(keep_two, send_two, grad_out, gated[:, cut:], Y_BIT, X_BIT, me)


def contract_kernel(place, gated_one, gated_two, grad_out, xn2, hidden, slope_gate, active, *refs):
    pieces, rest = (refs[:PIECES], refs[PIECES:])
    layer_out, keep_one, send_one, keep_two, send_two, weight, sems = rest
    me = place[0]
    cols = weight.shape[1]
    wait_all(fill(pieces, weight, sems, me, pl.ds(2 * cols, cols)))
    d_gated = dot_nn(grad_out[...], weight[...])
    pack(keep_one, send_one, xn2, (d_gated * slope_gate[...]).astype(BF16), Y_BIT, X_BIT, me)
    pack(keep_two, send_two, xn2, (d_gated * active[...]).astype(BF16), X_BIT, Y_BIT, me)
    skip = xn2.shape[1] // 2
    cut = gated_one.shape[1] - skip
    down = dot_nt(gated_one[:, skip:], weight[:, :cut]) + dot_nt(gated_two[:, skip:], weight[:, cut:])
    layer_out[...] = (hidden[...] + down).astype(BF16)


def hidden_back_kernel(place, pack_one, pack_two, grad_out, hidden, gains, *refs):
    first, third = (refs[:PIECES], refs[PIECES : 2 * PIECES])
    d_hidden, d_attention, gain_grad, lift_weight, weight, sems, sems_three = refs[2 * PIECES :]
    me = place[0]
    width = hidden.shape[1]
    copies = fill(first, lift_weight, sems, me, pl.ds(0, lift_weight.shape[1]))
    lasts = fill(third, weight, sems_three, me, pl.ds(3 * width, width))
    normed, scaled = norm_parts(hidden[...])
    wait_all(copies)
    cols = lift_weight.shape[1] // 2
    d_xn2 = dot_nt(pack_one[:, width // 2 :], lift_weight[:, :cols])
    d_xn2 = d_xn2 + dot_nt(pack_two[:, width // 2 :], lift_weight[:, cols:])
    d_norm, gain_term = norm_back(d_xn2, normed, scaled, gains[1:2, :])
    gain_grad[...] = gain_term
    total = grad_out[...].astype(F32) + d_norm
    d_hidden[...] = total
    rounded = total.astype(BF16)
    wait_all(lasts)
    d_attention[...] = dot_nt(rounded, weight[...]).astype(BF16)


def attend_back_kernel(
    place, queries, keys_values, edge, bias, totals, d_attention, cosine, sine, d_turned, d_keys_values, d_edge
):
    width = queries.shape[1]
    pair = 2 * HEAD_DIM
    factor = 1.0 / math.sqrt(HEAD_DIM)
    rows = queries.shape[0]
    is_first = head_masks((rows, pair))
    is_first_key = head_masks((rows + edge.shape[0], pair))
    for start in range(0, width, pair):
        here = slice(start, start + pair)
        there = slice(width + start, width + start + pair)
        two = queries[:, here]
        d_two = d_attention[:, here]
        keys = jnp.concatenate([keys_values[:, here], edge[:, here]], axis=0)
        vals = jnp.concatenate([keys_values[:, there], edge[:, there]], axis=0)
        d_queries, d_keys, d_vals = ([], [], [])
        for which in range(2):
            mask = is_first if which == 0 else jnp.logical_not(is_first)
            one = jnp.where(mask, two, jnp.zeros_like(two))
            d_one = jnp.where(mask, d_two, jnp.zeros_like(d_two))
            head = 2 * (start // pair) + which
            scores = dot_nt(one, keys) * factor + bias[...]
            recomputed = jnp.exp(scores - totals[:, head : head + 1])
            d_soft = dot_nt(d_one, vals)
            center = jnp.sum(recomputed * d_soft, axis=-1, keepdims=True)
            d_scores = (recomputed * (d_soft - center) * factor).astype(BF16)
            d_queries.append(dot_nn(d_scores, keys))
            d_keys.append(dot_tt(d_scores, two))
            d_vals.append(dot_tt(recomputed.astype(BF16), d_two))
        d_query = jnp.where(is_first, d_queries[0], d_queries[1])
        d_turned[:, here] = turn(d_query, cosine[...], -sine[...]).astype(BF16)
        d_key = jnp.where(is_first_key, d_keys[0], d_keys[1])
        d_val = jnp.where(is_first_key, d_vals[0], d_vals[1])
        d_keys_values[:, here] = d_key[:rows]
        d_keys_values[:, there] = d_val[:rows]
        d_edge[:, here] = d_key[rows:].astype(BF16)
        d_edge[:, there] = d_val[rows:].astype(BF16)


def keys_back_kernel(
    place, d_queries, d_keys_values, arrived, cosine, sine, xn1, keep_one, send_one, keep_two, send_two, summed, d_turned
):
    me, along = (place[0], place[1])
    width = xn1.shape[1]
    pair = 2 * HEAD_DIM
    rows = arrived.shape[0]
    summed[...] = d_keys_values[...]
    where = pl.ds(pl.multiple_of((1 - along) * rows, rows), rows)
    summed[where, :] = summed[where, :] + arrived[...].astype(F32)
    for start in range(0, width, pair):
        here = slice(start, start + pair)
        there = slice(width + start, width + start + pair)
        d_turned[:, there] = turn(summed[:, here], cosine[...], -sine[...]).astype(BF16)
    d_turned[:, :width] = d_queries[...]
    d_turned[:, 2 * width :] = summed[:, width:].astype(BF16)
    middle = d_turned.shape[1] // 2
    pack(keep_one, send_one, xn1, d_turned[:, :middle], X_BIT, Y_BIT, me)
    pack(keep_two, send_two, xn1, d_turned[:, middle:], Y_BIT, X_BIT, me)


def tokens_back_kernel(place, pack_one, pack_two, tokens, attention, d_hidden, gains, mlp_term, *refs):
    pieces, (keep, send, input_grad, weight, sems) = (refs[:PIECES], refs[PIECES:])
    rows = tokens.shape[0]
    width = tokens.shape[1]
    copies = fill(pieces, weight, sems, place[0], pl.ds(0, 3 * width))
    normed, scaled = norm_parts(tokens[...].astype(F32))
    wait_all(copies)
    middle = pack_one.shape[1] - width // 2
    d_xn1 = dot_nt(pack_one[:, width // 2 :], weight[:, :middle])
    d_xn1 = d_xn1 + dot_nt(pack_two[:, width // 2 :], weight[:, middle:])
    d_norm, gain_term = norm_back(d_xn1, normed, scaled, gains[0:1, :])
    pack(keep, send, attention, d_hidden[...].astype(BF16), Y_BIT, X_BIT, place[0])
    extra = keep.shape[0] - rows
    line = lax.broadcasted_iota(jnp.int32, (extra, width), 0)
    terms = jnp.where(line == 0, mlp_term[...], jnp.where(line == 1, gain_term, 0.0)).astype(BF16)
    for target in (keep, send):
        target[rows:, : width // 2] = jnp.zeros((extra, width // 2), BF16)
        target[rows:, width // 2 :] = terms
    input_grad[...] = (d_hidden[...] + d_norm).astype(BF16)


def product_kernel(width, rows, chip, other, own, sent, joined, *refs):
    terms, sems = (refs[0] if len(refs) > 1 else None, refs[-1])
    copies = []
    extra = 0 if terms is None else terms.shape[1]
    for index in range(4):
        part, start = ((chip, other)[index // 2], index % 2 * (rows + extra))
        source = part.at[pl.ds(start, rows)]
        copies.append(pltpu.make_async_copy(source, joined.at[pl.ds(index * rows, rows)], sems.at[index]))
        if terms is not None:
            copies.append(
                pltpu.make_async_copy(part.at[pl.ds(start + rows, extra)], terms.at[index], sems.at[4 + index])
            )
    for copy in copies:
        copy.start()
    wait_all(copies)
    block = lambda top, k: joined[2 * rows * top : 2 * rows * (top + 1), k * width : (k + 1) * width]
    right = joined[:, 4 * width :]
    left = jnp.concatenate([block(0, 2), block(1, 3)], axis=0)
    sent[:width] = dot_tt(left, right).astype(BF16)
    left = jnp.concatenate([block(0, 0), block(1, 1)], axis=0)
    own[:width] = dot_tt(left, right)
    if terms is not None:
        total = sum(terms[index, :, 4 * width :].astype(F32) for index in range(4))
        own[width:] = total
        sent[width:] = total.astype(BF16)


def call(kernel, outs, operands, scratch=(), smem=1, anywhere=(), flops=0, size=0):
    specs = []
    for index in range(len(operands)):
        if index < smem:
            specs.append(pl.BlockSpec(memory_space=pltpu.SMEM))
        elif index in anywhere:
            specs.append(pl.BlockSpec(memory_space=pltpu.HBM))
        else:
            specs.append(pl.BlockSpec(memory_space=pltpu.VMEM))
    return pl.pallas_call(
        kernel,
        out_shape=[jax.ShapeDtypeStruct(shape, kind) for shape, kind in outs],
        in_specs=specs,
        out_specs=[pl.BlockSpec(memory_space=pltpu.VMEM)] * len(outs),
        scratch_shapes=list(scratch),
        cost_estimate=pl.CostEstimate(flops=flops, bytes_accessed=size, transcendentals=0),
        compiler_params=pltpu.CompilerParams(vmem_limit_bytes=VMEM_BYTES),
    )(*operands)


def grad_rows(keep, over_link, width, before=(), after=()):
    return products(share(keep, over_link, before), width, after)


def share(keep, over_link, before=()):
    return jnp.concatenate(later([keep, over_link], before), axis=0)


def products(chip, width, after=()):
    rows = chip.shape[0] // 256 * 128
    extra = chip.shape[0] // 2 - rows
    cols = chip.shape[1] - 4 * width
    other = later(swap(chip, CORE_BIT), after)
    scratch = [pltpu.VMEM((4 * rows, 4 * width + cols), BF16)]
    if extra:
        scratch.append(pltpu.VMEM((4, extra, 4 * width + cols), BF16))
    return call(
        lambda *refs: product_kernel(width, rows, *refs),
        [((width + extra, cols), F32), ((width + extra, cols), BF16)],
        [chip, other],
        scratch + [pltpu.SemaphoreType.DMA((8,))],
        smem=0,
        anywhere=(0, 1),
        flops=16 * rows * width * cols,
        size=4 * rows * (4 * width + cols) * 2 + 6 * width * cols,
    )


def line_first(part):
    return lax.ppermute(part.astype(BF16), "replica", [(0, 1), (3, 2)])


def line_pair(part, first):
    return (part + first.astype(F32)).astype(BF16)


def line_middle(pair):
    return lax.ppermute(pair, "replica", [(1, 2), (2, 1)])


def line_total(pair, other):
    return (pair.astype(F32) + other.astype(F32)).astype(BF16)


def line_back(total):
    return lax.ppermute(total, "replica", [(1, 0), (2, 3)])


def line_end(total, back):
    place = lax.axis_index("replica")
    middle = (place == 1) | (place == 2)
    return jnp.where(middle, total, back).astype(F32)


def body_plane(
    tokens,
    input_gain,
    qkv_weight,
    output_weight,
    mlp_gain,
    expand_weight,
    contract_weight,
    positions,
    mask_bias,
    cotangent,
):
    me = lax.axis_index(PLANE)
    along = lax.axis_index("ctx")
    place = jnp.stack([me, along]).astype(jnp.int32)
    shard = qkv_weight.shape[0]
    true_width = expand_weight.shape[1] // 2
    fill_cols = -true_width % 128
    ff_width = true_width + fill_cols
    source, grad_out = (tokens[0], cotangent[0])
    rows, width = source.shape
    gains = jnp.stack([input_gain, mlp_gain], axis=1)
    gains = jnp.pad(gains, ((0, 0), (0, 126)))
    front = jnp.concatenate([qkv_weight, output_weight, gains], axis=1)
    widened = lambda values: jnp.pad(values, ((0, 0), (0, fill_cols)))
    feed = jnp.concatenate(
        [
            widened(expand_weight[:, :true_width]),
            widened(expand_weight[:, true_width:]),
            widened(contract_weight),
        ],
        axis=1,
    )
    fetched = fetch_pieces(front)
    packed = share_pieces(fetched)
    feed_fetched = fetch_pieces(feed, tuple(fetched[3:]))
    cosine, sine = rope_tables(positions[0], HEAD_DIM)
    cosine = jnp.concatenate([cosine[:, 0]] * 4, axis=1)
    sine = jnp.concatenate([-sine[:, 0], sine[:, 0]] * 2, axis=1)
    bias = mask_bias[0]
    bias = jnp.concatenate(
        [bias[:, HALF : HALF + rows], jnp.where(along == 0, bias[:, HALF + rows :], bias[:, :HALF])], axis=1
    )
    sems = pltpu.SemaphoreType.DMA((PIECES,))
    front_cols = front.shape[1]
    queries, keys_values, edge, xn1, full_gains = call(
        front_kernel,
        [((rows, width), BF16), ((rows, 2 * width), BF16), ((HALF, 2 * width), BF16), ((rows, width), BF16), ((8, width), F32)],
        [place, source, cosine, sine] + packed,
        [pltpu.VMEM((width, front_cols), BF16), sems],
        anywhere=range(4, 4 + PIECES),
        flops=6 * rows * width * width,
        size=2 * width * front_cols,
    )
    edge = swap(edge, X_BIT)
    attention, totals, hidden, xn2 = call(
        attend_kernel,
        [((rows, width), BF16), ((rows, 128), F32), ((rows, width), F32), ((rows, width), BF16)],
        [place, queries, keys_values, edge, bias, source, full_gains] + packed,
        [pltpu.VMEM((width, width), BF16), sems],
        anywhere=range(7, 7 + PIECES),
        flops=12 * rows * width * width,
        size=4 * width * width,
    )
    feed_pieces = share_pieces(feed_fetched, xn2)
    half = 4 * shard
    cut = -(-ff_width // 256) * 128
    cuts = [((rows, half + cut), BF16)] * 2 + [((rows, half + ff_width - cut), BF16)] * 2
    keep_c, send_c, keep_d, send_d, slope_gate, active = call(
        lift_kernel,
        cuts + [((rows, ff_width), F32)] * 2,
        [place, xn2, grad_out] + feed_pieces,
        [pltpu.VMEM((width, 2 * ff_width), BF16), sems],
        anywhere=range(3, 3 + PIECES),
        flops=4 * rows * width * ff_width,
        size=4 * width * ff_width,
    )
    layer_out, keep_g, send_g, keep_u, send_u = call(
        contract_kernel,
        [((rows, width), BF16)] + [((rows, half + ff_width), BF16)] * 4,
        [place, keep_c, keep_d, grad_out, xn2, hidden, slope_gate, active] + feed_pieces,
        [pltpu.VMEM((width, ff_width), BF16), sems],
        anywhere=range(8, 8 + PIECES),
        flops=4 * rows * width * ff_width,
        size=2 * width * ff_width,
    )
    d_hidden, d_attention, mlp_term = call(
        hidden_back_kernel,
        [((rows, width), F32), ((rows, width), BF16), ((1, width), F32)],
        [place, keep_g, keep_u, grad_out, hidden, full_gains] + feed_pieces + packed,
        [pltpu.VMEM((width, 2 * ff_width), BF16), pltpu.VMEM((width, width), BF16), sems, sems],
        anywhere=range(6, 6 + 2 * PIECES),
        flops=6 * rows * width * ff_width,
        size=6 * width * ff_width,
    )
    link_c = swap(send_c, X_BIT)
    link_d = swap(send_d, Y_BIT)
    link_g = swap(send_g, Y_BIT)
    link_u = swap(send_u, X_BIT)
    d_queries, d_keys_values, d_edge = call(
        attend_back_kernel,
        [((rows, width), BF16), ((rows, 2 * width), F32), ((HALF, 2 * width), BF16)],
        [place, queries, keys_values, edge, bias, totals, d_attention, cosine, sine],
        flops=20 * rows * width * width,
        size=4 * width * width,
    )
    first_own, first_sent = grad_rows(keep_c, link_c, shard, keep_g, d_edge)
    second_own, second_sent = grad_rows(keep_d, link_d, shard, keep_g, d_edge)
    first_back = swap(first_sent, Y_BIT)
    second_back = swap(second_sent, X_BIT)
    chip_g = share(keep_g, link_g, (first_sent, second_sent))
    chip_u = share(keep_u, link_u, (first_sent, second_sent))
    first_back, second_back = later((first_back, second_back), chip_g, chip_u)
    contract_part = jnp.concatenate(
        [first_own + first_back.astype(F32), second_own + second_back.astype(F32)], axis=1
    )
    contract_first = line_first(contract_part)
    gelu_own, gelu_sent = products(chip_g, shard, contract_part)
    gelu_back = swap(gelu_sent, X_BIT)
    gate_own, gate_sent = products(chip_u, shard, gelu_sent)
    gate_back = swap(gate_sent, Y_BIT)
    d_keys_values = later(d_keys_values, gate_sent)
    keep_kv, send_kv, keep_vk, send_vk = call(
        keys_back_kernel,
        [((rows, half + 3 * width // 2), BF16)] * 4,
        [place, d_queries, d_keys_values, swap(d_edge, X_BIT), cosine, sine, xn1],
        [pltpu.VMEM((rows, 2 * width), F32), pltpu.VMEM((rows, 3 * width), BF16)],
        flops=rows * width,
        size=8 * rows * width,
    )
    link_kv = swap(send_kv, X_BIT)
    link_vk = swap(send_vk, Y_BIT)
    contract_pair = line_pair(contract_part, later(contract_first, keep_kv))
    contract_other = line_middle(contract_pair)
    gelu_part = gelu_own + later(gelu_back, contract_pair).astype(F32)
    gelu_first = line_first(gelu_part)
    gate_part = gate_own + later(gate_back, gelu_part).astype(F32)
    gate_first = line_first(gate_part)
    contract_total = line_total(contract_pair, later(contract_other, gate_part))
    contract_last = line_back(contract_total)
    gelu_pair = line_pair(gelu_part, later(gelu_first, contract_total))
    gelu_other = line_middle(gelu_pair)
    chip_kv = share(keep_kv, link_kv, gelu_pair)
    chip_vk = share(keep_vk, link_vk, gelu_pair)
    low_own, low_sent = products(chip_kv, shard)
    low_back = swap(low_sent, Y_BIT)
    high_own, high_sent = products(chip_vk, shard, low_sent)
    high_back = swap(high_sent, X_BIT)
    d_hidden = later(d_hidden, high_sent)
    keep_o, send_o, input_grad = call(
        tokens_back_kernel,
        [((rows + 16, half + width), BF16)] * 2 + [((rows, width), BF16)],
        [place, keep_kv, keep_vk, source, attention, d_hidden, full_gains, mlp_term] + packed,
        [pltpu.VMEM((width, 3 * width), BF16), sems],
        anywhere=range(8, 8 + PIECES),
        flops=6 * rows * width * width,
        size=6 * width * width,
    )
    link_o = swap(send_o, Y_BIT)
    gelu_total = line_total(gelu_pair, later(gelu_other, keep_o, contract_last))
    gelu_last = line_back(gelu_total)
    gate_pair = line_pair(gate_part, later(gate_first, gelu_total))
    gate_other = line_middle(gate_pair)
    low_part = low_own + later(low_back, gate_pair).astype(F32)
    low_first = line_first(low_part)
    high_part = high_own + later(high_back, low_part).astype(F32)
    high_first = line_first(high_part)
    gate_total = line_total(gate_pair, later(gate_other, high_part))
    gate_last = line_back(gate_total)
    low_pair = line_pair(low_part, later(low_first, gate_total))
    low_other = line_middle(low_pair)
    out_own, out_sent = grad_rows(keep_o, link_o, shard, low_pair)
    out_back = swap(out_sent, X_BIT)
    high_pair = line_pair(high_part, later(high_first, out_sent, gelu_last))
    high_other = line_middle(high_pair)
    out_part = out_own + later(out_back, high_pair).astype(F32)
    out_first = line_first(out_part)
    low_total = line_total(low_pair, later(low_other, out_part))
    low_last = line_back(low_total)
    out_pair = line_pair(out_part, later(out_first, low_total))
    out_other = line_middle(out_pair)
    high_total = line_total(high_pair, later(high_other, out_pair, gate_last))
    high_last = line_back(high_total)
    out_total = line_total(out_pair, later(out_other, high_total))
    out_last = line_back(out_total)
    contract_grad = line_end(contract_total, later(contract_last, high_total))
    gelu_grad = line_end(gelu_total, later(gelu_last, high_total))
    gate_grad = line_end(gate_total, later(gate_last, high_total))
    all_grad = jnp.concatenate([line_end(low_total, low_last), line_end(high_total, high_last)], axis=1)
    out_grad = line_end(out_total, out_last)
    gain_rows = lax.dynamic_slice_in_dim(out_grad[shard : shard + 2], me * shard, shard, axis=1)
    return (
        layer_out[None],
        input_grad[None],
        gain_rows[1],
        all_grad,
        out_grad[:shard],
        gain_rows[0],
        jnp.concatenate([gelu_grad[:, :true_width], gate_grad[:, :true_width]], axis=1),
        contract_grad[:, :true_width],
    )


def solution(mesh):
    in_specs = (
        P(("replica", "fsdp"), "ctx", None),
        P(("fsdp", "ctx")),
        P(("fsdp", "ctx"), None),
        P(("fsdp", "ctx"), None),
        P(("fsdp", "ctx")),
        P(("fsdp", "ctx"), None),
        P(("fsdp", "ctx"), None),
        P(("replica", "fsdp"), "ctx"),
        P(("replica", "fsdp"), "ctx", None),
        P(("replica", "fsdp"), "ctx", None),
    )
    out_specs = (
        P(("replica", "fsdp"), "ctx", None),
        P(("replica", "fsdp"), "ctx", None),
        P(("fsdp", "ctx")),
        P(("fsdp", "ctx"), None),
        P(("fsdp", "ctx"), None),
        P(("fsdp", "ctx")),
        P(("fsdp", "ctx"), None),
        P(("fsdp", "ctx"), None),
    )
    sizes = (mesh.shape["replica"], mesh.shape["fsdp"], mesh.shape["ctx"])
    body = body_plane if sizes == (4, 4, 2) else body_generic
    return jax.shard_map(body, mesh=mesh, in_specs=in_specs, out_specs=out_specs, check_vma=False)
```

```python
import math

import jax
import jax.numpy as jnp
from jax import lax
from jax.experimental import pallas as pl
from jax.experimental.pallas import tpu as pltpu
from jax.sharding import PartitionSpec as P

HEAD_DIM = 64
HALF = 64


EPS = 1e-05
THETA = 10000.0


def extended_2(cells, sides, width):
    for axis, dim in sides:
        count = lax.axis_size(axis)
        ends = count - 1
        head = lax.slice_in_dim(cells, 0, width, axis=dim)
        tail = lax.slice_in_dim(cells, cells.shape[dim] - width, cells.shape[dim], axis=dim)
        cells = jnp.concatenate(
            [
                lax.ppermute(tail, axis, [(i, (i + 1) % count) for i in range(ends)]),
                cells,
                lax.ppermute(head, axis, [((i + 1) % count, i) for i in range(ends)]),
            ],
            axis=dim,
        )
    return cells


def from_behind(value, axis, steps):
    count = lax.axis_size(axis)
    first, last = (max(0, -steps), min(count, count - steps))
    return lax.ppermute(value, axis, [(source, source + steps) for source in range(first, last)])


def layer_norm(values, gain):
    center = values - jnp.mean(values, axis=-1, keepdims=True)
    variance = jnp.mean(center * center, axis=-1, keepdims=True)
    scaled = lax.rsqrt(variance + EPS)
    normed = center * scaled
    return (normed, scaled, (normed * gain.astype(jnp.float32)).astype(jnp.bfloat16))


def layer_norm_back(incoming, normed, scaled, gain):
    weighted = incoming * gain.astype(jnp.float32)
    gain_grad = jnp.sum(incoming * normed, axis=0)
    mean_one = jnp.mean(weighted, axis=-1, keepdims=True)
    mean_two = jnp.mean(weighted * normed, axis=-1, keepdims=True)
    return (scaled * (weighted - mean_one - normed * mean_two), gain_grad)


def rope_tables(positions, head_size):
    half_dim = head_size // 2
    exponent = jnp.arange(half_dim, dtype=jnp.float32) * (2.0 / head_size)
    frequency = jnp.exp(-math.log(THETA) * exponent)
    angles = positions.astype(jnp.float32)[:, None] * frequency[None, :]
    return (jnp.cos(angles)[:, None, :], jnp.sin(angles)[:, None, :])


def rotate(values, cosine, sine):
    half_dim = values.shape[-1] // 2
    lower_half, upper_half = (values[..., :half_dim], values[..., half_dim:])
    return jnp.concatenate(
        [lower_half * cosine - upper_half * sine, upper_half * cosine + lower_half * sine], axis=-1
    )


def rotate_back(values, cosine, sine):
    half_dim = values.shape[-1] // 2
    lower_half, upper_half = (values[..., :half_dim], values[..., half_dim:])
    return jnp.concatenate(
        [lower_half * cosine + upper_half * sine, upper_half * cosine - lower_half * sine], axis=-1
    )


def gelu_slope(values):
    cdf_part = 0.5 * (1.0 + jax.scipy.special.erf(values * (1.0 / math.sqrt(2.0))))
    density = jnp.exp(-0.5 * values * values) * (1.0 / math.sqrt(2.0 * math.pi))
    return cdf_part + values * density


def block_scores(queries, key_rows, additive):
    factor = 1.0 / math.sqrt(queries.shape[-1])
    scores = jnp.einsum("qhd,khd->hqk", queries, key_rows, preferred_element_type=jnp.float32)
    return scores * factor + additive[None]


def attend(queries, key_rows, value_rows, additive):
    scores = block_scores(queries, key_rows, additive)
    row_peak = jnp.max(scores, axis=-1, keepdims=True)
    exponent = jnp.exp(scores - row_peak)
    row_total = jnp.sum(exponent, axis=-1, keepdims=True)
    soft_weights = (exponent / row_total).astype(jnp.bfloat16)
    mixed = jnp.einsum("hqk,khd->qhd", soft_weights, value_rows, preferred_element_type=jnp.float32)
    return (mixed.astype(jnp.bfloat16), row_peak[..., 0] + jnp.log(row_total[..., 0]))


def attend_back(queries, key_rows, value_rows, additive, log_total, d_mixed):
    factor = 1.0 / math.sqrt(queries.shape[-1])
    scores = block_scores(queries, key_rows, additive)
    recomputed = jnp.exp(scores - log_total[..., None])
    d_soft = jnp.einsum("qhd,khd->hqk", d_mixed, value_rows, preferred_element_type=jnp.float32)
    center = jnp.sum(recomputed * d_soft, axis=-1, keepdims=True)
    d_scores = (recomputed * (d_soft - center) * factor).astype(jnp.bfloat16)
    d_queries = jnp.einsum("hqk,khd->qhd", d_scores, key_rows, preferred_element_type=jnp.float32)
    d_keys = jnp.einsum("hqk,qhd->khd", d_scores, queries, preferred_element_type=jnp.float32)
    d_values = jnp.einsum(
        "hqk,qhd->khd", recomputed.astype(jnp.bfloat16), d_mixed, preferred_element_type=jnp.float32
    )
    return (d_queries, d_keys, d_values)


def body_generic(
    tokens,
    input_gain,
    qkv_weight,
    output_weight,
    mlp_gain,
    expand_weight,
    contract_weight,
    positions,
    mask_bias,
    cotangent,
):
    gathered = (
        lax.all_gather(input_gain, ("fsdp", "ctx"), axis=0, tiled=True),
        lax.all_gather(qkv_weight, ("fsdp", "ctx"), axis=0, tiled=True),
        lax.all_gather(output_weight, ("fsdp", "ctx"), axis=0, tiled=True),
        lax.all_gather(mlp_gain, ("fsdp", "ctx"), axis=0, tiled=True),
        lax.all_gather(expand_weight, ("fsdp", "ctx"), axis=0, tiled=True),
        lax.all_gather(contract_weight, ("fsdp", "ctx"), axis=0, tiled=True),
    )
    full_input_gain, full_qkv, full_output, full_mlp_gain, full_expand, full_contract = gathered
    residual = tokens[0].astype(jnp.float32)
    row_count, model_width = residual.shape
    head_count = model_width // HEAD_DIM
    cosine, sine = rope_tables(positions[0], HEAD_DIM)
    normed1, scaled1, xn1 = layer_norm(residual, full_input_gain)
    projected = jnp.dot(xn1, full_qkv, preferred_element_type=jnp.float32).reshape(
        row_count, 3, head_count, HEAD_DIM
    )
    queries = rotate(projected[:, 0], cosine, sine).astype(jnp.bfloat16)
    key_rows = rotate(projected[:, 1], cosine, sine).astype(jnp.bfloat16)
    value_rows = projected[:, 2].astype(jnp.bfloat16)
    packed = jnp.concatenate(
        [key_rows.reshape(row_count, model_width), value_rows.reshape(row_count, model_width)],
        axis=1,
    )
    extended = extended_2(packed, (("ctx", 0),), HALF)
    extent = extended.shape[0]
    key_ext = extended[:, :model_width].reshape(extent, head_count, HEAD_DIM)
    value_ext = extended[:, model_width:].reshape(extent, head_count, HEAD_DIM)
    additive = mask_bias[0]
    mixed, log_total = attend(queries, key_ext, value_ext, additive)
    attention = mixed.reshape(row_count, model_width)
    hidden = residual + jnp.dot(attention, full_output, preferred_element_type=jnp.float32)
    normed2, scaled2, xn2 = layer_norm(hidden, full_mlp_gain)
    lifted = jnp.dot(xn2, full_expand, preferred_element_type=jnp.float32)
    ff_width = lifted.shape[1] // 2
    gelu_input = lifted[:, :ff_width]
    gate_part = lifted[:, ff_width:]
    activated = jax.nn.gelu(gelu_input, approximate=False)
    gated = (activated * gate_part).astype(jnp.bfloat16)
    down_out = jnp.einsum("tf,jf->tj", gated, full_contract, preferred_element_type=jnp.float32)
    layer_out = (hidden + down_out).astype(jnp.bfloat16)
    back_input_gain, back_qkv, back_output, back_mlp_gain, back_expand, back_contract = gathered
    grad_out = cotangent[0]
    d_gated = jnp.dot(grad_out, back_contract, preferred_element_type=jnp.float32)
    d_lifted = jnp.concatenate(
        [d_gated * gate_part * gelu_slope(gelu_input), d_gated * activated], axis=1
    ).astype(jnp.bfloat16)
    d_xn2 = jnp.einsum("tc,dc->td", d_lifted, back_expand, preferred_element_type=jnp.float32)
    d_norm2, mlp_gain_term = layer_norm_back(d_xn2, normed2, scaled2, back_mlp_gain)
    d_hidden = grad_out.astype(jnp.float32) + d_norm2
    d_proj = d_hidden.astype(jnp.bfloat16)
    d_attention = jnp.einsum(
        "tj,ij->ti", d_proj, back_output, preferred_element_type=jnp.float32
    ).astype(jnp.bfloat16)
    d_queries, d_key_ext, d_value_ext = attend_back(
        queries,
        key_ext,
        value_ext,
        additive,
        log_total,
        d_attention.reshape(row_count, head_count, HEAD_DIM),
    )
    grad_ext = jnp.concatenate(
        [d_key_ext.reshape(extent, model_width), d_value_ext.reshape(extent, model_width)], axis=1
    )
    from_next = from_behind(grad_ext[:HALF], "ctx", -1)
    from_prev = from_behind(grad_ext[row_count + HALF :], "ctx", 1)
    grad_kv = grad_ext[HALF : HALF + row_count]
    grad_kv = grad_kv + jnp.pad(from_prev, ((0, row_count - HALF), (0, 0)))
    grad_kv = grad_kv + jnp.pad(from_next, ((row_count - HALF, 0), (0, 0)))
    d_keys = rotate_back(
        grad_kv[:, :model_width].reshape(row_count, head_count, HEAD_DIM), cosine, sine
    )
    d_values = grad_kv[:, model_width:]
    d_queries = rotate_back(d_queries, cosine, sine)
    d_projected = jnp.concatenate(
        [
            d_queries.reshape(row_count, model_width),
            d_keys.reshape(row_count, model_width),
            d_values,
        ],
        axis=1,
    ).astype(jnp.bfloat16)
    d_xn1 = jnp.einsum("tc,dc->td", d_projected, back_qkv, preferred_element_type=jnp.float32)
    d_norm1, input_gain_term = layer_norm_back(d_xn1, normed1, scaled1, back_input_gain)
    input_grad = (d_hidden + d_norm1).astype(jnp.bfloat16)
    left_one, left_two, left_three, left_four = (xn1, attention, xn2, grad_out)
    gain_one, gain_two = (input_gain_term, mlp_gain_term)
    qkv_term = jnp.einsum("ti,tj->ij", left_one, d_projected, preferred_element_type=jnp.float32)
    output_term = jnp.einsum("ti,tj->ij", left_two, d_proj, preferred_element_type=jnp.float32)
    expand_term = jnp.einsum("ti,tj->ij", left_three, d_lifted, preferred_element_type=jnp.float32)
    contract_term = jnp.einsum("ti,tj->ij", left_four, gated, preferred_element_type=jnp.float32)
    first_gain = gain_one[:, None]
    second_gain = gain_two[:, None]
    shares = lax.psum_scatter(
        jnp.concatenate(
            [qkv_term, output_term, expand_term, contract_term, first_gain, second_gain], axis=1
        ),
        ("fsdp", "ctx"),
        scatter_dimension=0,
        tiled=True,
    )
    result = lax.psum(shares, "replica")
    qkv_cols = 3 * model_width
    expand_cols = 2 * ff_width
    qkv_grad = result[:, :qkv_cols]
    output_grad = result[:, qkv_cols : qkv_cols + model_width]
    offset = qkv_cols + model_width
    expand_grad = result[:, offset : offset + expand_cols]
    offset = offset + expand_cols
    contract_grad = result[:, offset : offset + ff_width]
    offset = offset + ff_width
    input_gain_grad = result[:, offset]
    mlp_gain_grad = result[:, offset + 1]
    return (
        layer_out[None],
        input_grad[None],
        input_gain_grad,
        qkv_grad,
        output_grad,
        mlp_gain_grad,
        expand_grad,
        contract_grad,
    )


X_BIT, CORE_BIT, Y_BIT = (1, 2, 4)
PLANE = ("fsdp", "ctx")
PLANE_SIZE = 8
PIECES = 10
VMEM_BYTES = 50 * 1024 * 1024
F32, BF16 = (jnp.float32, jnp.bfloat16)


def swap(value, bit):
    return lax.ppermute(value, PLANE, [(i, i ^ bit) for i in range(PLANE_SIZE)])


def later(value, *others):
    return lax.optimization_barrier((value, others))[0]


def fetch_pieces(own, after=()):
    own = later(own, after)
    half = own.shape[0] // 2
    over_x = swap(own, X_BIT)
    over_y = swap(own, Y_BIT)
    return [own, over_x, over_y, swap(over_x[:half], Y_BIT), swap(over_y[half:], X_BIT)]


def share_pieces(first, after=()):
    corners = [swap(later(part, after), CORE_BIT) for part in first[3:]]
    return first + [swap(part, CORE_BIT) for part in first[:3]] + corners


def fill(pieces, target, sems, me, columns=None):
    shard = target.shape[0] // PLANE_SIZE
    half = shard // 2
    corner = X_BIT | Y_BIT
    places = [(0, 0, shard), (X_BIT, 0, shard), (Y_BIT, 0, shard), (corner, 0, half), (corner, half, half)]
    places = places + [(offset | CORE_BIT, start, rows) for offset, start, rows in places]
    copies = []
    for index, (piece, (offset, start, rows)) in enumerate(zip(pieces, places)):
        row = pl.multiple_of((me ^ offset) * shard + start, half)
        source = piece if columns is None else piece.at[:, columns]
        copies.append(pltpu.make_async_copy(source, target.at[pl.ds(row, rows)], sems.at[index]))
    for copy in copies:
        copy.start()
    return copies


def wait_all(copies):
    for copy in copies:
        copy.wait()


def pack(keep, send, left, right, gather_bit, sum_bit, me):
    rows, width = (left.shape[0], left.shape[1] // PLANE_SIZE)
    for slot, offset in enumerate([0, CORE_BIT, sum_bit, CORE_BIT | sum_bit]):
        for target, flip in ((keep, 0), (send, gather_bit)):
            source = pl.multiple_of((me ^ (offset | flip)) * width, width)
            target[:rows, slot * width : (slot + 1) * width] = left[:, pl.ds(source, width)]
    keep[:rows, 4 * width :] = right
    send[:rows, 4 * width :] = right


def turn(values, cosine, sine):
    lane = lax.broadcasted_iota(jnp.int32, values.shape, 1)
    low = lane % HEAD_DIM < HEAD_DIM // 2
    other = jnp.where(
        low,
        pltpu.roll(values, values.shape[1] - HEAD_DIM // 2, 1),
        pltpu.roll(values, HEAD_DIM // 2, 1),
    )
    return values * cosine + other * sine


def dot_tt(one, two):
    return lax.dot_general(one, two, (((0,), (0,)), ((), ())), preferred_element_type=F32)


def dot_nt(one, two):
    return lax.dot_general(one, two, (((1,), (1,)), ((), ())), preferred_element_type=F32)


def dot_nn(one, two):
    return jnp.dot(one, two, preferred_element_type=F32)


def norm_parts(values):
    center = values - jnp.mean(values, axis=-1, keepdims=True)
    variance = jnp.mean(center * center, axis=-1, keepdims=True)
    scaled = lax.rsqrt(variance + EPS)
    return (center * scaled, scaled)


def norm_back(incoming, normed, scaled, gain):
    weighted = incoming * gain
    gain_grad = jnp.sum(incoming * normed, axis=0, keepdims=True)
    mean_one = jnp.mean(weighted, axis=-1, keepdims=True)
    mean_two = jnp.mean(weighted * normed, axis=-1, keepdims=True)
    return (scaled * (weighted - mean_one - normed * mean_two), gain_grad)


def front_kernel(place, tokens, cosine, sine, *refs):
    pieces, (queries, keys_values, edge, xn1, gains, weight, sems) = (refs[:PIECES], refs[PIECES:])
    me, along = (place[0], place[1])
    copies = fill(pieces, weight, sems, me)
    normed, _ = norm_parts(tokens[...].astype(F32))
    width = tokens.shape[1]
    wait_all(copies)
    turned = weight[:, 4 * width :].astype(F32).T
    gains[...] = turned[: gains.shape[0]]
    rounded = (normed * gains[0:1, :]).astype(BF16)
    xn1[...] = rounded
    pair = cosine.shape[1]
    projected = dot_nn(rounded, weight[:, : 3 * width])
    for start in range(0, width, pair):
        part = projected[:, start : start + pair]
        queries[:, start : start + pair] = turn(part, cosine[...], sine[...]).astype(BF16)
        part = projected[:, width + start : width + start + pair]
        keys_values[:, start : start + pair] = turn(part, cosine[...], sine[...]).astype(BF16)
    keys_values[:, width:] = projected[:, 2 * width :].astype(BF16)
    rows = edge.shape[0]
    edge[...] = keys_values[pl.ds(pl.multiple_of((1 - along) * rows, rows), rows), :]


def head_masks(shape):
    lane = lax.broadcasted_iota(jnp.int32, shape, 1)
    return lane < HEAD_DIM


def attend_kernel(place, queries, keys_values, edge, bias, tokens, gains, *refs):
    pieces, (attention, totals, hidden, xn2, weight, sems) = (refs[:PIECES], refs[PIECES:])
    width = tokens.shape[1]
    copies = fill(pieces, weight, sems, place[0], pl.ds(3 * width, width))
    pair = 2 * HEAD_DIM
    factor = 1.0 / math.sqrt(HEAD_DIM)
    rows = queries.shape[0]
    is_first = head_masks((rows, pair))
    lane = lax.broadcasted_iota(jnp.int32, totals.shape, 1)
    logs = jnp.zeros(totals.shape, F32)
    for start in range(0, width, pair):
        two = queries[:, start : start + pair]
        keys = jnp.concatenate([keys_values[:, start : start + pair], edge[:, start : start + pair]], axis=0)
        vals = jnp.concatenate(
            [keys_values[:, width + start : width + start + pair], edge[:, width + start : width + start + pair]],
            axis=0,
        )
        outs = []
        for which in range(2):
            mask = is_first if which == 0 else jnp.logical_not(is_first)
            one = jnp.where(mask, two, jnp.zeros_like(two))
            scores = dot_nt(one, keys) * factor + bias[...]
            peak = jnp.max(scores, axis=-1, keepdims=True)
            exponent = jnp.exp(scores - peak)
            total = jnp.sum(exponent, axis=-1, keepdims=True)
            soft = (exponent / total).astype(BF16)
            outs.append(dot_nn(soft, vals))
            logs = jnp.where(lane == 2 * (start // pair) + which, peak + jnp.log(total), logs)
        attention[:, start : start + pair] = jnp.where(is_first, outs[0], outs[1]).astype(BF16)
    totals[...] = logs
    wait_all(copies)
    result = tokens[...].astype(F32) + dot_nn(attention[...], weight[...])
    hidden[...] = result
    normed, _ = norm_parts(result)
    xn2[...] = (normed * gains[1:2, :]).astype(BF16)


def lift_kernel(place, xn2, grad_out, *refs):
    pieces, rest = (refs[:PIECES], refs[PIECES:])
    keep_one, send_one, keep_two, send_two, slope_gate, active, weight, sems = rest
    me = place[0]
    cols = active.shape[1]
    wait_all(fill(pieces, weight, sems, me, pl.ds(0, 2 * cols)))
    gelu_input = dot_nn(xn2[...], weight[:, :cols])
    gate_part = dot_nn(xn2[...], weight[:, cols:])
    cdf_part = 0.5 * (1.0 + lax.erf(gelu_input * (1.0 / math.sqrt(2.0))))
    density = jnp.exp(-0.5 * gelu_input * gelu_input) * (1.0 / math.sqrt(2.0 * math.pi))
    activated = gelu_input * cdf_part
    active[...] = activated
    slope_gate[...] = gate_part * (cdf_part + gelu_input * density)
    gated = (activated * gate_part).astype(BF16)
    cut = keep_one.shape[1] - xn2.shape[1] // 2
    pack(keep_one, send_one, grad_out, gated[:, :cut], X_BIT, Y_BIT, me)
    pack(keep_two, send_two, grad_out, gated[:, cut:], Y_BIT, X_BIT, me)


def contract_kernel(place, gated_one, gated_two, grad_out, xn2, hidden, slope_gate, active, *refs):
    pieces, rest = (refs[:PIECES], refs[PIECES:])
    layer_out, keep_one, send_one, keep_two, send_two, weight, sems = rest
    me = place[0]
    cols = weight.shape[1]
    wait_all(fill(pieces, weight, sems, me, pl.ds(2 * cols, cols)))
    d_gated = dot_nn(grad_out[...], weight[...])
    pack(keep_one, send_one, xn2, (d_gated * slope_gate[...]).astype(BF16), Y_BIT, X_BIT, me)
    pack(keep_two, send_two, xn2, (d_gated * active[...]).astype(BF16), X_BIT, Y_BIT, me)
    skip = xn2.shape[1] // 2
    cut = gated_one.shape[1] - skip
    down = dot_nt(gated_one[:, skip:], weight[:, :cut]) + dot_nt(gated_two[:, skip:], weight[:, cut:])
    layer_out[...] = (hidden[...] + down).astype(BF16)


def hidden_back_kernel(place, pack_one, pack_two, grad_out, hidden, gains, *refs):
    first, third = (refs[:PIECES], refs[PIECES : 2 * PIECES])
    d_hidden, d_attention, gain_grad, lift_weight, weight, sems, sems_three = refs[2 * PIECES :]
    me = place[0]
    width = hidden.shape[1]
    copies = fill(first, lift_weight, sems, me, pl.ds(0, lift_weight.shape[1]))
    lasts = fill(third, weight, sems_three, me, pl.ds(3 * width, width))
    normed, scaled = norm_parts(hidden[...])
    wait_all(copies)
    cols = lift_weight.shape[1] // 2
    d_xn2 = dot_nt(pack_one[:, width // 2 :], lift_weight[:, :cols])
    d_xn2 = d_xn2 + dot_nt(pack_two[:, width // 2 :], lift_weight[:, cols:])
    d_norm, gain_term = norm_back(d_xn2, normed, scaled, gains[1:2, :])
    gain_grad[...] = gain_term
    total = grad_out[...].astype(F32) + d_norm
    d_hidden[...] = total
    rounded = total.astype(BF16)
    wait_all(lasts)
    d_attention[...] = dot_nt(rounded, weight[...]).astype(BF16)


def attend_back_kernel(
    place, queries, keys_values, edge, bias, totals, d_attention, cosine, sine, d_turned, d_keys_values, d_edge
):
    width = queries.shape[1]
    pair = 2 * HEAD_DIM
    factor = 1.0 / math.sqrt(HEAD_DIM)
    rows = queries.shape[0]
    is_first = head_masks((rows, pair))
    is_first_key = head_masks((rows + edge.shape[0], pair))
    for start in range(0, width, pair):
        here = slice(start, start + pair)
        there = slice(width + start, width + start + pair)
        two = queries[:, here]
        d_two = d_attention[:, here]
        keys = jnp.concatenate([keys_values[:, here], edge[:, here]], axis=0)
        vals = jnp.concatenate([keys_values[:, there], edge[:, there]], axis=0)
        d_queries, d_keys, d_vals = ([], [], [])
        for which in range(2):
            mask = is_first if which == 0 else jnp.logical_not(is_first)
            one = jnp.where(mask, two, jnp.zeros_like(two))
            d_one = jnp.where(mask, d_two, jnp.zeros_like(d_two))
            head = 2 * (start // pair) + which
            scores = dot_nt(one, keys) * factor + bias[...]
            recomputed = jnp.exp(scores - totals[:, head : head + 1])
            d_soft = dot_nt(d_one, vals)
            center = jnp.sum(recomputed * d_soft, axis=-1, keepdims=True)
            d_scores = (recomputed * (d_soft - center) * factor).astype(BF16)
            d_queries.append(dot_nn(d_scores, keys))
            d_keys.append(dot_tt(d_scores, two))
            d_vals.append(dot_tt(recomputed.astype(BF16), d_two))
        d_query = jnp.where(is_first, d_queries[0], d_queries[1])
        d_turned[:, here] = turn(d_query, cosine[...], -sine[...]).astype(BF16)
        d_key = jnp.where(is_first_key, d_keys[0], d_keys[1])
        d_val = jnp.where(is_first_key, d_vals[0], d_vals[1])
        d_keys_values[:, here] = d_key[:rows]
        d_keys_values[:, there] = d_val[:rows]
        d_edge[:, here] = d_key[rows:].astype(BF16)
        d_edge[:, there] = d_val[rows:].astype(BF16)


def keys_back_kernel(
    place, d_queries, d_keys_values, arrived, cosine, sine, xn1, keep_one, send_one, keep_two, send_two, summed, d_turned
):
    me, along = (place[0], place[1])
    width = xn1.shape[1]
    pair = 2 * HEAD_DIM
    rows = arrived.shape[0]
    summed[...] = d_keys_values[...]
    where = pl.ds(pl.multiple_of((1 - along) * rows, rows), rows)
    summed[where, :] = summed[where, :] + arrived[...].astype(F32)
    for start in range(0, width, pair):
        here = slice(start, start + pair)
        there = slice(width + start, width + start + pair)
        d_turned[:, there] = turn(summed[:, here], cosine[...], -sine[...]).astype(BF16)
    d_turned[:, :width] = d_queries[...]
    d_turned[:, 2 * width :] = summed[:, width:].astype(BF16)
    middle = d_turned.shape[1] // 2
    pack(keep_one, send_one, xn1, d_turned[:, :middle], X_BIT, Y_BIT, me)
    pack(keep_two, send_two, xn1, d_turned[:, middle:], Y_BIT, X_BIT, me)


def tokens_back_kernel(place, pack_one, pack_two, tokens, attention, d_hidden, gains, mlp_term, *refs):
    pieces, (keep, send, input_grad, weight, sems) = (refs[:PIECES], refs[PIECES:])
    rows = tokens.shape[0]
    width = tokens.shape[1]
    copies = fill(pieces, weight, sems, place[0], pl.ds(0, 3 * width))
    normed, scaled = norm_parts(tokens[...].astype(F32))
    wait_all(copies)
    middle = pack_one.shape[1] - width // 2
    d_xn1 = dot_nt(pack_one[:, width // 2 :], weight[:, :middle])
    d_xn1 = d_xn1 + dot_nt(pack_two[:, width // 2 :], weight[:, middle:])
    d_norm, gain_term = norm_back(d_xn1, normed, scaled, gains[0:1, :])
    pack(keep, send, attention, d_hidden[...].astype(BF16), Y_BIT, X_BIT, place[0])
    extra = keep.shape[0] - rows
    line = lax.broadcasted_iota(jnp.int32, (extra, width), 0)
    terms = jnp.where(line == 0, mlp_term[...], jnp.where(line == 1, gain_term, 0.0)).astype(BF16)
    for target in (keep, send):
        target[rows:, : width // 2] = jnp.zeros((extra, width // 2), BF16)
        target[rows:, width // 2 :] = terms
    input_grad[...] = (d_hidden[...] + d_norm).astype(BF16)


def product_kernel(width, rows, chip, other, own, sent, joined, *refs):
    terms, sems = (refs[0] if len(refs) > 1 else None, refs[-1])
    copies = []
    extra = 0 if terms is None else terms.shape[1]
    for index in range(4):
        part, start = ((chip, other)[index // 2], index % 2 * (rows + extra))
        source = part.at[pl.ds(start, rows)]
        copies.append(pltpu.make_async_copy(source, joined.at[pl.ds(index * rows, rows)], sems.at[index]))
        if terms is not None:
            copies.append(
                pltpu.make_async_copy(part.at[pl.ds(start + rows, extra)], terms.at[index], sems.at[4 + index])
            )
    for copy in copies:
        copy.start()
    wait_all(copies)
    block = lambda top, k: joined[2 * rows * top : 2 * rows * (top + 1), k * width : (k + 1) * width]
    right = joined[:, 4 * width :]
    left = jnp.concatenate([block(0, 2), block(1, 3)], axis=0)
    sent[:width] = dot_tt(left, right).astype(BF16)
    left = jnp.concatenate([block(0, 0), block(1, 1)], axis=0)
    own[:width] = dot_tt(left, right)
    if terms is not None:
        total = sum(terms[index, :, 4 * width :].astype(F32) for index in range(4))
        own[width:] = total
        sent[width:] = total.astype(BF16)


def call(kernel, outs, operands, scratch=(), smem=1, anywhere=(), flops=0, size=0):
    specs = []
    for index in range(len(operands)):
        if index < smem:
            specs.append(pl.BlockSpec(memory_space=pltpu.SMEM))
        elif index in anywhere:
            specs.append(pl.BlockSpec(memory_space=pltpu.HBM))
        else:
            specs.append(pl.BlockSpec(memory_space=pltpu.VMEM))
    return pl.pallas_call(
        kernel,
        out_shape=[jax.ShapeDtypeStruct(shape, kind) for shape, kind in outs],
        in_specs=specs,
        out_specs=[pl.BlockSpec(memory_space=pltpu.VMEM)] * len(outs),
        scratch_shapes=list(scratch),
        cost_estimate=pl.CostEstimate(flops=flops, bytes_accessed=size, transcendentals=0),
        compiler_params=pltpu.CompilerParams(vmem_limit_bytes=VMEM_BYTES),
    )(*operands)


def grad_rows(keep, over_link, width, before=(), after=()):
    return products(share(keep, over_link, before), width, after)


def share(keep, over_link, before=()):
    return jnp.concatenate(later([keep, over_link], before), axis=0)


def products(chip, width, after=()):
    rows = chip.shape[0] // 256 * 128
    extra = chip.shape[0] // 2 - rows
    cols = chip.shape[1] - 4 * width
    other = later(swap(chip, CORE_BIT), after)
    scratch = [pltpu.VMEM((4 * rows, 4 * width + cols), BF16)]
    if extra:
        scratch.append(pltpu.VMEM((4, extra, 4 * width + cols), BF16))
    return call(
        lambda *refs: product_kernel(width, rows, *refs),
        [((width + extra, cols), F32), ((width + extra, cols), BF16)],
        [chip, other],
        scratch + [pltpu.SemaphoreType.DMA((8,))],
        smem=0,
        anywhere=(0, 1),
        flops=16 * rows * width * cols,
        size=4 * rows * (4 * width + cols) * 2 + 6 * width * cols,
    )


def line_first(part):
    return lax.ppermute(part.astype(BF16), "replica", [(0, 1), (3, 2)])


def line_pair(part, first):
    return (part + first.astype(F32)).astype(BF16)


def line_middle(pair):
    return lax.ppermute(pair, "replica", [(1, 2), (2, 1)])


def line_total(pair, other):
    return (pair.astype(F32) + other.astype(F32)).astype(BF16)


def line_back(total):
    return lax.ppermute(total, "replica", [(1, 0), (2, 3)])


def line_end(total, back):
    place = lax.axis_index("replica")
    middle = (place == 1) | (place == 2)
    return jnp.where(middle, total, back).astype(F32)


def body_plane(
    tokens,
    input_gain,
    qkv_weight,
    output_weight,
    mlp_gain,
    expand_weight,
    contract_weight,
    positions,
    mask_bias,
    cotangent,
):
    me = lax.axis_index(PLANE)
    along = lax.axis_index("ctx")
    place = jnp.stack([me, along]).astype(jnp.int32)
    shard = qkv_weight.shape[0]
    true_width = expand_weight.shape[1] // 2
    fill_cols = -true_width % 128
    ff_width = true_width + fill_cols
    source, grad_out = (tokens[0], cotangent[0])
    rows, width = source.shape
    gains = jnp.stack([input_gain, mlp_gain], axis=1)
    gains = jnp.pad(gains, ((0, 0), (0, 126)))
    front = jnp.concatenate([qkv_weight, output_weight, gains], axis=1)
    widened = lambda values: jnp.pad(values, ((0, 0), (0, fill_cols)))
    feed = jnp.concatenate(
        [
            widened(expand_weight[:, :true_width]),
            widened(expand_weight[:, true_width:]),
            widened(contract_weight),
        ],
        axis=1,
    )
    fetched = fetch_pieces(front)
    packed = share_pieces(fetched)
    feed_fetched = fetch_pieces(feed, tuple(fetched[3:]))
    cosine, sine = rope_tables(positions[0], HEAD_DIM)
    cosine = jnp.concatenate([cosine[:, 0]] * 4, axis=1)
    sine = jnp.concatenate([-sine[:, 0], sine[:, 0]] * 2, axis=1)
    bias = mask_bias[0]
    bias = jnp.concatenate(
        [bias[:, HALF : HALF + rows], jnp.where(along == 0, bias[:, HALF + rows :], bias[:, :HALF])], axis=1
    )
    sems = pltpu.SemaphoreType.DMA((PIECES,))
    front_cols = front.shape[1]
    queries, keys_values, edge, xn1, full_gains = call(
        front_kernel,
        [((rows, width), BF16), ((rows, 2 * width), BF16), ((HALF, 2 * width), BF16), ((rows, width), BF16), ((8, width), F32)],
        [place, source, cosine, sine] + packed,
        [pltpu.VMEM((width, front_cols), BF16), sems],
        anywhere=range(4, 4 + PIECES),
        flops=6 * rows * width * width,
        size=2 * width * front_cols,
    )
    edge = swap(edge, X_BIT)
    attention, totals, hidden, xn2 = call(
        attend_kernel,
        [((rows, width), BF16), ((rows, 128), F32), ((rows, width), F32), ((rows, width), BF16)],
        [place, queries, keys_values, edge, bias, source, full_gains] + packed,
        [pltpu.VMEM((width, width), BF16), sems],
        anywhere=range(7, 7 + PIECES),
        flops=12 * rows * width * width,
        size=4 * width * width,
    )
    feed_pieces = share_pieces(feed_fetched, xn2)
    half = 4 * shard
    cut = -(-ff_width // 256) * 128
    cuts = [((rows, half + cut), BF16)] * 2 + [((rows, half + ff_width - cut), BF16)] * 2
    keep_c, send_c, keep_d, send_d, slope_gate, active = call(
        lift_kernel,
        cuts + [((rows, ff_width), F32)] * 2,
        [place, xn2, grad_out] + feed_pieces,
        [pltpu.VMEM((width, 2 * ff_width), BF16), sems],
        anywhere=range(3, 3 + PIECES),
        flops=4 * rows * width * ff_width,
        size=4 * width * ff_width,
    )
    layer_out, keep_g, send_g, keep_u, send_u = call(
        contract_kernel,
        [((rows, width), BF16)] + [((rows, half + ff_width), BF16)] * 4,
        [place, keep_c, keep_d, grad_out, xn2, hidden, slope_gate, active] + feed_pieces,
        [pltpu.VMEM((width, ff_width), BF16), sems],
        anywhere=range(8, 8 + PIECES),
        flops=4 * rows * width * ff_width,
        size=2 * width * ff_width,
    )
    d_hidden, d_attention, mlp_term = call(
        hidden_back_kernel,
        [((rows, width), F32), ((rows, width), BF16), ((1, width), F32)],
        [place, keep_g, keep_u, grad_out, hidden, full_gains] + feed_pieces + packed,
        [pltpu.VMEM((width, 2 * ff_width), BF16), pltpu.VMEM((width, width), BF16), sems, sems],
        anywhere=range(6, 6 + 2 * PIECES),
        flops=6 * rows * width * ff_width,
        size=6 * width * ff_width,
    )
    link_c = swap(send_c, X_BIT)
    link_d = swap(send_d, Y_BIT)
    link_g = swap(send_g, Y_BIT)
    link_u = swap(send_u, X_BIT)
    d_queries, d_keys_values, d_edge = call(
        attend_back_kernel,
        [((rows, width), BF16), ((rows, 2 * width), F32), ((HALF, 2 * width), BF16)],
        [place, queries, keys_values, edge, bias, totals, d_attention, cosine, sine],
        flops=20 * rows * width * width,
        size=4 * width * width,
    )
    first_own, first_sent = grad_rows(keep_c, link_c, shard, keep_g, d_edge)
    second_own, second_sent = grad_rows(keep_d, link_d, shard, keep_g, d_edge)
    first_back = swap(first_sent, Y_BIT)
    second_back = swap(second_sent, X_BIT)
    chip_g = share(keep_g, link_g, (first_sent, second_sent))
    chip_u = share(keep_u, link_u, (first_sent, second_sent))
    first_back, second_back = later((first_back, second_back), chip_g, chip_u)
    contract_part = jnp.concatenate(
        [first_own + first_back.astype(F32), second_own + second_back.astype(F32)], axis=1
    )
    contract_first = line_first(contract_part)
    gelu_own, gelu_sent = products(chip_g, shard, contract_part)
    gelu_back = swap(gelu_sent, X_BIT)
    gate_own, gate_sent = products(chip_u, shard, gelu_sent)
    gate_back = swap(gate_sent, Y_BIT)
    d_keys_values = later(d_keys_values, gate_sent)
    keep_kv, send_kv, keep_vk, send_vk = call(
        keys_back_kernel,
        [((rows, half + 3 * width // 2), BF16)] * 4,
        [place, d_queries, d_keys_values, swap(d_edge, X_BIT), cosine, sine, xn1],
        [pltpu.VMEM((rows, 2 * width), F32), pltpu.VMEM((rows, 3 * width), BF16)],
        flops=rows * width,
        size=8 * rows * width,
    )
    link_kv = swap(send_kv, X_BIT)
    link_vk = swap(send_vk, Y_BIT)
    contract_pair = line_pair(contract_part, later(contract_first, keep_kv))
    contract_other = line_middle(contract_pair)
    gelu_part = gelu_own + later(gelu_back, contract_pair).astype(F32)
    gelu_first = line_first(gelu_part)
    gate_part = gate_own + later(gate_back, gelu_part).astype(F32)
    gate_first = line_first(gate_part)
    contract_total = line_total(contract_pair, later(contract_other, gate_part))
    contract_last = line_back(contract_total)
    gelu_pair = line_pair(gelu_part, later(gelu_first, contract_total))
    gelu_other = line_middle(gelu_pair)
    chip_kv = share(keep_kv, link_kv, gelu_pair)
    chip_vk = share(keep_vk, link_vk, gelu_pair)
    low_own, low_sent = products(chip_kv, shard)
    low_back = swap(low_sent, Y_BIT)
    high_own, high_sent = products(chip_vk, shard, low_sent)
    high_back = swap(high_sent, X_BIT)
    d_hidden = later(d_hidden, high_sent)
    keep_o, send_o, input_grad = call(
        tokens_back_kernel,
        [((rows + 16, half + width), BF16)] * 2 + [((rows, width), BF16)],
        [place, keep_kv, keep_vk, source, attention, d_hidden, full_gains, mlp_term] + packed,
        [pltpu.VMEM((width, 3 * width), BF16), sems],
        anywhere=range(8, 8 + PIECES),
        flops=6 * rows * width * width,
        size=6 * width * width,
    )
    link_o = swap(send_o, Y_BIT)
    gelu_total = line_total(gelu_pair, later(gelu_other, keep_o, contract_last))
    gelu_last = line_back(gelu_total)
    gate_pair = line_pair(gate_part, later(gate_first, gelu_total))
    gate_other = line_middle(gate_pair)
    low_part = low_own + later(low_back, gate_pair).astype(F32)
    low_first = line_first(low_part)
    high_part = high_own + later(high_back, low_part).astype(F32)
    high_first = line_first(high_part)
    gate_total = line_total(gate_pair, later(gate_other, high_part))
    gate_last = line_back(gate_total)
    low_pair = line_pair(low_part, later(low_first, gate_total, gelu_last))
    low_other = line_middle(low_pair)
    out_own, out_sent = grad_rows(keep_o, link_o, shard, low_pair)
    out_back = swap(out_sent, X_BIT)
    high_pair = line_pair(high_part, later(high_first, out_sent))
    high_other = line_middle(high_pair)
    out_part = out_own + later(out_back, high_pair).astype(F32)
    out_first = line_first(out_part)
    low_total = line_total(low_pair, later(low_other, out_part))
    low_last = line_back(low_total)
    out_pair = line_pair(out_part, later(out_first, low_total))
    out_other = line_middle(out_pair)
    high_total = line_total(high_pair, later(high_other, out_pair, gate_last))
    high_last = line_back(high_total)
    out_total = line_total(out_pair, later(out_other, high_total))
    out_last = line_back(out_total)
    contract_grad = line_end(contract_total, later(contract_last, high_total))
    gelu_grad = line_end(gelu_total, later(gelu_last, high_total))
    gate_grad = line_end(gate_total, later(gate_last, high_total))
    all_grad = jnp.concatenate([line_end(low_total, low_last), line_end(high_total, high_last)], axis=1)
    out_grad = line_end(out_total, out_last)
    gain_rows = lax.dynamic_slice_in_dim(out_grad[shard : shard + 2], me * shard, shard, axis=1)
    return (
        layer_out[None],
        input_grad[None],
        gain_rows[1],
        all_grad,
        out_grad[:shard],
        gain_rows[0],
        jnp.concatenate([gelu_grad[:, :true_width], gate_grad[:, :true_width]], axis=1),
        contract_grad[:, :true_width],
    )


def solution(mesh):
    in_specs = (
        P(("replica", "fsdp"), "ctx", None),
        P(("fsdp", "ctx")),
        P(("fsdp", "ctx"), None),
        P(("fsdp", "ctx"), None),
        P(("fsdp", "ctx")),
        P(("fsdp", "ctx"), None),
        P(("fsdp", "ctx"), None),
        P(("replica", "fsdp"), "ctx"),
        P(("replica", "fsdp"), "ctx", None),
        P(("replica", "fsdp"), "ctx", None),
    )
    out_specs = (
        P(("replica", "fsdp"), "ctx", None),
        P(("replica", "fsdp"), "ctx", None),
        P(("fsdp", "ctx")),
        P(("fsdp", "ctx"), None),
        P(("fsdp", "ctx"), None),
        P(("fsdp", "ctx")),
        P(("fsdp", "ctx"), None),
        P(("fsdp", "ctx"), None),
    )
    sizes = (mesh.shape["replica"], mesh.shape["fsdp"], mesh.shape["ctx"])
    body = body_plane if sizes == (4, 4, 2) else body_generic
    return jax.shard_map(body, mesh=mesh, in_specs=in_specs, out_specs=out_specs, check_vma=False)
```

```python
import math

import jax
import jax.numpy as jnp
from jax import lax
from jax.experimental import pallas as pl
from jax.experimental.pallas import tpu as pltpu
from jax.sharding import PartitionSpec as P

HEAD_DIM = 64
HALF = 64


EPS = 1e-05
THETA = 10000.0


def extended_2(cells, sides, width):
    for axis, dim in sides:
        count = lax.axis_size(axis)
        ends = count - 1
        head = lax.slice_in_dim(cells, 0, width, axis=dim)
        tail = lax.slice_in_dim(cells, cells.shape[dim] - width, cells.shape[dim], axis=dim)
        cells = jnp.concatenate(
            [
                lax.ppermute(tail, axis, [(i, (i + 1) % count) for i in range(ends)]),
                cells,
                lax.ppermute(head, axis, [((i + 1) % count, i) for i in range(ends)]),
            ],
            axis=dim,
        )
    return cells


def from_behind(value, axis, steps):
    count = lax.axis_size(axis)
    first, last = (max(0, -steps), min(count, count - steps))
    return lax.ppermute(value, axis, [(source, source + steps) for source in range(first, last)])


def layer_norm(values, gain):
    center = values - jnp.mean(values, axis=-1, keepdims=True)
    variance = jnp.mean(center * center, axis=-1, keepdims=True)
    scaled = lax.rsqrt(variance + EPS)
    normed = center * scaled
    return (normed, scaled, (normed * gain.astype(jnp.float32)).astype(jnp.bfloat16))


def layer_norm_back(incoming, normed, scaled, gain):
    weighted = incoming * gain.astype(jnp.float32)
    gain_grad = jnp.sum(incoming * normed, axis=0)
    mean_one = jnp.mean(weighted, axis=-1, keepdims=True)
    mean_two = jnp.mean(weighted * normed, axis=-1, keepdims=True)
    return (scaled * (weighted - mean_one - normed * mean_two), gain_grad)


def rope_tables(positions, head_size):
    half_dim = head_size // 2
    exponent = jnp.arange(half_dim, dtype=jnp.float32) * (2.0 / head_size)
    frequency = jnp.exp(-math.log(THETA) * exponent)
    angles = positions.astype(jnp.float32)[:, None] * frequency[None, :]
    return (jnp.cos(angles)[:, None, :], jnp.sin(angles)[:, None, :])


def rotate(values, cosine, sine):
    half_dim = values.shape[-1] // 2
    lower_half, upper_half = (values[..., :half_dim], values[..., half_dim:])
    return jnp.concatenate(
        [lower_half * cosine - upper_half * sine, upper_half * cosine + lower_half * sine], axis=-1
    )


def rotate_back(values, cosine, sine):
    half_dim = values.shape[-1] // 2
    lower_half, upper_half = (values[..., :half_dim], values[..., half_dim:])
    return jnp.concatenate(
        [lower_half * cosine + upper_half * sine, upper_half * cosine - lower_half * sine], axis=-1
    )


def gelu_slope(values):
    cdf_part = 0.5 * (1.0 + jax.scipy.special.erf(values * (1.0 / math.sqrt(2.0))))
    density = jnp.exp(-0.5 * values * values) * (1.0 / math.sqrt(2.0 * math.pi))
    return cdf_part + values * density


def block_scores(queries, key_rows, additive):
    factor = 1.0 / math.sqrt(queries.shape[-1])
    scores = jnp.einsum("qhd,khd->hqk", queries, key_rows, preferred_element_type=jnp.float32)
    return scores * factor + additive[None]


def attend(queries, key_rows, value_rows, additive):
    scores = block_scores(queries, key_rows, additive)
    row_peak = jnp.max(scores, axis=-1, keepdims=True)
    exponent = jnp.exp(scores - row_peak)
    row_total = jnp.sum(exponent, axis=-1, keepdims=True)
    soft_weights = (exponent / row_total).astype(jnp.bfloat16)
    mixed = jnp.einsum("hqk,khd->qhd", soft_weights, value_rows, preferred_element_type=jnp.float32)
    return (mixed.astype(jnp.bfloat16), row_peak[..., 0] + jnp.log(row_total[..., 0]))


def attend_back(queries, key_rows, value_rows, additive, log_total, d_mixed):
    factor = 1.0 / math.sqrt(queries.shape[-1])
    scores = block_scores(queries, key_rows, additive)
    recomputed = jnp.exp(scores - log_total[..., None])
    d_soft = jnp.einsum("qhd,khd->hqk", d_mixed, value_rows, preferred_element_type=jnp.float32)
    center = jnp.sum(recomputed * d_soft, axis=-1, keepdims=True)
    d_scores = (recomputed * (d_soft - center) * factor).astype(jnp.bfloat16)
    d_queries = jnp.einsum("hqk,khd->qhd", d_scores, key_rows, preferred_element_type=jnp.float32)
    d_keys = jnp.einsum("hqk,qhd->khd", d_scores, queries, preferred_element_type=jnp.float32)
    d_values = jnp.einsum(
        "hqk,qhd->khd", recomputed.astype(jnp.bfloat16), d_mixed, preferred_element_type=jnp.float32
    )
    return (d_queries, d_keys, d_values)


def body_generic(
    tokens,
    input_gain,
    qkv_weight,
    output_weight,
    mlp_gain,
    expand_weight,
    contract_weight,
    positions,
    mask_bias,
    cotangent,
):
    gathered = (
        lax.all_gather(input_gain, ("fsdp", "ctx"), axis=0, tiled=True),
        lax.all_gather(qkv_weight, ("fsdp", "ctx"), axis=0, tiled=True),
        lax.all_gather(output_weight, ("fsdp", "ctx"), axis=0, tiled=True),
        lax.all_gather(mlp_gain, ("fsdp", "ctx"), axis=0, tiled=True),
        lax.all_gather(expand_weight, ("fsdp", "ctx"), axis=0, tiled=True),
        lax.all_gather(contract_weight, ("fsdp", "ctx"), axis=0, tiled=True),
    )
    full_input_gain, full_qkv, full_output, full_mlp_gain, full_expand, full_contract = gathered
    residual = tokens[0].astype(jnp.float32)
    row_count, model_width = residual.shape
    head_count = model_width // HEAD_DIM
    cosine, sine = rope_tables(positions[0], HEAD_DIM)
    normed1, scaled1, xn1 = layer_norm(residual, full_input_gain)
    projected = jnp.dot(xn1, full_qkv, preferred_element_type=jnp.float32).reshape(
        row_count, 3, head_count, HEAD_DIM
    )
    queries = rotate(projected[:, 0], cosine, sine).astype(jnp.bfloat16)
    key_rows = rotate(projected[:, 1], cosine, sine).astype(jnp.bfloat16)
    value_rows = projected[:, 2].astype(jnp.bfloat16)
    packed = jnp.concatenate(
        [key_rows.reshape(row_count, model_width), value_rows.reshape(row_count, model_width)],
        axis=1,
    )
    extended = extended_2(packed, (("ctx", 0),), HALF)
    extent = extended.shape[0]
    key_ext = extended[:, :model_width].reshape(extent, head_count, HEAD_DIM)
    value_ext = extended[:, model_width:].reshape(extent, head_count, HEAD_DIM)
    additive = mask_bias[0]
    mixed, log_total = attend(queries, key_ext, value_ext, additive)
    attention = mixed.reshape(row_count, model_width)
    hidden = residual + jnp.dot(attention, full_output, preferred_element_type=jnp.float32)
    normed2, scaled2, xn2 = layer_norm(hidden, full_mlp_gain)
    lifted = jnp.dot(xn2, full_expand, preferred_element_type=jnp.float32)
    ff_width = lifted.shape[1] // 2
    gelu_input = lifted[:, :ff_width]
    gate_part = lifted[:, ff_width:]
    activated = jax.nn.gelu(gelu_input, approximate=False)
    gated = (activated * gate_part).astype(jnp.bfloat16)
    down_out = jnp.einsum("tf,jf->tj", gated, full_contract, preferred_element_type=jnp.float32)
    layer_out = (hidden + down_out).astype(jnp.bfloat16)
    back_input_gain, back_qkv, back_output, back_mlp_gain, back_expand, back_contract = gathered
    grad_out = cotangent[0]
    d_gated = jnp.dot(grad_out, back_contract, preferred_element_type=jnp.float32)
    d_lifted = jnp.concatenate(
        [d_gated * gate_part * gelu_slope(gelu_input), d_gated * activated], axis=1
    ).astype(jnp.bfloat16)
    d_xn2 = jnp.einsum("tc,dc->td", d_lifted, back_expand, preferred_element_type=jnp.float32)
    d_norm2, mlp_gain_term = layer_norm_back(d_xn2, normed2, scaled2, back_mlp_gain)
    d_hidden = grad_out.astype(jnp.float32) + d_norm2
    d_proj = d_hidden.astype(jnp.bfloat16)
    d_attention = jnp.einsum(
        "tj,ij->ti", d_proj, back_output, preferred_element_type=jnp.float32
    ).astype(jnp.bfloat16)
    d_queries, d_key_ext, d_value_ext = attend_back(
        queries,
        key_ext,
        value_ext,
        additive,
        log_total,
        d_attention.reshape(row_count, head_count, HEAD_DIM),
    )
    grad_ext = jnp.concatenate(
        [d_key_ext.reshape(extent, model_width), d_value_ext.reshape(extent, model_width)], axis=1
    )
    from_next = from_behind(grad_ext[:HALF], "ctx", -1)
    from_prev = from_behind(grad_ext[row_count + HALF :], "ctx", 1)
    grad_kv = grad_ext[HALF : HALF + row_count]
    grad_kv = grad_kv + jnp.pad(from_prev, ((0, row_count - HALF), (0, 0)))
    grad_kv = grad_kv + jnp.pad(from_next, ((row_count - HALF, 0), (0, 0)))
    d_keys = rotate_back(
        grad_kv[:, :model_width].reshape(row_count, head_count, HEAD_DIM), cosine, sine
    )
    d_values = grad_kv[:, model_width:]
    d_queries = rotate_back(d_queries, cosine, sine)
    d_projected = jnp.concatenate(
        [
            d_queries.reshape(row_count, model_width),
            d_keys.reshape(row_count, model_width),
            d_values,
        ],
        axis=1,
    ).astype(jnp.bfloat16)
    d_xn1 = jnp.einsum("tc,dc->td", d_projected, back_qkv, preferred_element_type=jnp.float32)
    d_norm1, input_gain_term = layer_norm_back(d_xn1, normed1, scaled1, back_input_gain)
    input_grad = (d_hidden + d_norm1).astype(jnp.bfloat16)
    left_one, left_two, left_three, left_four = (xn1, attention, xn2, grad_out)
    gain_one, gain_two = (input_gain_term, mlp_gain_term)
    qkv_term = jnp.einsum("ti,tj->ij", left_one, d_projected, preferred_element_type=jnp.float32)
    output_term = jnp.einsum("ti,tj->ij", left_two, d_proj, preferred_element_type=jnp.float32)
    expand_term = jnp.einsum("ti,tj->ij", left_three, d_lifted, preferred_element_type=jnp.float32)
    contract_term = jnp.einsum("ti,tj->ij", left_four, gated, preferred_element_type=jnp.float32)
    first_gain = gain_one[:, None]
    second_gain = gain_two[:, None]
    shares = lax.psum_scatter(
        jnp.concatenate(
            [qkv_term, output_term, expand_term, contract_term, first_gain, second_gain], axis=1
        ),
        ("fsdp", "ctx"),
        scatter_dimension=0,
        tiled=True,
    )
    result = lax.psum(shares, "replica")
    qkv_cols = 3 * model_width
    expand_cols = 2 * ff_width
    qkv_grad = result[:, :qkv_cols]
    output_grad = result[:, qkv_cols : qkv_cols + model_width]
    offset = qkv_cols + model_width
    expand_grad = result[:, offset : offset + expand_cols]
    offset = offset + expand_cols
    contract_grad = result[:, offset : offset + ff_width]
    offset = offset + ff_width
    input_gain_grad = result[:, offset]
    mlp_gain_grad = result[:, offset + 1]
    return (
        layer_out[None],
        input_grad[None],
        input_gain_grad,
        qkv_grad,
        output_grad,
        mlp_gain_grad,
        expand_grad,
        contract_grad,
    )


X_BIT, CORE_BIT, Y_BIT = (1, 2, 4)
PLANE = ("fsdp", "ctx")
PLANE_SIZE = 8
PIECES = 10
VMEM_BYTES = 50 * 1024 * 1024
F32, BF16 = (jnp.float32, jnp.bfloat16)


def swap(value, bit):
    return lax.ppermute(value, PLANE, [(i, i ^ bit) for i in range(PLANE_SIZE)])


def later(value, *others):
    return lax.optimization_barrier((value, others))[0]


def fetch_pieces(own, after=()):
    own = later(own, after)
    half = own.shape[0] // 2
    over_x = swap(own, X_BIT)
    over_y = swap(own, Y_BIT)
    return [own, over_x, over_y, swap(over_x[:half], Y_BIT), swap(over_y[half:], X_BIT)]


def share_pieces(first, after=()):
    corners = [swap(later(part, after), CORE_BIT) for part in first[3:]]
    return first + [swap(part, CORE_BIT) for part in first[:3]] + corners


def fill(pieces, target, sems, me, columns=None):
    shard = target.shape[0] // PLANE_SIZE
    half = shard // 2
    corner = X_BIT | Y_BIT
    places = [(0, 0, shard), (X_BIT, 0, shard), (Y_BIT, 0, shard), (corner, 0, half), (corner, half, half)]
    places = places + [(offset | CORE_BIT, start, rows) for offset, start, rows in places]
    copies = []
    for index, (piece, (offset, start, rows)) in enumerate(zip(pieces, places)):
        row = pl.multiple_of((me ^ offset) * shard + start, half)
        source = piece if columns is None else piece.at[:, columns]
        copies.append(pltpu.make_async_copy(source, target.at[pl.ds(row, rows)], sems.at[index]))
    for copy in copies:
        copy.start()
    return copies


def wait_all(copies):
    for copy in copies:
        copy.wait()


def pack(keep, send, left, right, gather_bit, sum_bit, me):
    rows, width = (left.shape[0], left.shape[1] // PLANE_SIZE)
    for slot, offset in enumerate([0, CORE_BIT, sum_bit, CORE_BIT | sum_bit]):
        for target, flip in ((keep, 0), (send, gather_bit)):
            source = pl.multiple_of((me ^ (offset | flip)) * width, width)
            target[:rows, slot * width : (slot + 1) * width] = left[:, pl.ds(source, width)]
    keep[:rows, 4 * width :] = right
    send[:rows, 4 * width :] = right


def turn(values, cosine, sine):
    lane = lax.broadcasted_iota(jnp.int32, values.shape, 1)
    low = lane % HEAD_DIM < HEAD_DIM // 2
    other = jnp.where(
        low,
        pltpu.roll(values, values.shape[1] - HEAD_DIM // 2, 1),
        pltpu.roll(values, HEAD_DIM // 2, 1),
    )
    return values * cosine + other * sine


def dot_tt(one, two):
    return lax.dot_general(one, two, (((0,), (0,)), ((), ())), preferred_element_type=F32)


def dot_nt(one, two):
    return lax.dot_general(one, two, (((1,), (1,)), ((), ())), preferred_element_type=F32)


def dot_nn(one, two):
    return jnp.dot(one, two, preferred_element_type=F32)


def norm_parts(values):
    center = values - jnp.mean(values, axis=-1, keepdims=True)
    variance = jnp.mean(center * center, axis=-1, keepdims=True)
    scaled = lax.rsqrt(variance + EPS)
    return (center * scaled, scaled)


def norm_back(incoming, normed, scaled, gain):
    weighted = incoming * gain
    gain_grad = jnp.sum(incoming * normed, axis=0, keepdims=True)
    mean_one = jnp.mean(weighted, axis=-1, keepdims=True)
    mean_two = jnp.mean(weighted * normed, axis=-1, keepdims=True)
    return (scaled * (weighted - mean_one - normed * mean_two), gain_grad)


def front_kernel(place, tokens, cosine, sine, *refs):
    pieces, (queries, keys_values, edge, xn1, gains, weight, sems) = (refs[:PIECES], refs[PIECES:])
    me, along = (place[0], place[1])
    copies = fill(pieces, weight, sems, me)
    normed, _ = norm_parts(tokens[...].astype(F32))
    width = tokens.shape[1]
    wait_all(copies)
    turned = weight[:, 4 * width :].astype(F32).T
    gains[...] = turned[: gains.shape[0]]
    rounded = (normed * gains[0:1, :]).astype(BF16)
    xn1[...] = rounded
    pair = cosine.shape[1]
    projected = dot_nn(rounded, weight[:, : 3 * width])
    for start in range(0, width, pair):
        part = projected[:, start : start + pair]
        queries[:, start : start + pair] = turn(part, cosine[...], sine[...]).astype(BF16)
        part = projected[:, width + start : width + start + pair]
        keys_values[:, start : start + pair] = turn(part, cosine[...], sine[...]).astype(BF16)
    keys_values[:, width:] = projected[:, 2 * width :].astype(BF16)
    rows = edge.shape[0]
    edge[...] = keys_values[pl.ds(pl.multiple_of((1 - along) * rows, rows), rows), :]


def head_masks(shape):
    lane = lax.broadcasted_iota(jnp.int32, shape, 1)
    return lane < HEAD_DIM


def attend_kernel(place, queries, keys_values, edge, bias, tokens, gains, *refs):
    pieces, (attention, totals, hidden, xn2, weight, sems) = (refs[:PIECES], refs[PIECES:])
    width = tokens.shape[1]
    copies = fill(pieces, weight, sems, place[0], pl.ds(3 * width, width))
    pair = 2 * HEAD_DIM
    factor = 1.0 / math.sqrt(HEAD_DIM)
    rows = queries.shape[0]
    is_first = head_masks((rows, pair))
    lane = lax.broadcasted_iota(jnp.int32, totals.shape, 1)
    logs = jnp.zeros(totals.shape, F32)
    for start in range(0, width, pair):
        two = queries[:, start : start + pair]
        keys = jnp.concatenate([keys_values[:, start : start + pair], edge[:, start : start + pair]], axis=0)
        vals = jnp.concatenate(
            [keys_values[:, width + start : width + start + pair], edge[:, width + start : width + start + pair]],
            axis=0,
        )
        outs = []
        for which in range(2):
            mask = is_first if which == 0 else jnp.logical_not(is_first)
            one = jnp.where(mask, two, jnp.zeros_like(two))
            scores = dot_nt(one, keys) * factor + bias[...]
            peak = jnp.max(scores, axis=-1, keepdims=True)
            exponent = jnp.exp(scores - peak)
            total = jnp.sum(exponent, axis=-1, keepdims=True)
            soft = (exponent / total).astype(BF16)
            outs.append(dot_nn(soft, vals))
            logs = jnp.where(lane == 2 * (start // pair) + which, peak + jnp.log(total), logs)
        attention[:, start : start + pair] = jnp.where(is_first, outs[0], outs[1]).astype(BF16)
    totals[...] = logs
    wait_all(copies)
    result = tokens[...].astype(F32) + dot_nn(attention[...], weight[...])
    hidden[...] = result
    normed, _ = norm_parts(result)
    xn2[...] = (normed * gains[1:2, :]).astype(BF16)


def lift_kernel(place, xn2, grad_out, *refs):
    pieces, rest = (refs[:PIECES], refs[PIECES:])
    keep_one, send_one, keep_two, send_two, slope_gate, active, weight, sems = rest
    me = place[0]
    cols = active.shape[1]
    wait_all(fill(pieces, weight, sems, me, pl.ds(0, 2 * cols)))
    gelu_input = dot_nn(xn2[...], weight[:, :cols])
    gate_part = dot_nn(xn2[...], weight[:, cols:])
    cdf_part = 0.5 * (1.0 + lax.erf(gelu_input * (1.0 / math.sqrt(2.0))))
    density = jnp.exp(-0.5 * gelu_input * gelu_input) * (1.0 / math.sqrt(2.0 * math.pi))
    activated = gelu_input * cdf_part
    active[...] = activated
    slope_gate[...] = gate_part * (cdf_part + gelu_input * density)
    gated = (activated * gate_part).astype(BF16)
    cut = keep_one.shape[1] - xn2.shape[1] // 2
    pack(keep_one, send_one, grad_out, gated[:, :cut], X_BIT, Y_BIT, me)
    pack(keep_two, send_two, grad_out, gated[:, cut:], Y_BIT, X_BIT, me)


def contract_kernel(place, gated_one, gated_two, grad_out, xn2, hidden, slope_gate, active, *refs):
    pieces, rest = (refs[:PIECES], refs[PIECES:])
    layer_out, keep_one, send_one, keep_two, send_two, weight, sems = rest
    me = place[0]
    cols = weight.shape[1]
    wait_all(fill(pieces, weight, sems, me, pl.ds(2 * cols, cols)))
    d_gated = dot_nn(grad_out[...], weight[...])
    pack(keep_one, send_one, xn2, (d_gated * slope_gate[...]).astype(BF16), Y_BIT, X_BIT, me)
    pack(keep_two, send_two, xn2, (d_gated * active[...]).astype(BF16), X_BIT, Y_BIT, me)
    skip = xn2.shape[1] // 2
    cut = gated_one.shape[1] - skip
    down = dot_nt(gated_one[:, skip:], weight[:, :cut]) + dot_nt(gated_two[:, skip:], weight[:, cut:])
    layer_out[...] = (hidden[...] + down).astype(BF16)


def hidden_back_kernel(place, pack_one, pack_two, grad_out, hidden, gains, *refs):
    first, third = (refs[:PIECES], refs[PIECES : 2 * PIECES])
    d_hidden, d_attention, gain_grad, lift_weight, weight, sems, sems_three = refs[2 * PIECES :]
    me = place[0]
    width = hidden.shape[1]
    copies = fill(first, lift_weight, sems, me, pl.ds(0, lift_weight.shape[1]))
    lasts = fill(third, weight, sems_three, me, pl.ds(3 * width, width))
    normed, scaled = norm_parts(hidden[...])
    wait_all(copies)
    cols = lift_weight.shape[1] // 2
    d_xn2 = dot_nt(pack_one[:, width // 2 :], lift_weight[:, :cols])
    d_xn2 = d_xn2 + dot_nt(pack_two[:, width // 2 :], lift_weight[:, cols:])
    d_norm, gain_term = norm_back(d_xn2, normed, scaled, gains[1:2, :])
    gain_grad[...] = gain_term
    total = grad_out[...].astype(F32) + d_norm
    d_hidden[...] = total
    rounded = total.astype(BF16)
    wait_all(lasts)
    d_attention[...] = dot_nt(rounded, weight[...]).astype(BF16)


def attend_back_kernel(
    place, queries, keys_values, edge, bias, totals, d_attention, cosine, sine, d_turned, d_keys_values, d_edge
):
    width = queries.shape[1]
    pair = 2 * HEAD_DIM
    factor = 1.0 / math.sqrt(HEAD_DIM)
    rows = queries.shape[0]
    is_first = head_masks((rows, pair))
    is_first_key = head_masks((rows + edge.shape[0], pair))
    for start in range(0, width, pair):
        here = slice(start, start + pair)
        there = slice(width + start, width + start + pair)
        two = queries[:, here]
        d_two = d_attention[:, here]
        keys = jnp.concatenate([keys_values[:, here], edge[:, here]], axis=0)
        vals = jnp.concatenate([keys_values[:, there], edge[:, there]], axis=0)
        d_queries, d_keys, d_vals = ([], [], [])
        for which in range(2):
            mask = is_first if which == 0 else jnp.logical_not(is_first)
            one = jnp.where(mask, two, jnp.zeros_like(two))
            d_one = jnp.where(mask, d_two, jnp.zeros_like(d_two))
            head = 2 * (start // pair) + which
            scores = dot_nt(one, keys) * factor + bias[...]
            recomputed = jnp.exp(scores - totals[:, head : head + 1])
            d_soft = dot_nt(d_one, vals)
            center = jnp.sum(recomputed * d_soft, axis=-1, keepdims=True)
            d_scores = (recomputed * (d_soft - center) * factor).astype(BF16)
            d_queries.append(dot_nn(d_scores, keys))
            d_keys.append(dot_tt(d_scores, two))
            d_vals.append(dot_tt(recomputed.astype(BF16), d_two))
        d_query = jnp.where(is_first, d_queries[0], d_queries[1])
        d_turned[:, here] = turn(d_query, cosine[...], -sine[...]).astype(BF16)
        d_key = jnp.where(is_first_key, d_keys[0], d_keys[1])
        d_val = jnp.where(is_first_key, d_vals[0], d_vals[1])
        d_keys_values[:, here] = d_key[:rows]
        d_keys_values[:, there] = d_val[:rows]
        d_edge[:, here] = d_key[rows:].astype(BF16)
        d_edge[:, there] = d_val[rows:].astype(BF16)


def keys_back_kernel(
    place, d_queries, d_keys_values, arrived, cosine, sine, xn1, keep_one, send_one, keep_two, send_two, summed, d_turned
):
    me, along = (place[0], place[1])
    width = xn1.shape[1]
    pair = 2 * HEAD_DIM
    rows = arrived.shape[0]
    summed[...] = d_keys_values[...]
    where = pl.ds(pl.multiple_of((1 - along) * rows, rows), rows)
    summed[where, :] = summed[where, :] + arrived[...].astype(F32)
    for start in range(0, width, pair):
        here = slice(start, start + pair)
        there = slice(width + start, width + start + pair)
        d_turned[:, there] = turn(summed[:, here], cosine[...], -sine[...]).astype(BF16)
    d_turned[:, :width] = d_queries[...]
    d_turned[:, 2 * width :] = summed[:, width:].astype(BF16)
    middle = d_turned.shape[1] // 2
    pack(keep_one, send_one, xn1, d_turned[:, :middle], X_BIT, Y_BIT, me)
    pack(keep_two, send_two, xn1, d_turned[:, middle:], Y_BIT, X_BIT, me)


def tokens_back_kernel(place, pack_one, pack_two, tokens, attention, d_hidden, gains, mlp_term, *refs):
    pieces, (keep, send, input_grad, weight, sems) = (refs[:PIECES], refs[PIECES:])
    rows = tokens.shape[0]
    width = tokens.shape[1]
    copies = fill(pieces, weight, sems, place[0], pl.ds(0, 3 * width))
    normed, scaled = norm_parts(tokens[...].astype(F32))
    wait_all(copies)
    middle = pack_one.shape[1] - width // 2
    d_xn1 = dot_nt(pack_one[:, width // 2 :], weight[:, :middle])
    d_xn1 = d_xn1 + dot_nt(pack_two[:, width // 2 :], weight[:, middle:])
    d_norm, gain_term = norm_back(d_xn1, normed, scaled, gains[0:1, :])
    pack(keep, send, attention, d_hidden[...].astype(BF16), Y_BIT, X_BIT, place[0])
    extra = keep.shape[0] - rows
    line = lax.broadcasted_iota(jnp.int32, (extra, width), 0)
    terms = jnp.where(line == 0, mlp_term[...], jnp.where(line == 1, gain_term, 0.0)).astype(BF16)
    for target in (keep, send):
        target[rows:, : width // 2] = jnp.zeros((extra, width // 2), BF16)
        target[rows:, width // 2 :] = terms
    input_grad[...] = (d_hidden[...] + d_norm).astype(BF16)


def product_kernel(width, rows, chip, other, own, sent, joined, *refs):
    terms, sems = (refs[0] if len(refs) > 1 else None, refs[-1])
    copies = []
    extra = 0 if terms is None else terms.shape[1]
    for index in range(4):
        part, start = ((chip, other)[index // 2], index % 2 * (rows + extra))
        source = part.at[pl.ds(start, rows)]
        copies.append(pltpu.make_async_copy(source, joined.at[pl.ds(index * rows, rows)], sems.at[index]))
        if terms is not None:
            copies.append(
                pltpu.make_async_copy(part.at[pl.ds(start + rows, extra)], terms.at[index], sems.at[4 + index])
            )
    for copy in copies:
        copy.start()
    wait_all(copies)
    block = lambda top, k: joined[2 * rows * top : 2 * rows * (top + 1), k * width : (k + 1) * width]
    right = joined[:, 4 * width :]
    left = jnp.concatenate([block(0, 2), block(1, 3)], axis=0)
    sent[:width] = dot_tt(left, right).astype(BF16)
    left = jnp.concatenate([block(0, 0), block(1, 1)], axis=0)
    own[:width] = dot_tt(left, right)
    if terms is not None:
        total = sum(terms[index, :, 4 * width :].astype(F32) for index in range(4))
        own[width:] = total
        sent[width:] = total.astype(BF16)


def call(kernel, outs, operands, scratch=(), smem=1, anywhere=(), flops=0, size=0):
    specs = []
    for index in range(len(operands)):
        if index < smem:
            specs.append(pl.BlockSpec(memory_space=pltpu.SMEM))
        elif index in anywhere:
            specs.append(pl.BlockSpec(memory_space=pltpu.HBM))
        else:
            specs.append(pl.BlockSpec(memory_space=pltpu.VMEM))
    return pl.pallas_call(
        kernel,
        out_shape=[jax.ShapeDtypeStruct(shape, kind) for shape, kind in outs],
        in_specs=specs,
        out_specs=[pl.BlockSpec(memory_space=pltpu.VMEM)] * len(outs),
        scratch_shapes=list(scratch),
        cost_estimate=pl.CostEstimate(flops=flops, bytes_accessed=size, transcendentals=0),
        compiler_params=pltpu.CompilerParams(vmem_limit_bytes=VMEM_BYTES),
    )(*operands)


def grad_rows(keep, over_link, width, before=(), after=()):
    return products(share(keep, over_link, before), width, after)


def share(keep, over_link, before=()):
    return jnp.concatenate(later([keep, over_link], before), axis=0)


def products(chip, width, after=()):
    rows = chip.shape[0] // 256 * 128
    extra = chip.shape[0] // 2 - rows
    cols = chip.shape[1] - 4 * width
    other = later(swap(chip, CORE_BIT), after)
    scratch = [pltpu.VMEM((4 * rows, 4 * width + cols), BF16)]
    if extra:
        scratch.append(pltpu.VMEM((4, extra, 4 * width + cols), BF16))
    return call(
        lambda *refs: product_kernel(width, rows, *refs),
        [((width + extra, cols), F32), ((width + extra, cols), BF16)],
        [chip, other],
        scratch + [pltpu.SemaphoreType.DMA((8,))],
        smem=0,
        anywhere=(0, 1),
        flops=16 * rows * width * cols,
        size=4 * rows * (4 * width + cols) * 2 + 6 * width * cols,
    )


def line_first(part):
    return lax.ppermute(part.astype(BF16), "replica", [(0, 1), (3, 2)])


def line_pair(part, first):
    return (part + first.astype(F32)).astype(BF16)


def line_middle(pair):
    return lax.ppermute(pair, "replica", [(1, 2), (2, 1)])


def line_total(pair, other):
    return (pair.astype(F32) + other.astype(F32)).astype(BF16)


def line_back(total):
    return lax.ppermute(total, "replica", [(1, 0), (2, 3)])


def line_end(total, back):
    place = lax.axis_index("replica")
    middle = (place == 1) | (place == 2)
    return jnp.where(middle, total, back).astype(F32)


def body_plane(
    tokens,
    input_gain,
    qkv_weight,
    output_weight,
    mlp_gain,
    expand_weight,
    contract_weight,
    positions,
    mask_bias,
    cotangent,
):
    me = lax.axis_index(PLANE)
    along = lax.axis_index("ctx")
    place = jnp.stack([me, along]).astype(jnp.int32)
    shard = qkv_weight.shape[0]
    true_width = expand_weight.shape[1] // 2
    fill_cols = -true_width % 128
    ff_width = true_width + fill_cols
    source, grad_out = (tokens[0], cotangent[0])
    rows, width = source.shape
    gains = jnp.stack([input_gain, mlp_gain], axis=1)
    gains = jnp.pad(gains, ((0, 0), (0, 126)))
    front = jnp.concatenate([qkv_weight, output_weight, gains], axis=1)
    widened = lambda values: jnp.pad(values, ((0, 0), (0, fill_cols)))
    feed = jnp.concatenate(
        [
            widened(expand_weight[:, :true_width]),
            widened(expand_weight[:, true_width:]),
            widened(contract_weight),
        ],
        axis=1,
    )
    fetched = fetch_pieces(front)
    packed = share_pieces(fetched)
    feed_fetched = fetch_pieces(feed, tuple(fetched[3:]))
    cosine, sine = rope_tables(positions[0], HEAD_DIM)
    cosine = jnp.concatenate([cosine[:, 0]] * 4, axis=1)
    sine = jnp.concatenate([-sine[:, 0], sine[:, 0]] * 2, axis=1)
    bias = mask_bias[0]
    bias = jnp.concatenate(
        [bias[:, HALF : HALF + rows], jnp.where(along == 0, bias[:, HALF + rows :], bias[:, :HALF])], axis=1
    )
    sems = pltpu.SemaphoreType.DMA((PIECES,))
    front_cols = front.shape[1]
    queries, keys_values, edge, xn1, full_gains = call(
        front_kernel,
        [((rows, width), BF16), ((rows, 2 * width), BF16), ((HALF, 2 * width), BF16), ((rows, width), BF16), ((8, width), F32)],
        [place, source, cosine, sine] + packed,
        [pltpu.VMEM((width, front_cols), BF16), sems],
        anywhere=range(4, 4 + PIECES),
        flops=6 * rows * width * width,
        size=2 * width * front_cols,
    )
    edge = swap(edge, X_BIT)
    attention, totals, hidden, xn2 = call(
        attend_kernel,
        [((rows, width), BF16), ((rows, 128), F32), ((rows, width), F32), ((rows, width), BF16)],
        [place, queries, keys_values, edge, bias, source, full_gains] + packed,
        [pltpu.VMEM((width, width), BF16), sems],
        anywhere=range(7, 7 + PIECES),
        flops=12 * rows * width * width,
        size=4 * width * width,
    )
    feed_pieces = share_pieces(feed_fetched, xn2)
    half = 4 * shard
    cut = -(-ff_width // 256) * 128
    cuts = [((rows, half + cut), BF16)] * 2 + [((rows, half + ff_width - cut), BF16)] * 2
    keep_c, send_c, keep_d, send_d, slope_gate, active = call(
        lift_kernel,
        cuts + [((rows, ff_width), F32)] * 2,
        [place, xn2, grad_out] + feed_pieces,
        [pltpu.VMEM((width, 2 * ff_width), BF16), sems],
        anywhere=range(3, 3 + PIECES),
        flops=4 * rows * width * ff_width,
        size=4 * width * ff_width,
    )
    layer_out, keep_g, send_g, keep_u, send_u = call(
        contract_kernel,
        [((rows, width), BF16)] + [((rows, half + ff_width), BF16)] * 4,
        [place, keep_c, keep_d, grad_out, xn2, hidden, slope_gate, active] + feed_pieces,
        [pltpu.VMEM((width, ff_width), BF16), sems],
        anywhere=range(8, 8 + PIECES),
        flops=4 * rows * width * ff_width,
        size=2 * width * ff_width,
    )
    d_hidden, d_attention, mlp_term = call(
        hidden_back_kernel,
        [((rows, width), F32), ((rows, width), BF16), ((1, width), F32)],
        [place, keep_g, keep_u, grad_out, hidden, full_gains] + feed_pieces + packed,
        [pltpu.VMEM((width, 2 * ff_width), BF16), pltpu.VMEM((width, width), BF16), sems, sems],
        anywhere=range(6, 6 + 2 * PIECES),
        flops=6 * rows * width * ff_width,
        size=6 * width * ff_width,
    )
    link_c = swap(send_c, X_BIT)
    link_d = swap(send_d, Y_BIT)
    link_g = swap(send_g, Y_BIT)
    link_u = swap(send_u, X_BIT)
    d_queries, d_keys_values, d_edge = call(
        attend_back_kernel,
        [((rows, width), BF16), ((rows, 2 * width), F32), ((HALF, 2 * width), BF16)],
        [place, queries, keys_values, edge, bias, totals, d_attention, cosine, sine],
        flops=20 * rows * width * width,
        size=4 * width * width,
    )
    first_own, first_sent = grad_rows(keep_c, link_c, shard, keep_g, d_edge)
    second_own, second_sent = grad_rows(keep_d, link_d, shard, keep_g, d_edge)
    first_back = swap(first_sent, Y_BIT)
    second_back = swap(second_sent, X_BIT)
    chip_g = share(keep_g, link_g, (first_sent, second_sent))
    chip_u = share(keep_u, link_u, (first_sent, second_sent))
    first_back, second_back = later((first_back, second_back), chip_g, chip_u)
    contract_part = jnp.concatenate(
        [first_own + first_back.astype(F32), second_own + second_back.astype(F32)], axis=1
    )
    contract_first = line_first(contract_part)
    gelu_own, gelu_sent = products(chip_g, shard, contract_part)
    gelu_back = swap(gelu_sent, X_BIT)
    gate_own, gate_sent = products(chip_u, shard, gelu_sent)
    gate_back = swap(gate_sent, Y_BIT)
    d_keys_values = later(d_keys_values, gate_sent)
    keep_kv, send_kv, keep_vk, send_vk = call(
        keys_back_kernel,
        [((rows, half + 3 * width // 2), BF16)] * 4,
        [place, d_queries, d_keys_values, swap(d_edge, X_BIT), cosine, sine, xn1],
        [pltpu.VMEM((rows, 2 * width), F32), pltpu.VMEM((rows, 3 * width), BF16)],
        flops=rows * width,
        size=8 * rows * width,
    )
    link_kv = swap(send_kv, X_BIT)
    link_vk = swap(send_vk, Y_BIT)
    contract_pair = line_pair(contract_part, later(contract_first, keep_kv))
    contract_other = line_middle(contract_pair)
    gelu_part = gelu_own + later(gelu_back, contract_pair).astype(F32)
    gelu_first = line_first(gelu_part)
    gate_part = gate_own + later(gate_back, gelu_part).astype(F32)
    gate_first = line_first(gate_part)
    contract_total = line_total(contract_pair, later(contract_other, gate_part))
    contract_last = line_back(contract_total)
    gelu_pair = line_pair(gelu_part, later(gelu_first, contract_total))
    gelu_other = line_middle(gelu_pair)
    chip_kv = share(keep_kv, link_kv, gelu_pair)
    chip_vk = share(keep_vk, link_vk, gelu_pair)
    low_own, low_sent = products(chip_kv, shard)
    low_back = swap(low_sent, Y_BIT)
    high_own, high_sent = products(chip_vk, shard, low_sent)
    high_back = swap(high_sent, X_BIT)
    d_hidden = later(d_hidden, high_sent)
    keep_o, send_o, input_grad = call(
        tokens_back_kernel,
        [((rows + 16, half + width), BF16)] * 2 + [((rows, width), BF16)],
        [place, keep_kv, keep_vk, source, attention, d_hidden, full_gains, mlp_term] + packed,
        [pltpu.VMEM((width, 3 * width), BF16), sems],
        anywhere=range(8, 8 + PIECES),
        flops=6 * rows * width * width,
        size=6 * width * width,
    )
    link_o = swap(send_o, Y_BIT)
    gelu_total = line_total(gelu_pair, later(gelu_other, keep_o, contract_last))
    gelu_last = line_back(gelu_total)
    gate_pair = line_pair(gate_part, later(gate_first, gelu_total))
    gate_other = line_middle(gate_pair)
    low_part = low_own + later(low_back, gate_pair).astype(F32)
    low_first = line_first(low_part)
    high_part = high_own + later(high_back, low_part).astype(F32)
    high_first = line_first(high_part)
    gate_total = line_total(gate_pair, later(gate_other, high_part))
    gate_last = line_back(gate_total)
    low_pair = line_pair(low_part, later(low_first, gate_total, gelu_last))
    low_other = line_middle(low_pair)
    out_own, out_sent = grad_rows(keep_o, link_o, shard, high_part)
    out_back = swap(out_sent, X_BIT)
    high_pair = line_pair(high_part, later(high_first, low_pair))
    high_other = line_middle(high_pair)
    out_part = out_own + later(out_back, high_pair, gate_last).astype(F32)
    out_first = line_first(out_part)
    low_total = line_total(low_pair, later(low_other, out_part))
    low_last = line_back(low_total)
    out_pair = line_pair(out_part, later(out_first, low_total))
    out_other = line_middle(out_pair)
    high_total = line_total(high_pair, later(high_other, out_pair))
    high_last = line_back(high_total)
    out_total = line_total(out_pair, later(out_other, high_total))
    out_last = line_back(out_total)
    contract_grad = line_end(contract_total, later(contract_last, high_total))
    gelu_grad = line_end(gelu_total, later(gelu_last, high_total))
    gate_grad = line_end(gate_total, later(gate_last, high_total))
    all_grad = jnp.concatenate([line_end(low_total, low_last), line_end(high_total, high_last)], axis=1)
    out_grad = line_end(out_total, out_last)
    gain_rows = lax.dynamic_slice_in_dim(out_grad[shard : shard + 2], me * shard, shard, axis=1)
    return (
        layer_out[None],
        input_grad[None],
        gain_rows[1],
        all_grad,
        out_grad[:shard],
        gain_rows[0],
        jnp.concatenate([gelu_grad[:, :true_width], gate_grad[:, :true_width]], axis=1),
        contract_grad[:, :true_width],
    )


def solution(mesh):
    in_specs = (
        P(("replica", "fsdp"), "ctx", None),
        P(("fsdp", "ctx")),
        P(("fsdp", "ctx"), None),
        P(("fsdp", "ctx"), None),
        P(("fsdp", "ctx")),
        P(("fsdp", "ctx"), None),
        P(("fsdp", "ctx"), None),
        P(("replica", "fsdp"), "ctx"),
        P(("replica", "fsdp"), "ctx", None),
        P(("replica", "fsdp"), "ctx", None),
    )
    out_specs = (
        P(("replica", "fsdp"), "ctx", None),
        P(("replica", "fsdp"), "ctx", None),
        P(("fsdp", "ctx")),
        P(("fsdp", "ctx"), None),
        P(("fsdp", "ctx"), None),
        P(("fsdp", "ctx")),
        P(("fsdp", "ctx"), None),
        P(("fsdp", "ctx"), None),
    )
    sizes = (mesh.shape["replica"], mesh.shape["fsdp"], mesh.shape["ctx"])
    body = body_plane if sizes == (4, 4, 2) else body_generic
    return jax.shard_map(body, mesh=mesh, in_specs=in_specs, out_specs=out_specs, check_vma=False)
```

```python
import math

import jax
import jax.numpy as jnp
from jax import lax
from jax.experimental import pallas as pl
from jax.experimental.pallas import tpu as pltpu
from jax.sharding import PartitionSpec as P

HEAD_DIM = 64
HALF = 64


EPS = 1e-05
THETA = 10000.0


def extended_2(cells, sides, width):
    for axis, dim in sides:
        count = lax.axis_size(axis)
        ends = count - 1
        head = lax.slice_in_dim(cells, 0, width, axis=dim)
        tail = lax.slice_in_dim(cells, cells.shape[dim] - width, cells.shape[dim], axis=dim)
        cells = jnp.concatenate(
            [
                lax.ppermute(tail, axis, [(i, (i + 1) % count) for i in range(ends)]),
                cells,
                lax.ppermute(head, axis, [((i + 1) % count, i) for i in range(ends)]),
            ],
            axis=dim,
        )
    return cells


def from_behind(value, axis, steps):
    count = lax.axis_size(axis)
    first, last = (max(0, -steps), min(count, count - steps))
    return lax.ppermute(value, axis, [(source, source + steps) for source in range(first, last)])


def layer_norm(values, gain):
    center = values - jnp.mean(values, axis=-1, keepdims=True)
    variance = jnp.mean(center * center, axis=-1, keepdims=True)
    scaled = lax.rsqrt(variance + EPS)
    normed = center * scaled
    return (normed, scaled, (normed * gain.astype(jnp.float32)).astype(jnp.bfloat16))


def layer_norm_back(incoming, normed, scaled, gain):
    weighted = incoming * gain.astype(jnp.float32)
    gain_grad = jnp.sum(incoming * normed, axis=0)
    mean_one = jnp.mean(weighted, axis=-1, keepdims=True)
    mean_two = jnp.mean(weighted * normed, axis=-1, keepdims=True)
    return (scaled * (weighted - mean_one - normed * mean_two), gain_grad)


def rope_tables(positions, head_size):
    half_dim = head_size // 2
    exponent = jnp.arange(half_dim, dtype=jnp.float32) * (2.0 / head_size)
    frequency = jnp.exp(-math.log(THETA) * exponent)
    angles = positions.astype(jnp.float32)[:, None] * frequency[None, :]
    return (jnp.cos(angles)[:, None, :], jnp.sin(angles)[:, None, :])


def rotate(values, cosine, sine):
    half_dim = values.shape[-1] // 2
    lower_half, upper_half = (values[..., :half_dim], values[..., half_dim:])
    return jnp.concatenate(
        [lower_half * cosine - upper_half * sine, upper_half * cosine + lower_half * sine], axis=-1
    )


def rotate_back(values, cosine, sine):
    half_dim = values.shape[-1] // 2
    lower_half, upper_half = (values[..., :half_dim], values[..., half_dim:])
    return jnp.concatenate(
        [lower_half * cosine + upper_half * sine, upper_half * cosine - lower_half * sine], axis=-1
    )


def gelu_slope(values):
    cdf_part = 0.5 * (1.0 + jax.scipy.special.erf(values * (1.0 / math.sqrt(2.0))))
    density = jnp.exp(-0.5 * values * values) * (1.0 / math.sqrt(2.0 * math.pi))
    return cdf_part + values * density


def block_scores(queries, key_rows, additive):
    factor = 1.0 / math.sqrt(queries.shape[-1])
    scores = jnp.einsum("qhd,khd->hqk", queries, key_rows, preferred_element_type=jnp.float32)
    return scores * factor + additive[None]


def attend(queries, key_rows, value_rows, additive):
    scores = block_scores(queries, key_rows, additive)
    row_peak = jnp.max(scores, axis=-1, keepdims=True)
    exponent = jnp.exp(scores - row_peak)
    row_total = jnp.sum(exponent, axis=-1, keepdims=True)
    soft_weights = (exponent / row_total).astype(jnp.bfloat16)
    mixed = jnp.einsum("hqk,khd->qhd", soft_weights, value_rows, preferred_element_type=jnp.float32)
    return (mixed.astype(jnp.bfloat16), row_peak[..., 0] + jnp.log(row_total[..., 0]))


def attend_back(queries, key_rows, value_rows, additive, log_total, d_mixed):
    factor = 1.0 / math.sqrt(queries.shape[-1])
    scores = block_scores(queries, key_rows, additive)
    recomputed = jnp.exp(scores - log_total[..., None])
    d_soft = jnp.einsum("qhd,khd->hqk", d_mixed, value_rows, preferred_element_type=jnp.float32)
    center = jnp.sum(recomputed * d_soft, axis=-1, keepdims=True)
    d_scores = (recomputed * (d_soft - center) * factor).astype(jnp.bfloat16)
    d_queries = jnp.einsum("hqk,khd->qhd", d_scores, key_rows, preferred_element_type=jnp.float32)
    d_keys = jnp.einsum("hqk,qhd->khd", d_scores, queries, preferred_element_type=jnp.float32)
    d_values = jnp.einsum(
        "hqk,qhd->khd", recomputed.astype(jnp.bfloat16), d_mixed, preferred_element_type=jnp.float32
    )
    return (d_queries, d_keys, d_values)


def body_generic(
    tokens,
    input_gain,
    qkv_weight,
    output_weight,
    mlp_gain,
    expand_weight,
    contract_weight,
    positions,
    mask_bias,
    cotangent,
):
    gathered = (
        lax.all_gather(input_gain, ("fsdp", "ctx"), axis=0, tiled=True),
        lax.all_gather(qkv_weight, ("fsdp", "ctx"), axis=0, tiled=True),
        lax.all_gather(output_weight, ("fsdp", "ctx"), axis=0, tiled=True),
        lax.all_gather(mlp_gain, ("fsdp", "ctx"), axis=0, tiled=True),
        lax.all_gather(expand_weight, ("fsdp", "ctx"), axis=0, tiled=True),
        lax.all_gather(contract_weight, ("fsdp", "ctx"), axis=0, tiled=True),
    )
    full_input_gain, full_qkv, full_output, full_mlp_gain, full_expand, full_contract = gathered
    residual = tokens[0].astype(jnp.float32)
    row_count, model_width = residual.shape
    head_count = model_width // HEAD_DIM
    cosine, sine = rope_tables(positions[0], HEAD_DIM)
    normed1, scaled1, xn1 = layer_norm(residual, full_input_gain)
    projected = jnp.dot(xn1, full_qkv, preferred_element_type=jnp.float32).reshape(
        row_count, 3, head_count, HEAD_DIM
    )
    queries = rotate(projected[:, 0], cosine, sine).astype(jnp.bfloat16)
    key_rows = rotate(projected[:, 1], cosine, sine).astype(jnp.bfloat16)
    value_rows = projected[:, 2].astype(jnp.bfloat16)
    packed = jnp.concatenate(
        [key_rows.reshape(row_count, model_width), value_rows.reshape(row_count, model_width)],
        axis=1,
    )
    extended = extended_2(packed, (("ctx", 0),), HALF)
    extent = extended.shape[0]
    key_ext = extended[:, :model_width].reshape(extent, head_count, HEAD_DIM)
    value_ext = extended[:, model_width:].reshape(extent, head_count, HEAD_DIM)
    additive = mask_bias[0]
    mixed, log_total = attend(queries, key_ext, value_ext, additive)
    attention = mixed.reshape(row_count, model_width)
    hidden = residual + jnp.dot(attention, full_output, preferred_element_type=jnp.float32)
    normed2, scaled2, xn2 = layer_norm(hidden, full_mlp_gain)
    lifted = jnp.dot(xn2, full_expand, preferred_element_type=jnp.float32)
    ff_width = lifted.shape[1] // 2
    gelu_input = lifted[:, :ff_width]
    gate_part = lifted[:, ff_width:]
    activated = jax.nn.gelu(gelu_input, approximate=False)
    gated = (activated * gate_part).astype(jnp.bfloat16)
    down_out = jnp.einsum("tf,jf->tj", gated, full_contract, preferred_element_type=jnp.float32)
    layer_out = (hidden + down_out).astype(jnp.bfloat16)
    back_input_gain, back_qkv, back_output, back_mlp_gain, back_expand, back_contract = gathered
    grad_out = cotangent[0]
    d_gated = jnp.dot(grad_out, back_contract, preferred_element_type=jnp.float32)
    d_lifted = jnp.concatenate(
        [d_gated * gate_part * gelu_slope(gelu_input), d_gated * activated], axis=1
    ).astype(jnp.bfloat16)
    d_xn2 = jnp.einsum("tc,dc->td", d_lifted, back_expand, preferred_element_type=jnp.float32)
    d_norm2, mlp_gain_term = layer_norm_back(d_xn2, normed2, scaled2, back_mlp_gain)
    d_hidden = grad_out.astype(jnp.float32) + d_norm2
    d_proj = d_hidden.astype(jnp.bfloat16)
    d_attention = jnp.einsum(
        "tj,ij->ti", d_proj, back_output, preferred_element_type=jnp.float32
    ).astype(jnp.bfloat16)
    d_queries, d_key_ext, d_value_ext = attend_back(
        queries,
        key_ext,
        value_ext,
        additive,
        log_total,
        d_attention.reshape(row_count, head_count, HEAD_DIM),
    )
    grad_ext = jnp.concatenate(
        [d_key_ext.reshape(extent, model_width), d_value_ext.reshape(extent, model_width)], axis=1
    )
    from_next = from_behind(grad_ext[:HALF], "ctx", -1)
    from_prev = from_behind(grad_ext[row_count + HALF :], "ctx", 1)
    grad_kv = grad_ext[HALF : HALF + row_count]
    grad_kv = grad_kv + jnp.pad(from_prev, ((0, row_count - HALF), (0, 0)))
    grad_kv = grad_kv + jnp.pad(from_next, ((row_count - HALF, 0), (0, 0)))
    d_keys = rotate_back(
        grad_kv[:, :model_width].reshape(row_count, head_count, HEAD_DIM), cosine, sine
    )
    d_values = grad_kv[:, model_width:]
    d_queries = rotate_back(d_queries, cosine, sine)
    d_projected = jnp.concatenate(
        [
            d_queries.reshape(row_count, model_width),
            d_keys.reshape(row_count, model_width),
            d_values,
        ],
        axis=1,
    ).astype(jnp.bfloat16)
    d_xn1 = jnp.einsum("tc,dc->td", d_projected, back_qkv, preferred_element_type=jnp.float32)
    d_norm1, input_gain_term = layer_norm_back(d_xn1, normed1, scaled1, back_input_gain)
    input_grad = (d_hidden + d_norm1).astype(jnp.bfloat16)
    left_one, left_two, left_three, left_four = (xn1, attention, xn2, grad_out)
    gain_one, gain_two = (input_gain_term, mlp_gain_term)
    qkv_term = jnp.einsum("ti,tj->ij", left_one, d_projected, preferred_element_type=jnp.float32)
    output_term = jnp.einsum("ti,tj->ij", left_two, d_proj, preferred_element_type=jnp.float32)
    expand_term = jnp.einsum("ti,tj->ij", left_three, d_lifted, preferred_element_type=jnp.float32)
    contract_term = jnp.einsum("ti,tj->ij", left_four, gated, preferred_element_type=jnp.float32)
    first_gain = gain_one[:, None]
    second_gain = gain_two[:, None]
    shares = lax.psum_scatter(
        jnp.concatenate(
            [qkv_term, output_term, expand_term, contract_term, first_gain, second_gain], axis=1
        ),
        ("fsdp", "ctx"),
        scatter_dimension=0,
        tiled=True,
    )
    result = lax.psum(shares, "replica")
    qkv_cols = 3 * model_width
    expand_cols = 2 * ff_width
    qkv_grad = result[:, :qkv_cols]
    output_grad = result[:, qkv_cols : qkv_cols + model_width]
    offset = qkv_cols + model_width
    expand_grad = result[:, offset : offset + expand_cols]
    offset = offset + expand_cols
    contract_grad = result[:, offset : offset + ff_width]
    offset = offset + ff_width
    input_gain_grad = result[:, offset]
    mlp_gain_grad = result[:, offset + 1]
    return (
        layer_out[None],
        input_grad[None],
        input_gain_grad,
        qkv_grad,
        output_grad,
        mlp_gain_grad,
        expand_grad,
        contract_grad,
    )


X_BIT, CORE_BIT, Y_BIT = (1, 2, 4)
PLANE = ("fsdp", "ctx")
PLANE_SIZE = 8
PIECES = 10
VMEM_BYTES = 50 * 1024 * 1024
F32, BF16 = (jnp.float32, jnp.bfloat16)


def swap(value, bit):
    return lax.ppermute(value, PLANE, [(i, i ^ bit) for i in range(PLANE_SIZE)])


def later(value, *others):
    return lax.optimization_barrier((value, others))[0]


def fetch_pieces(own, after=()):
    own = later(own, after)
    half = own.shape[0] // 2
    over_x = swap(own, X_BIT)
    over_y = swap(own, Y_BIT)
    return [own, over_x, over_y, swap(over_x[:half], Y_BIT), swap(over_y[half:], X_BIT)]


def share_pieces(first, after=()):
    corners = [swap(later(part, after), CORE_BIT) for part in first[3:]]
    return first + [swap(part, CORE_BIT) for part in first[:3]] + corners


def fill(pieces, target, sems, me, columns=None):
    shard = target.shape[0] // PLANE_SIZE
    half = shard // 2
    corner = X_BIT | Y_BIT
    places = [(0, 0, shard), (X_BIT, 0, shard), (Y_BIT, 0, shard), (corner, 0, half), (corner, half, half)]
    places = places + [(offset | CORE_BIT, start, rows) for offset, start, rows in places]
    copies = []
    for index, (piece, (offset, start, rows)) in enumerate(zip(pieces, places)):
        row = pl.multiple_of((me ^ offset) * shard + start, half)
        source = piece if columns is None else piece.at[:, columns]
        copies.append(pltpu.make_async_copy(source, target.at[pl.ds(row, rows)], sems.at[index]))
    for copy in copies:
        copy.start()
    return copies


def wait_all(copies):
    for copy in copies:
        copy.wait()


def pack(keep, send, left, right, gather_bit, sum_bit, me):
    rows, width = (left.shape[0], left.shape[1] // PLANE_SIZE)
    for slot, offset in enumerate([0, CORE_BIT, sum_bit, CORE_BIT | sum_bit]):
        for target, flip in ((keep, 0), (send, gather_bit)):
            source = pl.multiple_of((me ^ (offset | flip)) * width, width)
            target[:rows, slot * width : (slot + 1) * width] = left[:, pl.ds(source, width)]
    keep[:rows, 4 * width :] = right
    send[:rows, 4 * width :] = right


def turn(values, cosine, sine):
    lane = lax.broadcasted_iota(jnp.int32, values.shape, 1)
    low = lane % HEAD_DIM < HEAD_DIM // 2
    other = jnp.where(
        low,
        pltpu.roll(values, values.shape[1] - HEAD_DIM // 2, 1),
        pltpu.roll(values, HEAD_DIM // 2, 1),
    )
    return values * cosine + other * sine


def dot_tt(one, two):
    return lax.dot_general(one, two, (((0,), (0,)), ((), ())), preferred_element_type=F32)


def dot_nt(one, two):
    return lax.dot_general(one, two, (((1,), (1,)), ((), ())), preferred_element_type=F32)


def dot_nn(one, two):
    return jnp.dot(one, two, preferred_element_type=F32)


def norm_parts(values):
    center = values - jnp.mean(values, axis=-1, keepdims=True)
    variance = jnp.mean(center * center, axis=-1, keepdims=True)
    scaled = lax.rsqrt(variance + EPS)
    return (center * scaled, scaled)


def norm_back(incoming, normed, scaled, gain):
    weighted = incoming * gain
    gain_grad = jnp.sum(incoming * normed, axis=0, keepdims=True)
    mean_one = jnp.mean(weighted, axis=-1, keepdims=True)
    mean_two = jnp.mean(weighted * normed, axis=-1, keepdims=True)
    return (scaled * (weighted - mean_one - normed * mean_two), gain_grad)


def front_kernel(place, tokens, cosine, sine, *refs):
    pieces, (queries, keys_values, edge, xn1, gains, weight, sems) = (refs[:PIECES], refs[PIECES:])
    me, along = (place[0], place[1])
    copies = fill(pieces, weight, sems, me)
    normed, _ = norm_parts(tokens[...].astype(F32))
    width = tokens.shape[1]
    wait_all(copies)
    turned = weight[:, 4 * width :].astype(F32).T
    gains[...] = turned[: gains.shape[0]]
    rounded = (normed * gains[0:1, :]).astype(BF16)
    xn1[...] = rounded
    pair = cosine.shape[1]
    projected = dot_nn(rounded, weight[:, : 3 * width])
    for start in range(0, width, pair):
        part = projected[:, start : start + pair]
        queries[:, start : start + pair] = turn(part, cosine[...], sine[...]).astype(BF16)
        part = projected[:, width + start : width + start + pair]
        keys_values[:, start : start + pair] = turn(part, cosine[...], sine[...]).astype(BF16)
    keys_values[:, width:] = projected[:, 2 * width :].astype(BF16)
    rows = edge.shape[0]
    edge[...] = keys_values[pl.ds(pl.multiple_of((1 - along) * rows, rows), rows), :]


def head_masks(shape):
    lane = lax.broadcasted_iota(jnp.int32, shape, 1)
    return lane < HEAD_DIM


def attend_kernel(place, queries, keys_values, edge, bias, tokens, gains, *refs):
    pieces, (attention, totals, hidden, xn2, weight, sems) = (refs[:PIECES], refs[PIECES:])
    width = tokens.shape[1]
    copies = fill(pieces, weight, sems, place[0], pl.ds(3 * width, width))
    pair = 2 * HEAD_DIM
    factor = 1.0 / math.sqrt(HEAD_DIM)
    rows = queries.shape[0]
    is_first = head_masks((rows, pair))
    lane = lax.broadcasted_iota(jnp.int32, totals.shape, 1)
    logs = jnp.zeros(totals.shape, F32)
    for start in range(0, width, pair):
        two = queries[:, start : start + pair]
        keys = jnp.concatenate([keys_values[:, start : start + pair], edge[:, start : start + pair]], axis=0)
        vals = jnp.concatenate(
            [keys_values[:, width + start : width + start + pair], edge[:, width + start : width + start + pair]],
            axis=0,
        )
        outs = []
        for which in range(2):
            mask = is_first if which == 0 else jnp.logical_not(is_first)
            one = jnp.where(mask, two, jnp.zeros_like(two))
            scores = dot_nt(one, keys) * factor + bias[...]
            peak = jnp.max(scores, axis=-1, keepdims=True)
            exponent = jnp.exp(scores - peak)
            total = jnp.sum(exponent, axis=-1, keepdims=True)
            soft = (exponent / total).astype(BF16)
            outs.append(dot_nn(soft, vals))
            logs = jnp.where(lane == 2 * (start // pair) + which, peak + jnp.log(total), logs)
        attention[:, start : start + pair] = jnp.where(is_first, outs[0], outs[1]).astype(BF16)
    totals[...] = logs
    wait_all(copies)
    result = tokens[...].astype(F32) + dot_nn(attention[...], weight[...])
    hidden[...] = result
    normed, _ = norm_parts(result)
    xn2[...] = (normed * gains[1:2, :]).astype(BF16)


def lift_kernel(place, xn2, grad_out, *refs):
    pieces, rest = (refs[:PIECES], refs[PIECES:])
    keep_one, send_one, keep_two, send_two, slope_gate, active, weight, sems = rest
    me = place[0]
    cols = active.shape[1]
    wait_all(fill(pieces, weight, sems, me, pl.ds(0, 2 * cols)))
    gelu_input = dot_nn(xn2[...], weight[:, :cols])
    gate_part = dot_nn(xn2[...], weight[:, cols:])
    cdf_part = 0.5 * (1.0 + lax.erf(gelu_input * (1.0 / math.sqrt(2.0))))
    density = jnp.exp(-0.5 * gelu_input * gelu_input) * (1.0 / math.sqrt(2.0 * math.pi))
    activated = gelu_input * cdf_part
    active[...] = activated
    slope_gate[...] = gate_part * (cdf_part + gelu_input * density)
    gated = (activated * gate_part).astype(BF16)
    cut = keep_one.shape[1] - xn2.shape[1] // 2
    pack(keep_one, send_one, grad_out, gated[:, :cut], X_BIT, Y_BIT, me)
    pack(keep_two, send_two, grad_out, gated[:, cut:], Y_BIT, X_BIT, me)


def contract_kernel(place, gated_one, gated_two, grad_out, xn2, hidden, slope_gate, active, *refs):
    pieces, rest = (refs[:PIECES], refs[PIECES:])
    layer_out, keep_one, send_one, keep_two, send_two, weight, sems = rest
    me = place[0]
    cols = weight.shape[1]
    wait_all(fill(pieces, weight, sems, me, pl.ds(2 * cols, cols)))
    d_gated = dot_nn(grad_out[...], weight[...])
    pack(keep_one, send_one, xn2, (d_gated * slope_gate[...]).astype(BF16), Y_BIT, X_BIT, me)
    pack(keep_two, send_two, xn2, (d_gated * active[...]).astype(BF16), X_BIT, Y_BIT, me)
    skip = xn2.shape[1] // 2
    cut = gated_one.shape[1] - skip
    down = dot_nt(gated_one[:, skip:], weight[:, :cut]) + dot_nt(gated_two[:, skip:], weight[:, cut:])
    layer_out[...] = (hidden[...] + down).astype(BF16)


def hidden_back_kernel(place, pack_one, pack_two, grad_out, hidden, gains, *refs):
    first, third = (refs[:PIECES], refs[PIECES : 2 * PIECES])
    d_hidden, d_attention, gain_grad, lift_weight, weight, sems, sems_three = refs[2 * PIECES :]
    me = place[0]
    width = hidden.shape[1]
    copies = fill(first, lift_weight, sems, me, pl.ds(0, lift_weight.shape[1]))
    lasts = fill(third, weight, sems_three, me, pl.ds(3 * width, width))
    normed, scaled = norm_parts(hidden[...])
    wait_all(copies)
    cols = lift_weight.shape[1] // 2
    d_xn2 = dot_nt(pack_one[:, width // 2 :], lift_weight[:, :cols])
    d_xn2 = d_xn2 + dot_nt(pack_two[:, width // 2 :], lift_weight[:, cols:])
    d_norm, gain_term = norm_back(d_xn2, normed, scaled, gains[1:2, :])
    gain_grad[...] = gain_term
    total = grad_out[...].astype(F32) + d_norm
    d_hidden[...] = total
    rounded = total.astype(BF16)
    wait_all(lasts)
    d_attention[...] = dot_nt(rounded, weight[...]).astype(BF16)


def attend_back_kernel(
    place, queries, keys_values, edge, bias, totals, d_attention, cosine, sine, d_turned, d_keys_values, d_edge
):
    width = queries.shape[1]
    pair = 2 * HEAD_DIM
    factor = 1.0 / math.sqrt(HEAD_DIM)
    rows = queries.shape[0]
    is_first = head_masks((rows, pair))
    is_first_key = head_masks((rows + edge.shape[0], pair))
    for start in range(0, width, pair):
        here = slice(start, start + pair)
        there = slice(width + start, width + start + pair)
        two = queries[:, here]
        d_two = d_attention[:, here]
        keys = jnp.concatenate([keys_values[:, here], edge[:, here]], axis=0)
        vals = jnp.concatenate([keys_values[:, there], edge[:, there]], axis=0)
        d_queries, d_keys, d_vals = ([], [], [])
        for which in range(2):
            mask = is_first if which == 0 else jnp.logical_not(is_first)
            one = jnp.where(mask, two, jnp.zeros_like(two))
            d_one = jnp.where(mask, d_two, jnp.zeros_like(d_two))
            head = 2 * (start // pair) + which
            scores = dot_nt(one, keys) * factor + bias[...]
            recomputed = jnp.exp(scores - totals[:, head : head + 1])
            d_soft = dot_nt(d_one, vals)
            center = jnp.sum(recomputed * d_soft, axis=-1, keepdims=True)
            d_scores = (recomputed * (d_soft - center) * factor).astype(BF16)
            d_queries.append(dot_nn(d_scores, keys))
            d_keys.append(dot_tt(d_scores, two))
            d_vals.append(dot_tt(recomputed.astype(BF16), d_two))
        d_query = jnp.where(is_first, d_queries[0], d_queries[1])
        d_turned[:, here] = turn(d_query, cosine[...], -sine[...]).astype(BF16)
        d_key = jnp.where(is_first_key, d_keys[0], d_keys[1])
        d_val = jnp.where(is_first_key, d_vals[0], d_vals[1])
        d_keys_values[:, here] = d_key[:rows]
        d_keys_values[:, there] = d_val[:rows]
        d_edge[:, here] = d_key[rows:].astype(BF16)
        d_edge[:, there] = d_val[rows:].astype(BF16)


def keys_back_kernel(
    place, d_queries, d_keys_values, arrived, cosine, sine, xn1, keep_one, send_one, keep_two, send_two, summed, d_turned
):
    me, along = (place[0], place[1])
    width = xn1.shape[1]
    pair = 2 * HEAD_DIM
    rows = arrived.shape[0]
    summed[...] = d_keys_values[...]
    where = pl.ds(pl.multiple_of((1 - along) * rows, rows), rows)
    summed[where, :] = summed[where, :] + arrived[...].astype(F32)
    for start in range(0, width, pair):
        here = slice(start, start + pair)
        there = slice(width + start, width + start + pair)
        d_turned[:, there] = turn(summed[:, here], cosine[...], -sine[...]).astype(BF16)
    d_turned[:, :width] = d_queries[...]
    d_turned[:, 2 * width :] = summed[:, width:].astype(BF16)
    middle = d_turned.shape[1] // 2
    pack(keep_one, send_one, xn1, d_turned[:, :middle], X_BIT, Y_BIT, me)
    pack(keep_two, send_two, xn1, d_turned[:, middle:], Y_BIT, X_BIT, me)


def tokens_back_kernel(place, pack_one, pack_two, tokens, attention, d_hidden, gains, mlp_term, *refs):
    pieces, (keep, send, input_grad, weight, sems) = (refs[:PIECES], refs[PIECES:])
    rows = tokens.shape[0]
    width = tokens.shape[1]
    copies = fill(pieces, weight, sems, place[0], pl.ds(0, 3 * width))
    normed, scaled = norm_parts(tokens[...].astype(F32))
    wait_all(copies)
    middle = pack_one.shape[1] - width // 2
    d_xn1 = dot_nt(pack_one[:, width // 2 :], weight[:, :middle])
    d_xn1 = d_xn1 + dot_nt(pack_two[:, width // 2 :], weight[:, middle:])
    d_norm, gain_term = norm_back(d_xn1, normed, scaled, gains[0:1, :])
    pack(keep, send, attention, d_hidden[...].astype(BF16), Y_BIT, X_BIT, place[0])
    extra = keep.shape[0] - rows
    line = lax.broadcasted_iota(jnp.int32, (extra, width), 0)
    terms = jnp.where(line == 0, mlp_term[...], jnp.where(line == 1, gain_term, 0.0)).astype(BF16)
    for target in (keep, send):
        target[rows:, : width // 2] = jnp.zeros((extra, width // 2), BF16)
        target[rows:, width // 2 :] = terms
    input_grad[...] = (d_hidden[...] + d_norm).astype(BF16)


def product_kernel(width, rows, chip, other, own, sent, joined, *refs):
    terms, sems = (refs[0] if len(refs) > 1 else None, refs[-1])
    copies = []
    extra = 0 if terms is None else terms.shape[1]
    for index in range(4):
        part, start = ((chip, other)[index // 2], index % 2 * (rows + extra))
        source = part.at[pl.ds(start, rows)]
        copies.append(pltpu.make_async_copy(source, joined.at[pl.ds(index * rows, rows)], sems.at[index]))
        if terms is not None:
            copies.append(
                pltpu.make_async_copy(part.at[pl.ds(start + rows, extra)], terms.at[index], sems.at[4 + index])
            )
    for copy in copies:
        copy.start()
    wait_all(copies)
    block = lambda top, k: joined[2 * rows * top : 2 * rows * (top + 1), k * width : (k + 1) * width]
    right = joined[:, 4 * width :]
    left = jnp.concatenate([block(0, 2), block(1, 3)], axis=0)
    sent[:width] = dot_tt(left, right).astype(BF16)
    left = jnp.concatenate([block(0, 0), block(1, 1)], axis=0)
    own[:width] = dot_tt(left, right)
    if terms is not None:
        total = sum(terms[index, :, 4 * width :].astype(F32) for index in range(4))
        own[width:] = total
        sent[width:] = total.astype(BF16)


def call(kernel, outs, operands, scratch=(), smem=1, anywhere=(), flops=0, size=0):
    specs = []
    for index in range(len(operands)):
        if index < smem:
            specs.append(pl.BlockSpec(memory_space=pltpu.SMEM))
        elif index in anywhere:
            specs.append(pl.BlockSpec(memory_space=pltpu.HBM))
        else:
            specs.append(pl.BlockSpec(memory_space=pltpu.VMEM))
    return pl.pallas_call(
        kernel,
        out_shape=[jax.ShapeDtypeStruct(shape, kind) for shape, kind in outs],
        in_specs=specs,
        out_specs=[pl.BlockSpec(memory_space=pltpu.VMEM)] * len(outs),
        scratch_shapes=list(scratch),
        cost_estimate=pl.CostEstimate(flops=flops, bytes_accessed=size, transcendentals=0),
        compiler_params=pltpu.CompilerParams(vmem_limit_bytes=VMEM_BYTES),
    )(*operands)


def grad_rows(keep, over_link, width, before=(), after=()):
    return products(share(keep, over_link, before), width, after)


def share(keep, over_link, before=()):
    return jnp.concatenate(later([keep, over_link], before), axis=0)


def products(chip, width, after=()):
    rows = chip.shape[0] // 256 * 128
    extra = chip.shape[0] // 2 - rows
    cols = chip.shape[1] - 4 * width
    other = later(swap(chip, CORE_BIT), after)
    scratch = [pltpu.VMEM((4 * rows, 4 * width + cols), BF16)]
    if extra:
        scratch.append(pltpu.VMEM((4, extra, 4 * width + cols), BF16))
    return call(
        lambda *refs: product_kernel(width, rows, *refs),
        [((width + extra, cols), F32), ((width + extra, cols), BF16)],
        [chip, other],
        scratch + [pltpu.SemaphoreType.DMA((8,))],
        smem=0,
        anywhere=(0, 1),
        flops=16 * rows * width * cols,
        size=4 * rows * (4 * width + cols) * 2 + 6 * width * cols,
    )


def line_first(part):
    return lax.ppermute(part.astype(BF16), "replica", [(0, 1), (3, 2)])


def line_pair(part, first):
    return (part + first.astype(F32)).astype(BF16)


def line_middle(pair):
    return lax.ppermute(pair, "replica", [(1, 2), (2, 1)])


def line_total(pair, other):
    return (pair.astype(F32) + other.astype(F32)).astype(BF16)


def line_back(total):
    return lax.ppermute(total, "replica", [(1, 0), (2, 3)])


def line_end(total, back):
    place = lax.axis_index("replica")
    middle = (place == 1) | (place == 2)
    return jnp.where(middle, total, back).astype(F32)


def body_plane(
    tokens,
    input_gain,
    qkv_weight,
    output_weight,
    mlp_gain,
    expand_weight,
    contract_weight,
    positions,
    mask_bias,
    cotangent,
):
    me = lax.axis_index(PLANE)
    along = lax.axis_index("ctx")
    place = jnp.stack([me, along]).astype(jnp.int32)
    shard = qkv_weight.shape[0]
    true_width = expand_weight.shape[1] // 2
    fill_cols = -true_width % 128
    ff_width = true_width + fill_cols
    source, grad_out = (tokens[0], cotangent[0])
    rows, width = source.shape
    gains = jnp.stack([input_gain, mlp_gain], axis=1)
    gains = jnp.pad(gains, ((0, 0), (0, 126)))
    front = jnp.concatenate([qkv_weight, output_weight, gains], axis=1)
    widened = lambda values: jnp.pad(values, ((0, 0), (0, fill_cols)))
    feed = jnp.concatenate(
        [
            widened(expand_weight[:, :true_width]),
            widened(expand_weight[:, true_width:]),
            widened(contract_weight),
        ],
        axis=1,
    )
    fetched = fetch_pieces(front)
    packed = share_pieces(fetched)
    feed_fetched = fetch_pieces(feed, tuple(fetched[3:]))
    cosine, sine = rope_tables(positions[0], HEAD_DIM)
    cosine = jnp.concatenate([cosine[:, 0]] * 4, axis=1)
    sine = jnp.concatenate([-sine[:, 0], sine[:, 0]] * 2, axis=1)
    bias = mask_bias[0]
    bias = jnp.concatenate(
        [bias[:, HALF : HALF + rows], jnp.where(along == 0, bias[:, HALF + rows :], bias[:, :HALF])], axis=1
    )
    sems = pltpu.SemaphoreType.DMA((PIECES,))
    front_cols = front.shape[1]
    queries, keys_values, edge, xn1, full_gains = call(
        front_kernel,
        [((rows, width), BF16), ((rows, 2 * width), BF16), ((HALF, 2 * width), BF16), ((rows, width), BF16), ((8, width), F32)],
        [place, source, cosine, sine] + packed,
        [pltpu.VMEM((width, front_cols), BF16), sems],
        anywhere=range(4, 4 + PIECES),
        flops=6 * rows * width * width,
        size=2 * width * front_cols,
    )
    edge = swap(edge, X_BIT)
    attention, totals, hidden, xn2 = call(
        attend_kernel,
        [((rows, width), BF16), ((rows, 128), F32), ((rows, width), F32), ((rows, width), BF16)],
        [place, queries, keys_values, edge, bias, source, full_gains] + packed,
        [pltpu.VMEM((width, width), BF16), sems],
        anywhere=range(7, 7 + PIECES),
        flops=12 * rows * width * width,
        size=4 * width * width,
    )
    feed_pieces = share_pieces(feed_fetched, xn2)
    half = 4 * shard
    cut = -(-ff_width // 256) * 128
    cuts = [((rows, half + cut), BF16)] * 2 + [((rows, half + ff_width - cut), BF16)] * 2
    keep_c, send_c, keep_d, send_d, slope_gate, active = call(
        lift_kernel,
        cuts + [((rows, ff_width), F32)] * 2,
        [place, xn2, grad_out] + feed_pieces,
        [pltpu.VMEM((width, 2 * ff_width), BF16), sems],
        anywhere=range(3, 3 + PIECES),
        flops=4 * rows * width * ff_width,
        size=4 * width * ff_width,
    )
    layer_out, keep_g, send_g, keep_u, send_u = call(
        contract_kernel,
        [((rows, width), BF16)] + [((rows, half + ff_width), BF16)] * 4,
        [place, keep_c, keep_d, grad_out, xn2, hidden, slope_gate, active] + feed_pieces,
        [pltpu.VMEM((width, ff_width), BF16), sems],
        anywhere=range(8, 8 + PIECES),
        flops=4 * rows * width * ff_width,
        size=2 * width * ff_width,
    )
    d_hidden, d_attention, mlp_term = call(
        hidden_back_kernel,
        [((rows, width), F32), ((rows, width), BF16), ((1, width), F32)],
        [place, keep_g, keep_u, grad_out, hidden, full_gains] + feed_pieces + packed,
        [pltpu.VMEM((width, 2 * ff_width), BF16), pltpu.VMEM((width, width), BF16), sems, sems],
        anywhere=range(6, 6 + 2 * PIECES),
        flops=6 * rows * width * ff_width,
        size=6 * width * ff_width,
    )
    link_c = swap(send_c, X_BIT)
    link_d = swap(send_d, Y_BIT)
    link_g = swap(send_g, Y_BIT)
    link_u = swap(send_u, X_BIT)
    d_queries, d_keys_values, d_edge = call(
        attend_back_kernel,
        [((rows, width), BF16), ((rows, 2 * width), F32), ((HALF, 2 * width), BF16)],
        [place, queries, keys_values, edge, bias, totals, d_attention, cosine, sine],
        flops=20 * rows * width * width,
        size=4 * width * width,
    )
    first_own, first_sent = grad_rows(keep_c, link_c, shard, keep_g, d_edge)
    second_own, second_sent = grad_rows(keep_d, link_d, shard, keep_g, d_edge)
    first_back = swap(first_sent, Y_BIT)
    second_back = swap(second_sent, X_BIT)
    chip_g = share(keep_g, link_g, (first_sent, second_sent))
    chip_u = share(keep_u, link_u, (first_sent, second_sent))
    first_back, second_back = later((first_back, second_back), chip_g, chip_u)
    contract_part = jnp.concatenate(
        [first_own + first_back.astype(F32), second_own + second_back.astype(F32)], axis=1
    )
    contract_first = line_first(contract_part)
    gelu_own, gelu_sent = products(chip_g, shard, contract_part)
    gelu_back = swap(gelu_sent, X_BIT)
    gate_own, gate_sent = products(chip_u, shard, gelu_sent)
    gate_back = swap(gate_sent, Y_BIT)
    d_keys_values = later(d_keys_values, gate_sent)
    keep_kv, send_kv, keep_vk, send_vk = call(
        keys_back_kernel,
        [((rows, half + 3 * width // 2), BF16)] * 4,
        [place, d_queries, d_keys_values, swap(d_edge, X_BIT), cosine, sine, xn1],
        [pltpu.VMEM((rows, 2 * width), F32), pltpu.VMEM((rows, 3 * width), BF16)],
        flops=rows * width,
        size=8 * rows * width,
    )
    link_kv = swap(send_kv, X_BIT)
    link_vk = swap(send_vk, Y_BIT)
    contract_pair = line_pair(contract_part, later(contract_first, keep_kv))
    contract_other = line_middle(contract_pair)
    gelu_part = gelu_own + later(gelu_back, contract_pair).astype(F32)
    gelu_first = line_first(gelu_part)
    gate_part = gate_own + later(gate_back, gelu_part).astype(F32)
    gate_first = line_first(gate_part)
    contract_total = line_total(contract_pair, later(contract_other, gate_part))
    contract_last = line_back(contract_total)
    gelu_pair = line_pair(gelu_part, later(gelu_first, contract_total))
    gelu_other = line_middle(gelu_pair)
    chip_kv = share(keep_kv, link_kv, gelu_pair)
    chip_vk = share(keep_vk, link_vk, gelu_pair)
    low_own, low_sent = products(chip_kv, shard)
    low_back = swap(low_sent, Y_BIT)
    high_own, high_sent = products(chip_vk, shard, low_sent)
    high_back = swap(high_sent, X_BIT)
    d_hidden = later(d_hidden, high_sent)
    keep_o, send_o, input_grad = call(
        tokens_back_kernel,
        [((rows + 16, half + width), BF16)] * 2 + [((rows, width), BF16)],
        [place, keep_kv, keep_vk, source, attention, d_hidden, full_gains, mlp_term] + packed,
        [pltpu.VMEM((width, 3 * width), BF16), sems],
        anywhere=range(8, 8 + PIECES),
        flops=6 * rows * width * width,
        size=6 * width * width,
    )
    link_o = swap(send_o, Y_BIT)
    gelu_total = line_total(gelu_pair, later(gelu_other, keep_o, contract_last))
    gelu_last = line_back(gelu_total)
    gate_pair = line_pair(gate_part, later(gate_first, gelu_total))
    gate_other = line_middle(gate_pair)
    low_part = low_own + later(low_back, gate_pair).astype(F32)
    low_first = line_first(low_part)
    high_part = high_own + later(high_back, low_part).astype(F32)
    high_first = line_first(high_part)
    gate_total = line_total(gate_pair, later(gate_other, high_part))
    gate_last = line_back(gate_total)
    low_pair = line_pair(low_part, later(low_first, gate_total, gelu_last))
    low_other = line_middle(low_pair)
    out_own, out_sent = grad_rows(keep_o, link_o, shard, high_part)
    out_back = swap(out_sent, X_BIT)
    high_pair = line_pair(high_part, later(high_first, low_pair))
    high_other = line_middle(high_pair)
    low_total = line_total(low_pair, later(low_other, high_pair))
    low_last = line_back(low_total)
    out_part = out_own + later(out_back, low_total, gate_last).astype(F32)
    out_first = line_first(out_part)
    out_pair = line_pair(out_part, later(out_first, low_total))
    out_other = line_middle(out_pair)
    high_total = line_total(high_pair, later(high_other, out_pair))
    high_last = line_back(high_total)
    out_total = line_total(out_pair, later(out_other, high_total))
    out_last = line_back(out_total)
    contract_grad = line_end(contract_total, later(contract_last, high_total))
    gelu_grad = line_end(gelu_total, later(gelu_last, high_total))
    gate_grad = line_end(gate_total, later(gate_last, high_total))
    all_grad = jnp.concatenate([line_end(low_total, low_last), line_end(high_total, high_last)], axis=1)
    out_grad = line_end(out_total, out_last)
    gain_rows = lax.dynamic_slice_in_dim(out_grad[shard : shard + 2], me * shard, shard, axis=1)
    return (
        layer_out[None],
        input_grad[None],
        gain_rows[1],
        all_grad,
        out_grad[:shard],
        gain_rows[0],
        jnp.concatenate([gelu_grad[:, :true_width], gate_grad[:, :true_width]], axis=1),
        contract_grad[:, :true_width],
    )


def solution(mesh):
    in_specs = (
        P(("replica", "fsdp"), "ctx", None),
        P(("fsdp", "ctx")),
        P(("fsdp", "ctx"), None),
        P(("fsdp", "ctx"), None),
        P(("fsdp", "ctx")),
        P(("fsdp", "ctx"), None),
        P(("fsdp", "ctx"), None),
        P(("replica", "fsdp"), "ctx"),
        P(("replica", "fsdp"), "ctx", None),
        P(("replica", "fsdp"), "ctx", None),
    )
    out_specs = (
        P(("replica", "fsdp"), "ctx", None),
        P(("replica", "fsdp"), "ctx", None),
        P(("fsdp", "ctx")),
        P(("fsdp", "ctx"), None),
        P(("fsdp", "ctx"), None),
        P(("fsdp", "ctx")),
        P(("fsdp", "ctx"), None),
        P(("fsdp", "ctx"), None),
    )
    sizes = (mesh.shape["replica"], mesh.shape["fsdp"], mesh.shape["ctx"])
    body = body_plane if sizes == (4, 4, 2) else body_generic
    return jax.shard_map(body, mesh=mesh, in_specs=in_specs, out_specs=out_specs, check_vma=False)
```
